32 devices in a mesh: groups: 2 (over y), theta: 16 (over z, x, core).
Axes of the slice: x: 2, y: 2, z: 4, core: 2. Of those that a mesh axis runs over, the one named last changes fastest.
Arguments:
- state_now: float32 [5, 2, 64, 256, 128], P(None, None, 'theta', 'groups'), parts along dimension 3, may hold values from -6 to 6
- state_prev: float32 [5, 2, 64, 256, 128], P(None, None, 'theta', 'groups'), parts along dimension 3, may hold values from -6 to 6
- eddy_visc: float32 [2, 64, 256, 128], P(None, 'theta', 'groups'), parts along dimension 2, may hold values from 0.01 to 0.2
- mean_flow: float32 [2, 4], replicated, may hold values from 0.5 to 1
- offset: int32 [2], P('groups'), parts along dimension 0, may hold values from 0 to 63
Outputs:
- field: float32 [5, 2, 64, 256, 128], P(None, None, 'theta', 'groups'), parts along dimension 3
The draws below stay inside these ranges and needn't reach their ends.
There are 2 independent parts, one for each index of `groups`. The reference program is written for one: setup_inputs(seed, part) draws one part's arguments, and reference() takes and returns one part's arrays. A program takes and returns all parts, laid end to end along the dimension named above; an argument that names none is the same for every part. Nothing has to cross between parts.
All inputs are finite; a program needn't handle non-finite values.
Results may differ from the reference program's by a relative error of at most 0.00002.
Values sent between devices are 32-bit elements; how exact they have to be, the bound alone decides.
No kernel may reach another device: no remote copies, remote signals or barrier semaphores. Data moves between devices by JAX's collectives and lax.ppermute only.
A program may use at most 128 MiB of HBM per device.

```python
import math
import jax
import jax.numpy as jnp

R = 128
A = 128
ITERS = 2
NT = 64


def steps_of(key, extent, split, smallest, largest):
    factor_of, own = 1.0, jax.random.fold_in(key, 6)
    for axis_at, shards_of in split:
        steps = jnp.exp(jax.random.uniform(jax.random.fold_in(own, axis_at), (shards_of,), jnp.float32, smallest / len(split), largest / len(split)))
        factor_of = factor_of * jnp.repeat(steps, extent[axis_at] // shards_of).reshape([-1 if axis == axis_at else 1 for axis in range(len(extent))])
    return factor_of


def bell_draw(stream_key, extent, spread, bound, split=(), held_as=jnp.bfloat16):
    level = steps_of(stream_key, extent, split, -0.22, 0.18) if split else 1.0
    entries = jax.random.normal(stream_key, extent, jnp.float32) * spread * level
    return jnp.minimum(jnp.maximum(entries, -bound), bound).astype(held_as)


def setup_inputs(seed: int = 0, part: int = 0) -> dict:
    keys = jax.random.split(jax.random.key(seed), 6)
    part_keys = jax.random.split(jax.random.fold_in(keys[5], part), 6)
    return {
        "state_now": bell_draw(part_keys[0], (5, 2, NT, R, A), 1.0, 6.0, ((2, 16),), jnp.float32),
        "state_prev": bell_draw(part_keys[1], (5, 2, NT, R, A), 1.0, 6.0, ((2, 16),), jnp.float32),
        "eddy_visc": jnp.clip(jnp.exp(math.log(0.2) - 2.9957323 * jax.random.uniform(part_keys[2], (2, NT, R, A), jnp.float32) ** steps_of(part_keys[2], (2, NT, R, A), ((1, 16),), -0.2, 0.2)), 0.01, 0.2),
        "mean_flow": jnp.clip(jax.random.uniform(keys[3], (2, 4), jnp.float32, 0.5, 1.0), 0.5, 1.0),
        "offset": jax.random.randint(part_keys[4], (1,), 0, NT).astype(jnp.int32),
    }


PSEUDO_STEP = 0.2
PHYS_STEP = 1.0
SECTION_WEIGHTS = (0.6, 0.6, 1.0)


def operator_terms(padded, low_ghost, high_ghost, mean_row, eddy_row):
    center = padded[:, 1:-1]
    theta_diff = (padded[:, 2:] - padded[:, :-2]) * 0.5
    neighbours = padded[:, 2:] + padded[:, :-2]
    wall_sign = jnp.array([1.0, 1.0, 1.0, -1.0, 1.0], jnp.float32).reshape(5, 1, 1, 1)
    radial_pad = jnp.concatenate([center[:, :, :1] * wall_sign, center, center[:, :, -1:] * wall_sign], axis=2)
    radial_diff = (radial_pad[:, :, 2:] - radial_pad[:, :, :-2]) * 0.5
    neighbours = neighbours + radial_pad[:, :, 2:] + radial_pad[:, :, :-2]
    axial_pad = jnp.concatenate([low_ghost[..., None], center, high_ghost[..., None]], axis=3)
    axial_diff = (axial_pad[..., 2:] - axial_pad[..., :-2]) * 0.5
    neighbours = neighbours + axial_pad[..., 2:] + axial_pad[..., :-2]
    laplace = neighbours - 6.0 * center
    axial_speed = mean_row[0]
    swirl_speed = mean_row[1]
    density = mean_row[2]
    sound_speed = mean_row[3]
    convect = axial_speed * axial_diff + swirl_speed * theta_diff
    divergence = axial_diff[1] + theta_diff[2] + radial_diff[3]
    pressure_push = jnp.stack([density * divergence, axial_diff[4] / density, theta_diff[4] / density,
                               radial_diff[4] / density, density * sound_speed * sound_speed * divergence])
    return convect + pressure_push - eddy_row * laplace


def wrap_pad(row_field):
    return jnp.concatenate([row_field[:, -1:], row_field, row_field[:, :1]], axis=1)


def reference(state_now, state_prev, eddy_visc, mean_flow, offset):
    shift_cells = offset[0] % NT
    fixed_part = (state_prev - 4.0 * state_now) * (0.5 / PHYS_STEP)
    field = state_now
    for sweep in range(ITERS):
        start_field = field
        for weight in SECTION_WEIGHTS:
            rotor_row = field[:, 0]
            stator_row = field[:, 1]
            rotor_high = jnp.roll(stator_row[..., 0], -shift_cells, axis=1)
            stator_low = jnp.roll(rotor_row[..., -1], shift_cells, axis=1)
            rotor_terms = operator_terms(wrap_pad(rotor_row), jnp.zeros_like(rotor_high), rotor_high,
                                         mean_flow[0], eddy_visc[0])
            stator_terms = operator_terms(wrap_pad(stator_row), stator_low, stator_row[..., -1],
                                          mean_flow[1], eddy_visc[1])
            terms = jnp.stack([rotor_terms, stator_terms], axis=1)
            field = start_field - (weight * PSEUDO_STEP) * (terms + (1.5 / PHYS_STEP) * field + fixed_part)
    return field
```

```python
import jax
import jax.numpy as jnp
from jax import lax
from jax.experimental import pallas as pl
from jax.experimental.pallas import tpu as pltpu
from jax.sharding import PartitionSpec as P

ITERS = 2
PSEUDO_STEP = 0.2
PHYS_STEP = 1.0
SECTION_WEIGHTS = (0.6, 0.6, 1.0)
COMPS = 5
CHUNK = 32


def coefficients(mean_flow, weight, sign):
    a = weight * PSEUDO_STEP
    axial, swirl, density, sound = mean_flow[:, 0], mean_flow[:, 1], mean_flow[:, 2], mean_flow[:, 3]
    inverse = (0.5 * a) / density
    return jnp.stack(
        [
            (0.5 * a) * axial,
            (0.5 * a) * swirl * sign,
            (0.5 * a) * density,
            (0.5 * a) * density * sound * sound,
            inverse,
            inverse * sign,
            jnp.broadcast_to(sign, inverse.shape),
            jnp.full_like(inverse, a),
        ],
        axis=1,
    ).reshape(-1)


def update_rows(row, r0, ghost_at, center, before, after, base, fixed, eddy, ghosts, coef, store):
    radial, axial = center.shape[-2:]
    rows = pl.ds(r0, CHUNK)
    lane = lax.broadcasted_iota(jnp.int32, (CHUNK, axial), 1)
    first, last = lane == 0, lane == axial - 1
    k = [coef[row * 8 + i] for i in range(8)]
    e = k[7] * eddy[rows, :]
    damp = 6.0 * e + (1.5 / PHYS_STEP) * k[7]
    ghost = ghosts[rows, :]
    parts, da, dt, dr = [], [], [], []
    for c in range(COMPS):
        f = center[c, rows, :]
        up, down = before[c, rows, :], after[c, rows, :]
        wall = -1.0 if c == 3 else 1.0
        if r0 == 0:
            low = jnp.concatenate([f[:1] * wall, center[c, pl.ds(0, CHUNK - 1), :]], axis=0)
        else:
            low = center[c, pl.ds(r0 - 1, CHUNK), :]
        if r0 + CHUNK == radial:
            high = jnp.concatenate([center[c, pl.ds(r0 + 1, CHUNK - 1), :], f[-1:] * wall], axis=0)
        else:
            high = center[c, pl.ds(r0 + 1, CHUNK), :]
        at = ghost_at(c)
        behind, ahead = pltpu.roll(f, 1, 1), pltpu.roll(f, axial - 1, 1)
        if row == 0:
            behind = jnp.where(first, 0.0, behind)
            ahead = jnp.where(last, pltpu.roll(ghost, (axial - 1 - at) % axial, 1), ahead)
        else:
            behind = jnp.where(first, pltpu.roll(ghost, (axial - at) % axial, 1), behind)
            ahead = jnp.where(last, f, ahead)
        around = ((up + down) + (low + high)) + (behind + ahead)
        da.append(ahead - behind)
        dt.append(down - up)
        dr.append(high - low if c >= 3 else None)
        start = base[c, rows, :] - k[7] * fixed[c, rows, :]
        parts.append(start - damp * f + e * around - k[0] * da[c] - k[1] * dt[c])
    div = da[1] + k[6] * dt[2] + dr[3]
    push = (k[2] * div, k[4] * da[4], k[5] * dt[4], k[4] * dr[4], k[3] * div)
    for c in range(COMPS):
        store(c, rows, parts[c] - push[c])


def pack_plane(row, value, tile, rows, at):
    axial = value.shape[-1]
    lane = lax.broadcasted_iota(jnp.int32, value.shape, 1)
    shift = (at - (axial - 1 if row == 0 else 0)) % axial
    tile[rows, :] = jnp.where(lane == at, pltpu.roll(value, shift, 1) if shift else value, tile[rows, :])


def outer_kernel(cells, last, coef, place, center, inner, across, base, fixed, eddy, ghost, *rest):
    if last:
        _, out, columns, made, sem = rest
    else:
        out, planes, columns, tile = rest
        made = out
    columns[...] = ghost[...].T
    radial = center.shape[2]
    if not last:
        tile[...] = jnp.zeros_like(tile)
    for row in range(2):
        for r0 in range(0, radial, CHUNK):

            def store(c, rows, value):
                made[c, row, rows, :] = value
                if not last:
                    pack_plane(row, value, tile, rows, row * COMPS + c)

            update_rows(
                row, r0, lambda c: (row * COMPS + c) * cells, center.at[:, row], across.at[:, row],
                inner.at[:, row, 0], base.at[:, row], fixed.at[:, row], eddy.at[row], columns, coef, store,
            )
    if last:
        copy = pltpu.make_async_copy(made, out.at[:, :, place[0]], sem)
        copy.start()
        copy.wait()
    else:
        planes[...] = tile[...].T


def inner_kernel(cells, last, coef, place, inner, outer, partner, base, fixed, eddy, ghost, *rest):
    if last:
        out, columns, made, sem = rest
    else:
        made, border, planes, columns, tile = rest
    columns[...] = ghost[...].T
    radial = inner.shape[3]
    depth = cells - 1
    copies = []
    if not last:
        tile[...] = jnp.zeros_like(tile)
    for j in range(depth):
        for row in range(2):
            for r0 in range(0, radial, CHUNK):

                def store(c, rows, value):
                    made[c, row, j, rows, :] = value
                    if not last:
                        if j == depth - 1:
                            border[c, row, rows, :] = value
                        pack_plane(row, value, tile, rows, (row * COMPS + c) * depth + j)

                before = outer.at[:, row] if j == 0 else inner.at[:, row, j - 1]
                after = partner.at[:, row] if j == depth - 1 else inner.at[:, row, j + 1]
                update_rows(
                    row, r0, lambda c: (row * COMPS + c) * cells + j + 1, inner.at[:, row, j], before, after,
                    base.at[:, row, j], fixed.at[:, row, j], eddy.at[row, j], columns, coef, store,
                )
        if last:
            copy = pltpu.make_async_copy(made.at[:, :, j], out.at[:, :, place[0] + place[1] * (j + 1)], sem.at[j])
            copy.start()
            copies.append(copy)
    for copy in copies:
        copy.wait()
    if not last:
        planes[...] = tile[...].T


VMEM = pl.BlockSpec(memory_space=pltpu.VMEM)
SMEM = pl.BlockSpec(memory_space=pltpu.SMEM)
ANY = pl.BlockSpec(memory_space=pl.ANY)


def call_outer(cells, coef, place, center, inner, across, base, fixed, eddy, ghost, partial=None):
    _, _, radial, axial = center.shape
    f32 = jnp.float32
    last = partial is not None
    shape = jax.ShapeDtypeStruct(center.shape, f32)
    columns = pltpu.VMEM((radial, axial), f32)
    args = [coef, place, center, inner, across, base, fixed, eddy, ghost]
    if last:
        return pl.pallas_call(
            lambda *refs: outer_kernel(cells, True, *refs),
            out_shape=jax.ShapeDtypeStruct(partial.shape, f32),
            in_specs=[SMEM] * 2 + [VMEM] * 7 + [ANY],
            out_specs=ANY,
            input_output_aliases={9: 0},
            scratch_shapes=[columns, pltpu.VMEM(center.shape, f32), pltpu.SemaphoreType.DMA],
            compiler_params=pltpu.CompilerParams(vmem_limit_bytes=48 << 20),
            name="outer_last",
        )(*args, partial)
    return pl.pallas_call(
        lambda *refs: outer_kernel(cells, False, *refs),
        out_shape=(shape, jax.ShapeDtypeStruct((axial, radial), f32)),
        in_specs=[SMEM] * 2 + [VMEM] * 7,
        out_specs=(VMEM, VMEM),
        scratch_shapes=[columns, columns],
        compiler_params=pltpu.CompilerParams(vmem_limit_bytes=48 << 20),
        name="outer",
    )(*args)


def call_inner(cells, coef, place, inner, outer, partner, base, fixed, eddy, ghost, whole=None):
    _, _, _, radial, axial = inner.shape
    f32 = jnp.float32
    columns = pltpu.VMEM((radial, axial), f32)
    args = [coef, place, inner, outer, partner, base, fixed, eddy, ghost]
    if whole is not None:
        return pl.pallas_call(
            lambda *refs: inner_kernel(cells, True, *refs),
            out_shape=jax.ShapeDtypeStruct(whole, f32),
            in_specs=[SMEM] * 2 + [VMEM] * 7,
            out_specs=ANY,
            scratch_shapes=[columns, pltpu.VMEM(inner.shape, f32), pltpu.SemaphoreType.DMA((cells - 1,))],
            compiler_params=pltpu.CompilerParams(vmem_limit_bytes=48 << 20),
            name="inner_last",
        )(*args)
    return pl.pallas_call(
        lambda *refs: inner_kernel(cells, False, *refs),
        out_shape=(
            jax.ShapeDtypeStruct(inner.shape, f32),
            jax.ShapeDtypeStruct(outer.shape, f32),
            jax.ShapeDtypeStruct((axial, radial), f32),
        ),
        in_specs=[SMEM] * 2 + [VMEM] * 7,
        out_specs=(VMEM, VMEM, VMEM),
        scratch_shapes=[columns, columns],
        compiler_params=pltpu.CompilerParams(vmem_limit_bytes=48 << 20),
        name="inner",
    )(*args)


def shifted(value, steps):
    count = lax.axis_size("theta")
    return lax.ppermute(value, "theta", [(i, (i + steps) % count) for i in range(count)])


def across_chips(value):
    count = lax.axis_size("theta")
    pairs = [(i, (i - 1 if i % 2 == 0 else i + 1) % count) for i in range(count)]
    return lax.ppermute(value, "theta", pairs)


def within_chip(value):
    count = lax.axis_size("theta")
    return lax.ppermute(value, "theta", [(i, i ^ 1) for i in range(count)])


def facing_planes(rotor, stator, sectors):
    count = lax.axis_size("theta")
    if count <= 16:

        def branch(steps):
            return lambda a, b: (shifted(a, steps), shifted(a, steps + 1), shifted(b, -steps), shifted(b, -steps - 1))

        return lax.switch(sectors, [branch(i) for i in range(count)], rotor, stator)
    amounts = jnp.stack([sectors, sectors + 1, count - sectors, count - sectors - 1]) % count
    stacked = jnp.stack([rotor, rotor, stator, stator])
    for level in range((count - 1).bit_length()):
        taken = ((amounts >> level) & 1) == 1
        stacked = jnp.where(taken[:, None, None, None], shifted(stacked, 1 << level), stacked)
    return stacked[0], stacked[1], stacked[2], stacked[3]


def ghost_tile(rotor, stator, sectors, within, flip, axial):
    cells, radial = rotor.shape[1:]
    near, far, ahead, further = facing_planes(rotor, stator, sectors)
    low = lax.dynamic_slice_in_dim(jnp.concatenate([far, near], axis=1), cells - within, cells, 1)
    high = lax.dynamic_slice_in_dim(jnp.concatenate([ahead, further], axis=1), within, cells, 1)
    both = jnp.stack([high, low])
    both = jnp.where(flip, both[:, :, ::-1], both).reshape(2 * COMPS * cells, radial)
    return jnp.pad(both, ((0, axial - both.shape[0]), (0, 0)))


def per_device(state_now, state_prev, eddy_visc, mean_flow, offset):
    cells, radial, axial = state_now.shape[2:]
    count = lax.axis_size("theta")
    core = lax.axis_index("theta") % 2
    flip = core == 1
    sign = jnp.where(flip, -1.0, 1.0).astype(jnp.float32)
    shift_cells = offset[0] % (cells * count)
    sectors, within = shift_cells // cells, shift_cells % cells
    depth = cells - 1

    def split(x, dim):
        outer = lax.dynamic_index_in_dim(x, core * depth, dim, keepdims=False)
        forward = lax.slice_in_dim(x, 1, cells, axis=dim)
        backward = lax.rev(lax.slice_in_dim(x, 0, depth, axis=dim), (dim,))
        return outer, jnp.where(flip, backward, forward)

    outer, inner = split(state_now, 2)
    across = across_chips(outer)
    partner = within_chip(inner[:, :, depth - 1])
    rotor, stator = state_now[:, 0, :, :, axial - 1], state_now[:, 1, :, :, 0]
    ghost = ghost_tile(rotor, stator, sectors, within, flip, axial)
    fixed_outer, fixed_inner = split((state_prev - 4.0 * state_now) * (0.5 / PHYS_STEP), 2)
    eddy_outer, eddy_inner = split(eddy_visc, 1)
    place = jnp.stack([core * depth, 1 - 2 * core]).astype(jnp.int32)
    for sweep in range(ITERS):
        base_outer, base_inner = outer, inner
        for section, weight in enumerate(SECTION_WEIGHTS):
            coef = coefficients(mean_flow, weight, sign)
            if sweep == ITERS - 1 and section == len(SECTION_WEIGHTS) - 1:
                result = call_inner(
                    cells, coef, place, inner, outer, partner, base_inner, fixed_inner, eddy_inner, ghost, state_now.shape
                )
                return call_outer(
                    cells, coef, place, outer, inner, across, base_outer, fixed_outer, eddy_outer, ghost, result
                )
            new_outer, lines = call_outer(
                cells, coef, place, outer, inner, across, base_outer, fixed_outer, eddy_outer, ghost
            )
            across = across_chips(new_outer)
            new_inner, border, more = call_inner(
                cells, coef, place, inner, outer, partner, base_inner, fixed_inner, eddy_inner, ghost
            )
            partner = within_chip(border)
            outer, inner = new_outer, new_inner
            planes = jnp.concatenate(
                [
                    lines[: 2 * COMPS].reshape(2, COMPS, 1, radial),
                    more[: 2 * COMPS * depth].reshape(2, COMPS, depth, radial),
                ],
                axis=2,
            )
            planes = jnp.where(flip, planes[:, :, ::-1], planes)
            ghost = ghost_tile(planes[0], planes[1], sectors, within, flip, axial)


def solution(mesh):
    placed = (
        P(None, None, "theta", "groups", None),
        P(None, None, "theta", "groups", None),
        P(None, "theta", "groups", None),
        P(),
        P("groups"),
    )
    return jax.shard_map(
        per_device,
        mesh=mesh,
        in_specs=placed,
        out_specs=P(None, None, "theta", "groups", None),
        check_vma=False,
    )
```

```python
import jax
import jax.numpy as jnp
from jax import lax
from jax.experimental import pallas as pl
from jax.experimental.pallas import tpu as pltpu
from jax.sharding import PartitionSpec as P

ITERS = 2
PSEUDO_STEP = 0.2
PHYS_STEP = 1.0
SECTION_WEIGHTS = (0.6, 0.6, 1.0)
COMPS = 5
CHUNK = 32
STRIP = 8
EDGE = 4
NEED = 6
PARTS = 2
PIECES = 4


def scalars_of(mean_flow, sign):
    flow = jnp.concatenate([mean_flow, 1.0 / mean_flow[:, 2:3]], axis=1).reshape(-1)
    return jnp.concatenate([flow, jnp.broadcast_to(sign, (6,))])


def coefficients(scalars, row, weight):
    a = weight * PSEUDO_STEP
    axial, swirl, density, sound, inverse = (scalars[row * 5 + i] for i in range(5))
    sign = scalars[10]
    half = 0.5 * a
    mass, lift = half * density, half * inverse
    return half * axial, half * swirl * sign, mass, mass * sound * sound, lift, lift * sign, sign, a


def advance(k, f, up, down, low, high, behind, ahead, base, fixed, eddy):
    e = k[7] * eddy
    damp = 6.0 * e + (1.5 / PHYS_STEP) * k[7]
    da = [ahead[c] - behind[c] for c in range(COMPS)]
    dt = [down[c] - up[c] for c in range(COMPS)]
    dr = [high[c] - low[c] if c >= 3 else None for c in range(COMPS)]
    div = da[1] + k[6] * dt[2] + dr[3]
    push = (k[2] * div, k[4] * da[4], k[5] * dt[4], k[4] * dr[4], k[3] * div)
    new = []
    for c in range(COMPS):
        around = ((up[c] + down[c]) + (low[c] + high[c])) + (behind[c] + ahead[c])
        kept = (base[c] - k[7] * fixed[c]) - damp * f[c]
        new.append(kept + e * around - k[0] * da[c] - k[1] * dt[c] - push[c])
    return new


def fixed_part(now, prev):
    return (prev - 4.0 * now) * (0.5 / PHYS_STEP)


def layer_rows(ref, row, size, first=0):
    return lambda c, r, n: ref[pl.ds((c * 2 + row) * size + r - first, n), :]


def joined(refs, row, size):
    def read(c, r, n):
        p, q = r // size, (r + n - 1) // size
        if p == q:
            return layer_rows(refs[p], row, size, p * size)(c, r, n)
        cut = q * size - r
        return jnp.concatenate(
            [layer_rows(refs[p], row, size, p * size)(c, r, cut), layer_rows(refs[q], row, size, q * size)(c, r + cut, n - cut)]
        )

    return read


def pieces(refs, row, size, piece):
    def read(c, r, n):
        at, first = divmod((c * 2 + row) * size + r, piece)
        return refs[at][pl.ds(first, n), :]

    return read


def plain_rows(ref, row, layer):
    return lambda c, r, n: ref[c, row, layer, pl.ds(r, n), :]


def update_rows(row, r0, radial, ghost_at, center, before, after, base, now, prev, eddy, ghosts, coef, store):
    ghost = ghosts[pl.ds(r0, CHUNK), :]
    axial = ghost.shape[-1]
    lane = lax.broadcasted_iota(jnp.int32, ghost.shape, 1)
    first, last = lane == 0, lane == axial - 1
    f, low, high, behind, ahead = [], [], [], [], []
    for c in range(COMPS):
        f.append(center(c, r0, CHUNK))
        wall = -1.0 if c == 3 else 1.0
        if r0 == 0:
            low.append(jnp.concatenate([f[c][:1] * wall, center(c, 0, CHUNK - 1)], axis=0))
        else:
            low.append(center(c, r0 - 1, CHUNK))
        if r0 + CHUNK == radial:
            high.append(jnp.concatenate([center(c, r0 + 1, CHUNK - 1), f[c][-1:] * wall], axis=0))
        else:
            high.append(center(c, r0 + 1, CHUNK))
        at = ghost_at(c)
        lower, upper = pltpu.roll(f[c], 1, 1), pltpu.roll(f[c], axial - 1, 1)
        if row == 0:
            lower = jnp.where(first, 0.0, lower)
            upper = jnp.where(last, pltpu.roll(ghost, (axial - 1 - at) % axial, 1), upper)
        else:
            lower = jnp.where(first, pltpu.roll(ghost, (axial - at) % axial, 1), lower)
            upper = jnp.where(last, f[c], upper)
        behind.append(lower)
        ahead.append(upper)
    every = range(COMPS)
    read = lambda source: [source(c, r0, CHUNK) for c in every]
    new = advance(
        coef[row], f, read(before), read(after), low, high, behind, ahead,
        read(base), [fixed_part(now(c, r0, CHUNK), prev(c, r0, CHUNK)) for c in every], eddy(r0, CHUNK),
    )
    for c in every:
        store(c, r0, new[c])


def pack_columns(tile, lines, radial, columns):
    axial = tile.shape[-1]
    lane = lax.broadcasted_iota(jnp.int32, (CHUNK, axial), 1)
    for r0 in range(0, radial, CHUNK):
        packed = jnp.zeros((CHUNK, axial), jnp.float32)
        for i, (row, c, center) in enumerate(columns):
            value, shift = center(c, r0, CHUNK), (i - (axial - 1 if row == 0 else 0)) % axial
            packed = jnp.where(lane == i, pltpu.roll(value, shift, 1) if shift else value, packed)
        tile[pl.ds(r0, CHUNK), :] = packed
    lines[...] = tile[...].T


def ghost_columns(tile, columns, faces):
    tile[...] = jnp.zeros_like(tile)
    for i, (strip, side) in enumerate(faces):
        face = 0 if side == 0 else STRIP - 1
        tile[pl.ds(i, 1), :] = strip[pl.ds(face, 1), :]
    columns[...] = tile[...].T


def strip_layer(coef, side, cur, up, down, lines, base, now, prev, eddy):
    radial = eddy.shape[-1]
    sub = lax.broadcasted_iota(jnp.int32, (STRIP, radial), 0)
    lane = lax.broadcasted_iota(jnp.int32, (STRIP, radial), 1)
    low, high, behind, ahead = [], [], [], []
    for c in range(COMPS):
        value = cur[c]
        wall = -value if c == 3 else value
        lower, upper = pltpu.roll(value, 1, 0), pltpu.roll(value, STRIP - 1, 0)
        if side == 0:
            lower = jnp.where(sub == 0, lines[c], lower)
        else:
            upper = jnp.where(sub == STRIP - 1, lines[c], upper)
        low.append(jnp.where(lane == 0, wall, pltpu.roll(value, 1, 1)))
        high.append(jnp.where(lane == radial - 1, wall, pltpu.roll(value, radial - 1, 1)))
        behind.append(lower)
        ahead.append(upper)
    fixed = [fixed_part(now[c], prev[c]) for c in range(COMPS)]
    return advance(coef[1 - side], cur, up, down, low, high, behind, ahead, base, fixed, eddy)


def edge_of(ref, side, c, separate, offset):
    if separate:
        return ref[side, c]
    got = ref[pl.ds(offset + EDGE * (side * COMPS + c), EDGE), :]
    rest = jnp.zeros((STRIP - EDGE, got.shape[1]), jnp.float32)
    return jnp.concatenate([got, rest] if side == 0 else [rest, got], axis=0)


def put_edge(ref, side, c, value, offset):
    start = 0 if side == 0 else STRIP - EDGE
    ref[pl.ds(offset + EDGE * (side * COMPS + c), EDGE), :] = value[start : start + EDGE]


class Plan:
    def __init__(self, n, shape):
        self.weight = SECTION_WEIGHTS[(n - 1) % len(SECTION_WEIGHTS)]
        self.n, self.total = n, ITERS * len(SECTION_WEIGHTS)
        self.cells, self.radial, self.axial = shape[2:]
        self.depth, self.size = self.cells - 1, self.radial // PARTS
        self.piece = 2 * COMPS * self.radial // PIECES
        self.final = n == self.total
        self.strips = n < self.total
        self.edges = n < self.total - 1


def place_of(scalars, depth):
    odd = scalars[10] < 0.0
    return jnp.where(odd, depth, 0), jnp.where(odd, -1, 1)


def outer_kernel(plan, p, refs):
    size, radial = plan.size, plan.radial
    scalars, eddy, prev, inner, strip = (refs.pop(0) for _ in range(5))
    place = place_of(scalars, plan.depth)
    coef = [coefficients(scalars, row, plan.weight) for row in range(2)]
    mine = [refs.pop(0) for _ in range(PARTS)]
    now, base, across = refs.pop(0), refs.pop(0), refs.pop(0)
    works = p == 0 and plan.strips
    if works:
        edges = refs.pop(0) if plan.n == 1 else across
        strip_inner, strip_now, strip_prev, strip_eddy = (refs.pop(0) for _ in range(4))
        strip_base = refs.pop(0)
    if p > 0 and not plan.final:
        refs.pop(0)
    if plan.final:
        refs.pop(0)
    out = refs.pop(0)
    if works:
        strip_out = refs.pop(0)
    tile, columns = refs.pop(0), refs.pop(0)
    if plan.final:
        made, sem = refs.pop(0), refs.pop(0)
    else:
        made = out
    ghost_columns(tile, columns, [(strip.at[side, c], side) for side in range(2) for c in range(COMPS)])
    for row in range(2):
        for r0 in range(p * size, (p + 1) * size, CHUNK):

            def store(c, r, value):
                made[pl.ds((c * 2 + row) * size + r - p * size, CHUNK), :] = value

            inside = plain_rows(inner, row, place[0] + place[1] if plan.n == 1 else 0)
            part = lambda ref: layer_rows(ref, row, size, p * size)
            update_rows(
                row, r0, radial, lambda c: row * COMPS + c, joined(mine, row, size), part(across), inside, part(base),
                part(now), part(prev), lambda r, n: eddy[row, pl.ds(r, n), :], columns, coef, store,
            )
    if plan.final:
        copies = []
        for c in range(COMPS):
            for row in range(2):
                source = made.at[pl.ds((c * 2 + row) * size, size), :]
                target = out.at[c, row, place[0], pl.ds(p * size, size), :]
                copies.append(pltpu.make_async_copy(source, target, sem.at[c * 2 + row]))
                copies[-1].start()
        for copy in copies:
            copy.wait()
    if works:
        lines = tile
        pack_columns(
            columns, lines, radial, [(row, c, joined(mine, row, size)) for row in range(2) for c in range(COMPS)]
        )
        every = range(COMPS)
        for side in range(2):
            result = strip_layer(
                coef, side, [strip[side, c] for c in every],
                [edge_of(edges, side, c, plan.n == 1, 2 * COMPS * size) for c in every],
                [strip_inner[side, c, 0] for c in every], [lines[pl.ds(side * COMPS + c, 1), :] for c in every],
                [strip_base[side, c] for c in every], [strip_now[side, c] for c in every],
                [strip_prev[side, c] for c in every], strip_eddy[side],
            )
            for c in every:
                strip_out[side, c] = result[c]
                if plan.edges:
                    put_edge(out, side, c, result[c], 2 * COMPS * size)


def inner_kernel(plan, refs):
    size, radial, depth = plan.size, plan.radial, plan.depth
    scalars, eddy, prev, now, inner, strip = (refs.pop(0) for _ in range(6))
    place = place_of(scalars, plan.depth)
    coef = [coefficients(scalars, row, plan.weight) for row in range(2)]
    if plan.n == 1:
        inner = now
    outer = [refs.pop(0) for _ in range(PARTS)]
    partner, base = [refs.pop(0) for _ in range(PIECES)], refs.pop(0)
    if plan.strips:
        edges = refs.pop(0) if plan.n == 1 else partner[-1]
        strip_outer, strip_now, strip_prev, strip_eddy, strip_base = (refs.pop(0) for _ in range(5))
    if plan.strips:
        refs.pop(0)
    made = refs.pop(0)
    if plan.strips:
        border, strip_out = [refs.pop(0) for _ in range(PIECES)], refs.pop(0)
    tile, columns = refs.pop(0), refs.pop(0)
    if plan.final:
        out, made, sem = made, refs.pop(0), refs.pop(0)
    ghost_columns(
        tile, columns, [(strip.at[side, c, j], side) for side in range(2) for c in range(COMPS) for j in range(depth)]
    )
    copies = []
    at = lambda j: place[0] + place[1] * (j + 1)
    own = lambda j: at(j) if plan.n == 1 else j
    for j in range(depth):
        for row in range(2):
            for r0 in range(0, radial, CHUNK):

                def store(c, r, value):
                    made[c, row, j, pl.ds(r, CHUNK), :] = value
                    if plan.strips and j == depth - 1:
                        piece, at_row = divmod((c * 2 + row) * radial + r, plan.piece)
                        border[piece][pl.ds(at_row, CHUNK), :] = value

                before = joined(outer, row, size) if j == 0 else plain_rows(inner, row, own(j - 1))
                after = pieces(partner, row, radial, plan.piece) if j == depth - 1 else plain_rows(inner, row, own(j + 1))
                first = plan.n <= len(SECTION_WEIGHTS)
                update_rows(
                    row, r0, radial, lambda c: (row * COMPS + c) * depth + j, plain_rows(inner, row, own(j)), before,
                    after, plain_rows(base, row, at(j) if first else j), plain_rows(now, row, at(j)),
                    plain_rows(prev, row, at(j)), lambda r, n: eddy[row, at(j), pl.ds(r, n), :], columns, coef, store,
                )
        if plan.final:
            copies.append(pltpu.make_async_copy(made.at[:, :, j], out.at[:, :, at(j)], sem.at[j]))
            copies[-1].start()
    for copy in copies:
        copy.wait()
    if plan.strips:
        lines = tile
        pack_columns(
            columns, lines, radial,
            [(row, c, plain_rows(inner, row, own(j))) for row in range(2) for c in range(COMPS) for j in range(depth)],
        )
        every = range(COMPS)
        for side in range(2):
            for j in range(depth):
                if j < depth - 1:
                    down = [strip[side, c, j + 1] for c in every]
                else:
                    down = [edge_of(edges, side, c, plan.n == 1, plan.piece) for c in every]
                result = strip_layer(
                    coef, side, [strip[side, c, j] for c in every],
                    [strip_outer[side, c] if j == 0 else strip[side, c, j - 1] for c in every], down,
                    [lines[pl.ds((side * COMPS + c) * depth + j, 1), :] for c in every],
                    [strip_base[side, c, j] for c in every], [strip_now[side, c, j] for c in every],
                    [strip_prev[side, c, j] for c in every], strip_eddy[side, j],
                )
                for c in every:
                    strip_out[side, c, j] = result[c]
                    if j == depth - 1 and plan.edges:
                        put_edge(border[-1], side, c, result[c], plan.piece)


def strip_items():
    items, at = [], 0
    for kind, c in [(0, c) for c in range(COMPS)] + [(1, c) for c in range(COMPS)] + [(2, 0)]:
        count = NEED if kind == 0 else NEED - 1
        items.append((kind, c, count, at))
        at += count
    return items, at


def gather_kernel(now, prev, eddy, rotor, stator):
    _, _, cells, radial, axial = now.shape
    per_tile = axial // STRIP
    block = lax.broadcasted_iota(jnp.int32, (radial, axial), 1) // STRIP
    items = [(item, t) for item in strip_items()[0] for t in range(cells)]
    for row, out in enumerate((rotor, stator)):
        begin = axial - STRIP if row == 0 else 0
        for p in range(0, len(items), per_tile):
            tile = jnp.zeros((radial, axial), jnp.float32)
            for q, ((kind, c, _, _), t) in enumerate(items[p : p + per_tile]):
                value = eddy[row, t] if kind == 2 else (now, prev)[kind][c, row, t]
                shift = (q * STRIP - begin) % axial
                tile = jnp.where(block == q, pltpu.roll(value, shift, 1) if shift else value, tile)
            turned = tile.T
            for q, ((_, _, count, at), t) in enumerate(items[p : p + per_tile]):
                first = q * STRIP + (STRIP - count if row == 0 else 0)
                out[t, pl.ds(at, count), :] = turned[first : first + count]


def scatter_kernel(depth, scalars, within, near, far, ahead, further, before, beyond, *outs):
    cells = depth + 1
    radial = near.shape[-1]
    now_out, now_in, prev_out, prev_in, eddy_out, eddy_in, across, partner = outs
    first, step = place_of(scalars, depth)

    def read(side, j, at, count, edge):
        t = first + step * j
        if side == 0:
            index, one, two, extra, outside = within[0] + t, ahead, further, before, within[0] + t < 0
        else:
            index, one, two, extra = cells - within[0] + t, far, near, beyond
            outside = index >= 2 * cells
        rows = pl.ds(at, count)
        early = one[jnp.clip(index, 0, depth), rows, :]
        late = two[jnp.clip(index - cells, 0, depth), rows, :]
        value = jnp.where(index < cells, early, late)
        if edge:
            value = jnp.where(outside, extra[rows, :], value)
        rest = jnp.zeros((STRIP - count, radial), jnp.float32)
        return jnp.concatenate([value, rest] if side == 0 else [rest, value], axis=0)

    for side in range(2):
        for kind, c, count, at in strip_items()[0]:
            for j in range(cells):
                value = read(side, j, at, count, False)
                if kind == 2 and j == 0:
                    eddy_out[side] = value
                elif kind == 2:
                    eddy_in[side, j - 1] = value
                elif j == 0:
                    (now_out, prev_out)[kind][side, c] = value
                else:
                    (now_in, prev_in)[kind][side, c, j - 1] = value
            if kind == 0:
                across[side, c] = read(side, -1, at, count, True)
                partner[side, c] = read(side, cells, at, count, True)


VMEM = pl.BlockSpec(memory_space=pltpu.VMEM)
SMEM = pl.BlockSpec(memory_space=pltpu.SMEM)
ANY = pl.BlockSpec(memory_space=pl.ANY)


def run(kernel, scalars, arrays, outs, scratch, name, final=None, out_shape=None):
    scalars, arrays = list(scalars), [pltpu.with_memory_space_constraint(x, pltpu.VMEM) for x in arrays]
    in_specs = [SMEM] * len(scalars) + [VMEM] * len(arrays)
    if out_shape is not None:
        outs, out_specs = jax.ShapeDtypeStruct(out_shape, jnp.float32), ANY
    else:
        out_specs = (VMEM,) * len(outs)
    aliases = {}
    if final is not None:
        aliases = {len(in_specs): 0}
        in_specs, arrays = in_specs + [ANY], arrays + [final]
    return pl.pallas_call(
        lambda *refs: kernel(list(refs)),
        out_shape=outs,
        in_specs=in_specs,
        out_specs=out_specs,
        input_output_aliases=aliases,
        scratch_shapes=scratch,
        compiler_params=pltpu.CompilerParams(vmem_limit_bytes=16 << 20),
        cost_estimate=pl.CostEstimate(flops=1, bytes_accessed=1, transcendentals=0),
        name=name,
    )(*scalars, *arrays)


def call_gather(now, prev, eddy):
    cells, radial = now.shape[2:4]
    out = pltpu.VMEM((cells, strip_items()[1], radial), jnp.float32)
    return run(lambda refs: gather_kernel(*refs), [], [now, prev, eddy], (out, out), [], "gather_strips")


def call_scatter(scalars, within, moved):
    cells, _, radial = moved[0].shape
    shape = lambda *lead: pltpu.VMEM((2, *lead, STRIP, radial), jnp.float32)
    both = [shape(COMPS), shape(COMPS, cells - 1)]
    outs = (*both, *both, shape(), shape(cells - 1), shape(COMPS), shape(COMPS))
    return run(
        lambda refs: scatter_kernel(cells - 1, *refs), [scalars, within.reshape(1)], moved, outs, [], "scatter_strips"
    )


def shifted(value, steps):
    count = lax.axis_size("theta")
    return lax.ppermute(value, "theta", [(i, (i + steps) % count) for i in range(count)])


def across_chips(value):
    count = lax.axis_size("theta")
    pairs = [(i, (i - 1 if i % 2 == 0 else i + 1) % count) for i in range(count)]
    return lax.ppermute(value, "theta", pairs)


def within_chip(value):
    count = lax.axis_size("theta")
    return lax.ppermute(value, "theta", [(i, i ^ 1) for i in range(count)])


def faced(outer, rotor, stator, sectors):
    count = lax.axis_size("theta")
    if count <= 16:

        def branch(steps):
            def exchange(outer, rotor, stator):
                return (
                    across_chips(outer), shifted(rotor, steps), shifted(rotor, steps + 1), shifted(stator, -steps),
                    shifted(stator, -steps - 1), shifted(stator[-1], 1 - steps), shifted(rotor[0], steps - 1),
                )

            return exchange

        return lax.switch(sectors, [branch(i) for i in range(count)], outer, rotor, stator)
    amounts = jnp.stack([sectors, sectors + 1, count - sectors, count - sectors - 1]) % count
    wide_rotor = jnp.concatenate([rotor, shifted(rotor[:1], -1)])
    wide_stator = jnp.concatenate([stator, shifted(stator[-1:], 1)])
    stacked = jnp.stack([wide_rotor, wide_rotor, wide_stator, wide_stator])
    for level in range((count - 1).bit_length()):
        taken = ((amounts >> level) & 1) == 1
        stacked = jnp.where(taken[:, None, None, None], shifted(stacked, 1 << level), stacked)
    return across_chips(outer), *(stacked[i, :-1] for i in range(4)), stacked[2, -1], stacked[0, -1]


def per_device(state_now, state_prev, eddy_visc, mean_flow, offset):
    shape = state_now.shape
    cells, radial, axial = shape[2:]
    count = lax.axis_size("theta")
    core = lax.axis_index("theta") % 2
    scalars = scalars_of(mean_flow, jnp.where(core == 1, -1.0, 1.0).astype(jnp.float32))
    shift_cells = offset[0] % (cells * count)
    sectors, within = shift_cells // cells, shift_cells % cells
    depth, size = cells - 1, radial // PARTS

    def layer(x, at):
        return lax.dynamic_index_in_dim(x, at, 2, keepdims=False)

    def in_parts(x):
        return [x[:, :, p * size : (p + 1) * size].reshape(2 * COMPS * size, axial) for p in range(PARTS)]

    outer = in_parts(layer(state_now, core * depth))
    across = [across_chips(x) for x in outer[:-1]]
    sectors = lax.optimization_barrier((sectors, across))[0]
    rotor, stator = call_gather(state_now, state_prev, eddy_visc)
    moved = faced(outer[-1], rotor, stator, sectors)
    across.append(moved[0])
    border = layer(state_now, (1 - core) * depth).reshape(PIECES, -1, axial)
    partner = [within_chip(border[i]) for i in range(PIECES)]
    prev_outer = in_parts(layer(state_prev, core * depth))
    eddy_outer = lax.dynamic_index_in_dim(eddy_visc, core * depth, 1, keepdims=False)
    now_out, now_in, prev_out, prev_in, eddy_out, eddy_in, edge_across, edge_within = call_scatter(
        scalars, within, moved[1:]
    )

    now_outer, inner, strip_out, strip_in = outer, state_now, now_out, now_in
    f32 = jnp.float32
    square = pltpu.VMEM((radial, axial), f32)
    n = 0
    for _ in range(ITERS):
        base_outer, base_inner, base_out, base_in = outer, inner, strip_out, strip_in
        for _ in SECTION_WEIGHTS:
            n += 1
            plan = Plan(n, shape)

            def outer_call(p, ordered):
                arrays = [eddy_outer, prev_outer[p], inner, strip_out, *outer, now_outer[p], base_outer[p], across[p]]
                outs = [pltpu.VMEM((2 * COMPS * size, axial), f32)]
                if p == 0 and plan.edges:
                    outs = [pltpu.VMEM((2 * COMPS * (size + EDGE), axial), f32)]
                if p == 0 and plan.strips:
                    arrays += [edge_across] if n == 1 else []
                    arrays += [strip_in, now_out, prev_out, eddy_out, base_out]
                    outs.append(pltpu.VMEM(strip_out.shape, f32))
                scratch = [square, square]
                if plan.final:
                    scratch += [pltpu.VMEM((2 * COMPS * size, axial), f32), pltpu.SemaphoreType.DMA((2 * COMPS,))]
                elif p > 0:
                    arrays.append(ordered)
                return run(
                    lambda refs: outer_kernel(plan, p, refs), [scalars], arrays, tuple(outs), scratch, "outer",
                    ordered if plan.final else None, shape if plan.final else None,
                )

            def inner_call(ordered):
                arrays = [eddy_visc, state_prev, state_now, inner, strip_in, *outer, *partner, base_inner]
                outs = [pltpu.VMEM((COMPS, 2, depth, radial, axial), f32)]
                if plan.strips:
                    arrays += [edge_within] if n == 1 else []
                    arrays += [strip_out, now_in, prev_in, eddy_in, base_in, ordered]
                    outs += [pltpu.VMEM((plan.piece, axial), f32)] * (PIECES - 1)
                    rows = plan.piece + (2 * COMPS * EDGE if plan.edges else 0)
                    outs += [pltpu.VMEM((rows, axial), f32), pltpu.VMEM(strip_in.shape, f32)]
                scratch = [square, square]
                if plan.final:
                    scratch += [pltpu.VMEM((COMPS, 2, depth, radial, axial), f32), pltpu.SemaphoreType.DMA((depth,))]
                return run(
                    lambda refs: inner_kernel(plan, refs), [scalars], arrays, tuple(outs), scratch, "inner", None,
                    shape if plan.final else None,
                )

            if plan.final:
                made = inner_call(None)
                for p in range(PARTS):
                    made = outer_call(p, made)
                return made
            new_outer = []
            for p in range(PARTS):
                got = outer_call(p, new_outer[-1] if p else None)
                new_outer.append(got[0])
                if p == 0:
                    new_strip_out = got[1]
            made = inner_call(new_outer[-1])
            across = [across_chips(x) for x in new_outer]
            partner = [within_chip(x) for x in made[1:-1]]
            inner, strip_in = made[0], made[-1]
            outer, strip_out = new_outer, new_strip_out


def solution(mesh):
    placed = (
        P(None, None, "theta", "groups", None),
        P(None, None, "theta", "groups", None),
        P(None, "theta", "groups", None),
        P(),
        P("groups"),
    )
    return jax.shard_map(
        per_device,
        mesh=mesh,
        in_specs=placed,
        out_specs=P(None, None, "theta", "groups", None),
        check_vma=False,
    )
```

```python
import jax
import jax.numpy as jnp
from jax import lax
from jax.experimental import pallas as pl
from jax.experimental.pallas import tpu as pltpu
from jax.sharding import PartitionSpec as P

ITERS = 2
PSEUDO_STEP = 0.2
PHYS_STEP = 1.0
SECTION_WEIGHTS = (0.6, 0.6, 1.0)
COMPS = 5
CHUNK = 32
STRIP = 8
EDGE = 4
NEED = 6
HALF = 32
PARTS = 2
PIECES = 4


def scalars_of(mean_flow, sign):
    flow = jnp.concatenate([mean_flow, 1.0 / mean_flow[:, 2:3]], axis=1).reshape(-1)
    return jnp.concatenate([flow, jnp.broadcast_to(sign, (6,))])


def coefficients(scalars, row, weight):
    a = weight * PSEUDO_STEP
    axial, swirl, density, sound, inverse = (scalars[row * 5 + i] for i in range(5))
    sign = scalars[10]
    half = 0.5 * a
    mass, lift = half * density, half * inverse
    return half * axial, half * swirl * sign, mass, mass * sound * sound, lift, lift * sign, sign, a


def advance(k, f, up, down, low, high, behind, ahead, base, fixed, eddy):
    e = k[7] * eddy
    damp = 6.0 * e + (1.5 / PHYS_STEP) * k[7]
    da = [ahead[c] - behind[c] for c in range(COMPS)]
    dt = [down[c] - up[c] for c in range(COMPS)]
    dr = [high[c] - low[c] if c >= 3 else None for c in range(COMPS)]
    div = da[1] + k[6] * dt[2] + dr[3]
    push = (k[2] * div, k[4] * da[4], k[5] * dt[4], k[4] * dr[4], k[3] * div)
    new = []
    for c in range(COMPS):
        around = ((up[c] + down[c]) + (low[c] + high[c])) + (behind[c] + ahead[c])
        kept = (base[c] - k[7] * fixed[c]) - damp * f[c]
        new.append(kept + e * around - k[0] * da[c] - k[1] * dt[c] - push[c])
    return new


def fixed_part(now, prev):
    return (prev - 4.0 * now) * (0.5 / PHYS_STEP)


def layer_rows(ref, row, size, first=0):
    return lambda c, r, n: ref[pl.ds((c * 2 + row) * size + r - first, n), :]


def joined(refs, row, size):
    def read(c, r, n):
        p, q = r // size, (r + n - 1) // size
        if p == q:
            return layer_rows(refs[p], row, size, p * size)(c, r, n)
        cut = q * size - r
        return jnp.concatenate(
            [layer_rows(refs[p], row, size, p * size)(c, r, cut), layer_rows(refs[q], row, size, q * size)(c, r + cut, n - cut)]
        )

    return read


def pieces(refs, row, size, piece):
    def read(c, r, n):
        at, first = divmod((c * 2 + row) * size + r, piece)
        return refs[at][pl.ds(first, n), :]

    return read


def plain_rows(ref, row, layer):
    return lambda c, r, n: ref[c, row, layer, pl.ds(r, n), :]


def update_rows(row, r0, radial, ghost_at, center, before, after, base, now, prev, eddy, ghosts, coef, store):
    ghost = ghosts[pl.ds(r0, CHUNK), :]
    axial = ghost.shape[-1]
    lane = lax.broadcasted_iota(jnp.int32, ghost.shape, 1)
    first, last = lane == 0, lane == axial - 1
    f, low, high, behind, ahead = [], [], [], [], []
    for c in range(COMPS):
        f.append(center(c, r0, CHUNK))
        wall = -1.0 if c == 3 else 1.0
        if r0 == 0:
            low.append(jnp.concatenate([f[c][:1] * wall, center(c, 0, CHUNK - 1)], axis=0))
        else:
            low.append(center(c, r0 - 1, CHUNK))
        if r0 + CHUNK == radial:
            high.append(jnp.concatenate([center(c, r0 + 1, CHUNK - 1), f[c][-1:] * wall], axis=0))
        else:
            high.append(center(c, r0 + 1, CHUNK))
        at = ghost_at(c)
        lower, upper = pltpu.roll(f[c], 1, 1), pltpu.roll(f[c], axial - 1, 1)
        if row == 0:
            lower = jnp.where(first, 0.0, lower)
            upper = jnp.where(last, pltpu.roll(ghost, (axial - 1 - at) % axial, 1), upper)
        else:
            lower = jnp.where(first, pltpu.roll(ghost, (axial - at) % axial, 1), lower)
            upper = jnp.where(last, f[c], upper)
        behind.append(lower)
        ahead.append(upper)
    every = range(COMPS)
    read = lambda source: [source(c, r0, CHUNK) for c in every]
    new = advance(
        coef[row], f, read(before), read(after), low, high, behind, ahead,
        read(base), [fixed_part(now(c, r0, CHUNK), prev(c, r0, CHUNK)) for c in every], eddy(r0, CHUNK),
    )
    for c in every:
        store(c, r0, new[c])


def pack_columns(tile, lines, radial, columns):
    axial = tile.shape[-1]
    lane = lax.broadcasted_iota(jnp.int32, (CHUNK, axial), 1)
    for r0 in range(0, radial, CHUNK):
        packed = jnp.zeros((CHUNK, axial), jnp.float32)
        for i, (row, c, center) in enumerate(columns):
            value, shift = center(c, r0, CHUNK), (i - (axial - 1 if row == 0 else 0)) % axial
            packed = jnp.where(lane == i, pltpu.roll(value, shift, 1) if shift else value, packed)
        tile[pl.ds(r0, CHUNK), :] = packed
    lines[...] = tile[...].T


def ghost_columns(tile, columns, faces):
    tile[...] = jnp.zeros_like(tile)
    for i, (strip, side) in enumerate(faces):
        face = 0 if side == 0 else STRIP - 1
        tile[pl.ds(i, 1), :] = strip[pl.ds(face, 1), :]
    columns[...] = tile[...].T


def strip_layer(coef, side, cur, up, down, lines, base, now, prev, eddy):
    radial = eddy.shape[-1]
    sub = lax.broadcasted_iota(jnp.int32, (STRIP, radial), 0)
    lane = lax.broadcasted_iota(jnp.int32, (STRIP, radial), 1)
    low, high, behind, ahead = [], [], [], []
    for c in range(COMPS):
        value = cur[c]
        wall = -value if c == 3 else value
        lower, upper = pltpu.roll(value, 1, 0), pltpu.roll(value, STRIP - 1, 0)
        if side == 0:
            lower = jnp.where(sub == 0, lines[c], lower)
        else:
            upper = jnp.where(sub == STRIP - 1, lines[c], upper)
        low.append(jnp.where(lane == 0, wall, pltpu.roll(value, 1, 1)))
        high.append(jnp.where(lane == radial - 1, wall, pltpu.roll(value, radial - 1, 1)))
        behind.append(lower)
        ahead.append(upper)
    fixed = [fixed_part(now[c], prev[c]) for c in range(COMPS)]
    return advance(coef[1 - side], cur, up, down, low, high, behind, ahead, base, fixed, eddy)


def edge_of(ref, side, c, separate, offset):
    if separate:
        return ref[side, c]
    got = ref[pl.ds(offset + EDGE * (side * COMPS + c), EDGE), :]
    rest = jnp.zeros((STRIP - EDGE, got.shape[1]), jnp.float32)
    return jnp.concatenate([got, rest] if side == 0 else [rest, got], axis=0)


def put_edge(ref, side, c, value, offset):
    start = 0 if side == 0 else STRIP - EDGE
    ref[pl.ds(offset + EDGE * (side * COMPS + c), EDGE), :] = value[start : start + EDGE]


class Plan:
    def __init__(self, n, shape):
        self.weight = SECTION_WEIGHTS[(n - 1) % len(SECTION_WEIGHTS)]
        self.n, self.total = n, ITERS * len(SECTION_WEIGHTS)
        self.cells, self.radial, self.axial = shape[2:]
        self.depth, self.size = self.cells - 1, self.radial // PARTS
        self.piece = 2 * COMPS * self.radial // PIECES
        self.final = n == self.total
        self.strips = n < self.total
        self.edges = n < self.total - 1


def place_of(scalars, depth):
    odd = scalars[10] < 0.0
    return jnp.where(odd, depth, 0), jnp.where(odd, -1, 1)


def outer_kernel(plan, p, refs):
    size, radial = plan.size, plan.radial
    scalars, eddy, prev, inner, strip = (refs.pop(0) for _ in range(5))
    place = place_of(scalars, plan.depth)
    coef = [coefficients(scalars, row, plan.weight) for row in range(2)]
    mine = [refs.pop(0) for _ in range(PARTS)]
    now, base, across = refs.pop(0), refs.pop(0), refs.pop(0)
    works = p == 0 and plan.strips
    if works:
        edges = refs.pop(0) if plan.n == 1 else across
        strip_inner, strip_now, strip_prev, strip_eddy = (refs.pop(0) for _ in range(4))
        strip_base = refs.pop(0)
    if p > 0 and not plan.final:
        refs.pop(0)
    if plan.final:
        refs.pop(0)
    out = refs.pop(0)
    if works:
        strip_out = refs.pop(0)
    tile, columns = refs.pop(0), refs.pop(0)
    if plan.final:
        made, sem = refs.pop(0), refs.pop(0)
    else:
        made = out
    ghost_columns(tile, columns, [(strip.at[side, c], side) for side in range(2) for c in range(COMPS)])
    for row in range(2):
        for r0 in range(p * size, (p + 1) * size, CHUNK):

            def store(c, r, value):
                made[pl.ds((c * 2 + row) * size + r - p * size, CHUNK), :] = value

            inside = plain_rows(inner, row, place[0] + place[1] if plan.n == 1 else 0)
            part = lambda ref: layer_rows(ref, row, size, p * size)
            update_rows(
                row, r0, radial, lambda c: row * COMPS + c, joined(mine, row, size), part(across), inside, part(base),
                part(now), part(prev), lambda r, n: eddy[row, pl.ds(r, n), :], columns, coef, store,
            )
    if plan.final:
        copies = []
        for c in range(COMPS):
            for row in range(2):
                source = made.at[pl.ds((c * 2 + row) * size, size), :]
                target = out.at[c, row, place[0], pl.ds(p * size, size), :]
                copies.append(pltpu.make_async_copy(source, target, sem.at[c * 2 + row]))
                copies[-1].start()
        for copy in copies:
            copy.wait()
    if works:
        lines = tile
        pack_columns(
            columns, lines, radial, [(row, c, joined(mine, row, size)) for row in range(2) for c in range(COMPS)]
        )
        every = range(COMPS)
        for side in range(2):
            result = strip_layer(
                coef, side, [strip[side, c] for c in every],
                [edge_of(edges, side, c, plan.n == 1, 2 * COMPS * size) for c in every],
                [strip_inner[side, c, 0] for c in every], [lines[pl.ds(side * COMPS + c, 1), :] for c in every],
                [strip_base[side, c] for c in every], [strip_now[side, c] for c in every],
                [strip_prev[side, c] for c in every], strip_eddy[side],
            )
            for c in every:
                strip_out[side, c] = result[c]
                if plan.edges:
                    put_edge(out, side, c, result[c], 2 * COMPS * size)


def inner_kernel(plan, refs):
    size, radial, depth = plan.size, plan.radial, plan.depth
    scalars, eddy, prev, now, inner, strip = (refs.pop(0) for _ in range(6))
    place = place_of(scalars, plan.depth)
    coef = [coefficients(scalars, row, plan.weight) for row in range(2)]
    if plan.n == 1:
        inner = now
    outer = [refs.pop(0) for _ in range(PARTS)]
    partner, base = [refs.pop(0) for _ in range(1 if plan.n == 1 else PIECES)], refs.pop(0)
    if plan.strips:
        edges = refs.pop(0) if plan.n == 1 else partner[-1]
        strip_outer, strip_now, strip_prev, strip_eddy, strip_base = (refs.pop(0) for _ in range(5))
    if plan.strips:
        refs.pop(0)
    made = refs.pop(0)
    if plan.strips:
        border, strip_out = [refs.pop(0) for _ in range(PIECES)], refs.pop(0)
    tile, columns = refs.pop(0), refs.pop(0)
    if plan.final:
        out, made, sem = made, refs.pop(0), refs.pop(0)
    ghost_columns(
        tile, columns, [(strip.at[side, c, j], side) for side in range(2) for c in range(COMPS) for j in range(depth)]
    )
    copies = []
    at = lambda j: place[0] + place[1] * (j + 1)
    own = lambda j: at(j) if plan.n == 1 else j
    for j in range(depth):
        for row in range(2):
            for r0 in range(0, radial, CHUNK):

                def store(c, r, value):
                    made[c, row, j, pl.ds(r, CHUNK), :] = value
                    if plan.strips and j == depth - 1:
                        piece, at_row = divmod((c * 2 + row) * radial + r, plan.piece)
                        border[piece][pl.ds(at_row, CHUNK), :] = value

                before = joined(outer, row, size) if j == 0 else plain_rows(inner, row, own(j - 1))
                after = pieces(partner, row, radial, partner[0].shape[0]) if j == depth - 1 else plain_rows(inner, row, own(j + 1))
                first = plan.n <= len(SECTION_WEIGHTS)
                update_rows(
                    row, r0, radial, lambda c: (row * COMPS + c) * depth + j, plain_rows(inner, row, own(j)), before,
                    after, plain_rows(base, row, at(j) if first else j), plain_rows(now, row, at(j)),
                    plain_rows(prev, row, at(j)), lambda r, n: eddy[row, at(j), pl.ds(r, n), :], columns, coef, store,
                )
        if plan.final:
            copies.append(pltpu.make_async_copy(made.at[:, :, j], out.at[:, :, at(j)], sem.at[j]))
            copies[-1].start()
    for copy in copies:
        copy.wait()
    if plan.strips:
        lines = tile
        pack_columns(
            columns, lines, radial,
            [(row, c, plain_rows(inner, row, own(j))) for row in range(2) for c in range(COMPS) for j in range(depth)],
        )
        every = range(COMPS)
        for side in range(2):
            for j in range(depth):
                if j < depth - 1:
                    down = [strip[side, c, j + 1] for c in every]
                else:
                    down = [edge_of(edges, side, c, plan.n == 1, plan.piece) for c in every]
                result = strip_layer(
                    coef, side, [strip[side, c, j] for c in every],
                    [strip_outer[side, c] if j == 0 else strip[side, c, j - 1] for c in every], down,
                    [lines[pl.ds((side * COMPS + c) * depth + j, 1), :] for c in every],
                    [strip_base[side, c, j] for c in every], [strip_now[side, c, j] for c in every],
                    [strip_prev[side, c, j] for c in every], strip_eddy[side, j],
                )
                for c in every:
                    strip_out[side, c, j] = result[c]
                    if j == depth - 1 and plan.edges:
                        put_edge(border[-1], side, c, result[c], plan.piece)


def strip_items():
    now = [(0, c, NEED, c * NEED) for c in range(COMPS)]
    rest = [(1, c, NEED - 1, c * (NEED - 1)) for c in range(COMPS)]
    return now + rest + [(2, 0, NEED - 1, COMPS * (NEED - 1))]


def gather_kernel(scalars, now, prev, eddy, *outs):
    _, _, cells, radial, axial = now.shape
    depth, size = cells - 1, radial // PARTS
    first, step = place_of(scalars, depth)
    border, now_outer, prev_outer, eddy_outer = outs[2], outs[3 : 3 + PARTS], outs[3 + PARTS : -1], outs[-1]
    for c in range(COMPS):
        for row in range(2):
            for r0 in range(0, radial, CHUNK):
                rows = pl.ds(r0, CHUNK)
                border[pl.ds((c * 2 + row) * radial + r0, CHUNK), :] = now[c, row, first + step * depth, rows, :]
                p, at_row = r0 // size, (c * 2 + row) * size + r0 % size
                now_outer[p][pl.ds(at_row, CHUNK), :] = now[c, row, first, rows, :]
                prev_outer[p][pl.ds(at_row, CHUNK), :] = prev[c, row, first, rows, :]
    for row in range(2):
        eddy_outer[row] = eddy[row, first]
    per_tile = axial // STRIP
    block = lax.broadcasted_iota(jnp.int32, (radial, axial), 1) // STRIP
    items = [(item, t) for item in strip_items() for t in range(cells)]
    outs[0][...] = jnp.zeros_like(outs[0])
    outs[1][...] = jnp.zeros_like(outs[1])
    for row in range(2):
        mine, other = outs[row], outs[1 - row]
        begin = axial - STRIP if row == 0 else 0
        for p in range(0, len(items), per_tile):
            tile = jnp.zeros((radial, axial), jnp.float32)
            for q, ((kind, c, _, _), t) in enumerate(items[p : p + per_tile]):
                value = eddy[row, t] if kind == 2 else (now, prev)[kind][c, row, t]
                shift = (q * STRIP - begin) % axial
                tile = jnp.where(block == q, pltpu.roll(value, shift, 1) if shift else value, tile)
            turned = tile.T
            for q, ((kind, _, count, at), t) in enumerate(items[p : p + per_tile]):
                start = q * STRIP + (STRIP - count if row == 0 else 0)
                value = turned[start : start + count]
                mine[pl.ds((2 * t + (kind > 0)) * HALF + at, count), :] = value
                if kind == 0 and t == (0 if row == 0 else depth):
                    other[pl.ds(2 * cells * HALF + at, count), :] = value


def align_kernel(depth, within, rotor, stator, rotor_behind, stator_ahead, *outs):
    cells = depth + 1
    edge = 2 * cells * HALF

    def block(own, side, sidestart, far, theta, half):
        at = lambda x: pl.multiple_of((2 * jnp.clip(x, 0, depth) + half) * HALF, HALF)
        near = own[pl.ds(at(theta), HALF), :]
        beside = side[pl.ds(at(theta - sidestart), HALF), :]
        value = jnp.where((theta >= 0) & (theta < cells), near, beside)
        if half == 0:
            value = jnp.where(theta == (cells if sidestart < 0 else -1), far[pl.ds(edge, HALF), :], value)
        return value

    for row, out in enumerate(outs):
        own, side, far = (rotor, rotor_behind, stator_ahead) if row == 0 else (stator, stator_ahead, rotor_behind)
        start = -within[0] if row == 0 else within[0]
        sidestart = -cells if row == 0 else cells
        for k in range(-1, cells + 1):
            for half in range(2):
                if half and k in (-1, cells):
                    continue
                at_row = 0 if k < 0 else (1 + 2 * k + half) * HALF
                out[pl.ds(at_row, HALF), :] = block(own, side, sidestart, far, start + k, half)


def scatter_kernel(depth, scalars, rotor, stator, *outs):
    cells = depth + 1
    radial = rotor.shape[-1]
    now_out, now_in, prev_out, prev_in, eddy_out, eddy_in, across, partner = outs
    first, step = place_of(scalars, depth)
    for side, ref in enumerate((stator, rotor)):
        for kind, c, count, at in strip_items():

            def read(row):
                value = ref[pl.ds(row, count), :]
                rest = jnp.zeros((STRIP - count, radial), jnp.float32)
                return jnp.concatenate([value, rest] if side == 0 else [rest, value], axis=0)

            for j in range(cells):
                start = (1 + 2 * (first + step * j) + (kind > 0)) * HALF
                value = read(pl.multiple_of(start, HALF) + at)
                if kind == 2 and j == 0:
                    eddy_out[side] = value
                elif kind == 2:
                    eddy_in[side, j - 1] = value
                elif j == 0:
                    (now_out, prev_out)[kind][side, c] = value
                else:
                    (now_in, prev_in)[kind][side, c, j - 1] = value
            if kind == 0:
                low, high = read(at), read((1 + 2 * cells) * HALF + at)
                across[side, c] = jnp.where(step > 0, low, high)
                partner[side, c] = jnp.where(step > 0, high, low)


VMEM = pl.BlockSpec(memory_space=pltpu.VMEM)
SMEM = pl.BlockSpec(memory_space=pltpu.SMEM)
ANY = pl.BlockSpec(memory_space=pl.ANY)


def run(kernel, scalars, arrays, outs, scratch, name, final=None, out_shape=None, pinned=True):
    scalars, arrays = list(scalars), list(arrays)
    if pinned:
        arrays = [pltpu.with_memory_space_constraint(x, pltpu.VMEM) for x in arrays]
    in_specs = [SMEM] * len(scalars) + [VMEM] * len(arrays)
    if out_shape is not None:
        outs, out_specs = jax.ShapeDtypeStruct(out_shape, jnp.float32), ANY
    else:
        out_specs = (VMEM,) * len(outs)
    aliases = {}
    if final is not None:
        aliases = {len(in_specs): 0}
        in_specs, arrays = in_specs + [ANY], arrays + [final]
    return pl.pallas_call(
        lambda *refs: kernel(list(refs)),
        out_shape=outs,
        in_specs=in_specs,
        out_specs=out_specs,
        input_output_aliases=aliases,
        scratch_shapes=scratch,
        compiler_params=pltpu.CompilerParams(vmem_limit_bytes=16 << 20),
        cost_estimate=pl.CostEstimate(flops=1, bytes_accessed=1, transcendentals=0),
        name=name,
    )(*scalars, *arrays)


def call_gather(scalars, now, prev, eddy):
    cells, radial, axial = now.shape[2:]
    plain = lambda *shape: jax.ShapeDtypeStruct(shape, jnp.float32)
    strips = plain(2 * HALF * cells + HALF, radial)
    part = plain(2 * COMPS * radial // PARTS, axial)
    outs = (strips,) * 2 + (plain(2 * COMPS * radial, axial),) + (part,) * (2 * PARTS) + (plain(2, radial, axial),)
    got = run(lambda refs: gather_kernel(*refs), [scalars], [now, prev, eddy], outs, [], "gather_strips")
    return got[:2], got[2], got[3 : 3 + PARTS], got[3 + PARTS : -1], got[-1]


def call_align(within, strips, cells):
    rotor, stator = strips
    moved = [shifted(rotor, 1), shifted(stator, -1)]
    rows = jax.ShapeDtypeStruct((2 * HALF * (cells + 1), rotor.shape[1]), jnp.float32)
    return run(
        lambda refs: align_kernel(cells - 1, *refs), [within.reshape(1)], [rotor, stator, *moved], (rows, rows), [],
        "align_strips", pinned=False,
    )


def call_scatter(scalars, rotor, stator, cells):
    radial = rotor.shape[1]
    shape = lambda *lead: pltpu.VMEM((2, *lead, STRIP, radial), jnp.float32)
    both = [shape(COMPS), shape(COMPS, cells - 1)]
    outs = (*both, *both, shape(), shape(cells - 1), shape(COMPS), shape(COMPS))
    return run(
        lambda refs: scatter_kernel(cells - 1, *refs), [scalars], [rotor, stator], outs, [], "scatter_strips",
        pinned=False,
    )


def shifted(value, steps):
    count = lax.axis_size("theta")
    return lax.ppermute(value, "theta", [(i, (i + steps) % count) for i in range(count)])


def across_chips(value):
    count = lax.axis_size("theta")
    pairs = [(i, (i - 1 if i % 2 == 0 else i + 1) % count) for i in range(count)]
    return lax.ppermute(value, "theta", pairs)


def within_chip(value):
    count = lax.axis_size("theta")
    return lax.ppermute(value, "theta", [(i, i ^ 1) for i in range(count)])


def faced(outer, border, rotor, stator, sectors):
    count = lax.axis_size("theta")
    if count <= 16:

        def branch(steps):
            def exchange(outer, border, rotor, stator):
                return across_chips(outer), within_chip(border), shifted(rotor, steps), shifted(stator, -steps)

            return exchange

        return lax.switch(sectors, [branch(i) for i in range(count)], outer, border, rotor, stator)
    amounts = jnp.stack([sectors, count - sectors]) % count
    stacked = jnp.stack([rotor, stator])
    for level in range((count - 1).bit_length()):
        taken = ((amounts >> level) & 1) == 1
        stacked = jnp.where(taken[:, None, None], shifted(stacked, 1 << level), stacked)
    return across_chips(outer), within_chip(border), stacked[0], stacked[1]


def per_device(state_now, state_prev, eddy_visc, mean_flow, offset):
    shape = state_now.shape
    cells, radial, axial = shape[2:]
    count = lax.axis_size("theta")
    core = lax.axis_index("theta") % 2
    scalars = scalars_of(mean_flow, jnp.where(core == 1, -1.0, 1.0).astype(jnp.float32))
    shift_cells = offset[0] % (cells * count)
    depth, size = cells - 1, radial // PARTS

    early = lax.dynamic_index_in_dim(state_now[:, :, :, :size], core * depth, 2, keepdims=False)
    across = [across_chips(early.reshape(2 * COMPS * size, axial))]
    strips, border, outer, prev_outer, eddy_outer = call_gather(scalars, state_now, state_prev, eddy_visc)
    rotor, stator = call_align(shift_cells % cells, strips, cells)
    sectors = lax.optimization_barrier((shift_cells // cells, across))[0]
    late, border, rotor, stator = faced(outer[1], border, rotor, stator, sectors)
    across.append(late)
    partner = [border]
    now_out, now_in, prev_out, prev_in, eddy_out, eddy_in, edge_across, edge_within = call_scatter(
        scalars, rotor, stator, cells
    )

    now_outer, inner, strip_out, strip_in = outer, state_now, now_out, now_in
    f32 = jnp.float32
    square = pltpu.VMEM((radial, axial), f32)
    n = 0
    for _ in range(ITERS):
        base_outer, base_inner, base_out, base_in = outer, inner, strip_out, strip_in
        for _ in SECTION_WEIGHTS:
            n += 1
            plan = Plan(n, shape)

            def outer_call(p, ordered):
                arrays = [eddy_outer, prev_outer[p], inner, strip_out, *outer, now_outer[p], base_outer[p], across[p]]
                outs = [pltpu.VMEM((2 * COMPS * size, axial), f32)]
                if p == 0 and plan.edges:
                    outs = [pltpu.VMEM((2 * COMPS * (size + EDGE), axial), f32)]
                if p == 0 and plan.strips:
                    arrays += [edge_across] if n == 1 else []
                    arrays += [strip_in, now_out, prev_out, eddy_out, base_out]
                    outs.append(pltpu.VMEM(strip_out.shape, f32))
                scratch = [square, square]
                if plan.final:
                    scratch += [pltpu.VMEM((2 * COMPS * size, axial), f32), pltpu.SemaphoreType.DMA((2 * COMPS,))]
                elif p > 0:
                    arrays.append(ordered)
                return run(
                    lambda refs: outer_kernel(plan, p, refs), [scalars], arrays, tuple(outs), scratch, "outer",
                    ordered if plan.final else None, shape if plan.final else None, n > 1,
                )

            def inner_call(ordered):
                arrays = [eddy_visc, state_prev, state_now, inner, strip_in, *outer, *partner, base_inner]
                outs = [pltpu.VMEM((COMPS, 2, depth, radial, axial), f32)]
                if plan.strips:
                    arrays += [edge_within] if n == 1 else []
                    arrays += [strip_out, now_in, prev_in, eddy_in, base_in, ordered]
                    outs += [pltpu.VMEM((plan.piece, axial), f32)] * (PIECES - 1)
                    rows = plan.piece + (2 * COMPS * EDGE if plan.edges else 0)
                    outs += [pltpu.VMEM((rows, axial), f32), pltpu.VMEM(strip_in.shape, f32)]
                scratch = [square, square]
                if plan.final:
                    scratch += [pltpu.VMEM((COMPS, 2, depth, radial, axial), f32), pltpu.SemaphoreType.DMA((depth,))]
                return run(
                    lambda refs: inner_kernel(plan, refs), [scalars], arrays, tuple(outs), scratch, "inner", None,
                    shape if plan.final else None, n > 1,
                )

            if plan.final:
                made = inner_call(None)
                for p in range(PARTS):
                    made = outer_call(p, made)
                return made
            new_outer = []
            for p in range(PARTS):
                got = outer_call(p, new_outer[-1] if p else None)
                new_outer.append(got[0])
                if p == 0:
                    new_strip_out = got[1]
            made = inner_call(new_outer[-1])
            across = [across_chips(x) for x in new_outer]
            partner = [within_chip(x) for x in made[1:-1]]
            inner, strip_in = made[0], made[-1]
            outer, strip_out = new_outer, new_strip_out


def solution(mesh):
    placed = (
        P(None, None, "theta", "groups", None),
        P(None, None, "theta", "groups", None),
        P(None, "theta", "groups", None),
        P(),
        P("groups"),
    )
    return jax.shard_map(
        per_device,
        mesh=mesh,
        in_specs=placed,
        out_specs=P(None, None, "theta", "groups", None),
        check_vma=False,
    )
```

```python
import jax
import jax.numpy as jnp
from jax import lax
from jax.experimental import pallas as pl
from jax.experimental.pallas import tpu as pltpu
from jax.sharding import PartitionSpec as P

ITERS = 2
PSEUDO_STEP = 0.2
PHYS_STEP = 1.0
SECTION_WEIGHTS = (0.6, 0.6, 1.0)
COMPS = 5
CHUNK = 32
STRIP = 8
EDGE = 4
NEED = 6
HALF = 32
PARTS = 2
PIECES = (4, 3, 3)


def scalars_of(mean_flow, sign):
    flow = jnp.concatenate([mean_flow, 1.0 / mean_flow[:, 2:3]], axis=1).reshape(-1)
    return jnp.concatenate([flow, jnp.broadcast_to(sign, (6,))])


def coefficients(scalars, row, weight):
    a = weight * PSEUDO_STEP
    axial, swirl, density, sound, inverse = (scalars[row * 5 + i] for i in range(5))
    sign = scalars[10]
    half = 0.5 * a
    mass, lift = half * density, half * inverse
    return half * axial, half * swirl * sign, mass, mass * sound * sound, lift, lift * sign, sign, a


def advance(k, f, up, down, low, high, behind, ahead, kept, eddy):
    e = k[7] * eddy
    damp = 6.0 * e + (1.5 / PHYS_STEP) * k[7]
    da = [ahead[c] - behind[c] for c in range(COMPS)]
    dt = [down[c] - up[c] for c in range(COMPS)]
    dr = [high[c] - low[c] if c >= 3 else None for c in range(COMPS)]
    div = da[1] + k[6] * dt[2] + dr[3]
    push = (k[2] * div, k[4] * da[4], k[5] * dt[4], k[4] * dr[4], k[3] * div)
    new = []
    for c in range(COMPS):
        around = ((up[c] + down[c]) + (low[c] + high[c])) + (behind[c] + ahead[c])
        new.append((kept[c] - damp * f[c]) + e * around - k[0] * da[c] - k[1] * dt[c] - push[c])
    return new


def kept_part(a, base, now, prev):
    a = a * (0.5 / PHYS_STEP)
    if base is None:
        return (1.0 + 4.0 * a) * now - a * prev
    return (base + (4.0 * a) * now) - a * prev


def layer_rows(ref, row, size, first=0):
    return lambda c, r, n: ref[pl.ds((c * 2 + row) * size + r - first, n), :]


def part_rows(ref, row, plan, p):
    whole = ref.shape[0] == 2 * COMPS * plan.radial
    return layer_rows(ref, row, plan.radial) if whole else layer_rows(ref, row, plan.size, p * plan.size)


def joined(refs, row, size):
    def read(c, r, n):
        p, q = r // size, (r + n - 1) // size
        if p == q:
            return layer_rows(refs[p], row, size, p * size)(c, r, n)
        cut = q * size - r
        return jnp.concatenate(
            [layer_rows(refs[p], row, size, p * size)(c, r, cut), layer_rows(refs[q], row, size, q * size)(c, r + cut, n - cut)]
        )

    return read


def piece_of(index):
    for at, count in enumerate(PIECES):
        if index < count:
            return at, index
        index -= count


def pieces(refs, row, size):
    def read(c, r, n):
        at, index = piece_of(c * 2 + row) if len(refs) > 1 else (0, c * 2 + row)
        return refs[at][pl.ds(index * size + r, n), :]

    return read


def plain_rows(ref, row, layer):
    return lambda c, r, n: ref[c, row, layer, pl.ds(r, n), :]


def update_rows(row, r0, radial, ghost_at, center, before, after, base, now, prev, eddy, ghosts, coef, store):
    ghost = ghosts[pl.ds(r0, CHUNK), :]
    axial = ghost.shape[-1]
    lane = lax.broadcasted_iota(jnp.int32, ghost.shape, 1)
    first, last = lane == 0, lane == axial - 1
    f, low, high, behind, ahead = [], [], [], [], []
    for c in range(COMPS):
        f.append(center(c, r0, CHUNK))
        wall = -1.0 if c == 3 else 1.0
        if r0 == 0:
            low.append(jnp.concatenate([f[c][:1] * wall, center(c, 0, CHUNK - 1)], axis=0))
        else:
            low.append(center(c, r0 - 1, CHUNK))
        if r0 + CHUNK == radial:
            high.append(jnp.concatenate([center(c, r0 + 1, CHUNK - 1), f[c][-1:] * wall], axis=0))
        else:
            high.append(center(c, r0 + 1, CHUNK))
        at = ghost_at(c)
        lower, upper = pltpu.roll(f[c], 1, 1), pltpu.roll(f[c], axial - 1, 1)
        if row == 0:
            lower = jnp.where(first, 0.0, lower)
            upper = jnp.where(last, pltpu.roll(ghost, (axial - 1 - at) % axial, 1), upper)
        else:
            lower = jnp.where(first, pltpu.roll(ghost, (axial - at) % axial, 1), lower)
            upper = jnp.where(last, f[c], upper)
        behind.append(lower)
        ahead.append(upper)
    every = range(COMPS)
    read = lambda source: [source(c, r0, CHUNK) for c in every]
    new = advance(
        coef[row], f, read(before), read(after), low, high, behind, ahead,
        [kept_part(coef[row][7], base and base(c, r0, CHUNK), now(c, r0, CHUNK), prev(c, r0, CHUNK)) for c in every],
        eddy(r0, CHUNK),
    )
    for c in every:
        store(c, r0, new[c])


def pack_columns(tile, lines, radial, columns):
    axial = tile.shape[-1]
    lane = lax.broadcasted_iota(jnp.int32, (CHUNK, axial), 1)
    for r0 in range(0, radial, CHUNK):
        packed = jnp.zeros((CHUNK, axial), jnp.float32)
        for i, (row, c, center) in enumerate(columns):
            value, shift = center(c, r0, CHUNK), (i - (axial - 1 if row == 0 else 0)) % axial
            packed = jnp.where(lane == i, pltpu.roll(value, shift, 1) if shift else value, packed)
        tile[pl.ds(r0, CHUNK), :] = packed
    lines[...] = tile[...].T


def ghost_columns(tile, columns, faces):
    tile[...] = jnp.zeros_like(tile)
    for i, (strip, side) in enumerate(faces):
        face = 0 if side == 0 else STRIP - 1
        tile[pl.ds(i, 1), :] = strip[pl.ds(face, 1), :]
    columns[...] = tile[...].T


def strip_layer(coef, side, cur, up, down, lines, base, now, prev, eddy):
    radial = eddy.shape[-1]
    sub = lax.broadcasted_iota(jnp.int32, (STRIP, radial), 0)
    lane = lax.broadcasted_iota(jnp.int32, (STRIP, radial), 1)
    low, high, behind, ahead = [], [], [], []
    for c in range(COMPS):
        value = cur[c]
        wall = -value if c == 3 else value
        lower, upper = pltpu.roll(value, 1, 0), pltpu.roll(value, STRIP - 1, 0)
        if side == 0:
            lower = jnp.where(sub == 0, lines[c], lower)
        else:
            upper = jnp.where(sub == STRIP - 1, lines[c], upper)
        low.append(jnp.where(lane == 0, wall, pltpu.roll(value, 1, 1)))
        high.append(jnp.where(lane == radial - 1, wall, pltpu.roll(value, radial - 1, 1)))
        behind.append(lower)
        ahead.append(upper)
    kept = [kept_part(coef[0][7], base[c], now[c], prev[c]) for c in range(COMPS)]
    return advance(coef[1 - side], cur, up, down, low, high, behind, ahead, kept, eddy)


def edge_of(ref, side, c, separate, offset):
    if separate:
        return ref[side, c]
    got = ref[pl.ds(offset + EDGE * (side * COMPS + c), EDGE), :]
    rest = jnp.zeros((STRIP - EDGE, got.shape[1]), jnp.float32)
    return jnp.concatenate([got, rest] if side == 0 else [rest, got], axis=0)


def put_edge(ref, side, c, value, offset):
    start = 0 if side == 0 else STRIP - EDGE
    ref[pl.ds(offset + EDGE * (side * COMPS + c), EDGE), :] = value[start : start + EDGE]


class Plan:
    def __init__(self, n, shape):
        self.weight = SECTION_WEIGHTS[(n - 1) % len(SECTION_WEIGHTS)]
        self.n, self.total = n, ITERS * len(SECTION_WEIGHTS)
        self.cells, self.radial, self.axial = shape[2:]
        self.depth, self.size = self.cells - 1, self.radial // PARTS
        self.piece = PIECES[-1] * self.radial
        self.early = n <= len(SECTION_WEIGHTS)
        self.final = n == self.total
        self.strips = n < self.total
        self.edges = n < self.total - 1


def place_of(depth):
    odd = lax.axis_index("theta") % 2 == 1
    return jnp.where(odd, depth, 0), jnp.where(odd, -1, 1)


def outer_kernel(plan, p, refs):
    size, radial = plan.size, plan.radial
    scalars, eddy, prev, inner = (refs.pop(0) for _ in range(4))
    place = place_of(plan.depth)
    coef = [coefficients(scalars, row, plan.weight) for row in range(2)]
    mine = [refs.pop(0) for _ in range(PARTS)]
    now = refs.pop(0)
    base = None if plan.early else refs.pop(0)
    across, strip = refs.pop(0), refs.pop(0)
    works = p == 0 and plan.strips
    if works:
        edges = refs.pop(0) if plan.n == 1 else across
        strip_inner, strip_now, strip_prev, strip_eddy = (refs.pop(0) for _ in range(4))
        strip_base = refs.pop(0)
    if p > 0 and not plan.final:
        refs.pop(0)
    if plan.final:
        refs.pop(0)
    out = refs.pop(0)
    if works:
        strip_out = refs.pop(0)
    tile, columns = refs.pop(0), refs.pop(0)
    if plan.final:
        made, sem = refs.pop(0), refs.pop(0)
    else:
        made = out
    copies = []
    ghost_columns(tile, columns, [(strip.at[side, c], side) for side in range(2) for c in range(COMPS)])
    for row in range(2):
        for r0 in range(p * size, (p + 1) * size, CHUNK):

            def store(c, r, value):
                made[pl.ds((c * 2 + row) * size + r - p * size, CHUNK), :] = value

            part = lambda ref: part_rows(ref, row, plan, p)
            inside = part(inner) if plan.n == 1 else plain_rows(inner, row, 0)
            update_rows(
                row, r0, radial, lambda c: row * COMPS + c, joined(mine, row, size), part(across), inside,
                None if plan.early else part(base), part(now), part(prev), lambda r, n: eddy[row, pl.ds(r, n), :], columns,
                coef, store,
            )
        if plan.final:
            for c in range(COMPS):
                source = made.at[pl.ds((c * 2 + row) * size, size), :]
                target = out.at[c, row, place[0], pl.ds(p * size, size), :]
                copies.append(pltpu.make_async_copy(source, target, sem.at[len(copies)]))
                copies[-1].start()
    for copy in copies:
        copy.wait()
    if works:
        lines = tile
        pack_columns(
            columns, lines, radial, [(row, c, joined(mine, row, size)) for row in range(2) for c in range(COMPS)]
        )
        every = range(COMPS)
        for side in range(2):
            result = strip_layer(
                coef, side, [strip[side, c] for c in every],
                [edge_of(edges, side, c, plan.n == 1, 2 * COMPS * size) for c in every],
                [strip_inner[side, c, 0] for c in every], [lines[pl.ds(side * COMPS + c, 1), :] for c in every],
                [strip_base[side, c] for c in every], [strip_now[side, c] for c in every],
                [strip_prev[side, c] for c in every], strip_eddy[side],
            )
            for c in every:
                strip_out[side, c] = result[c]
                if plan.edges:
                    put_edge(out, side, c, result[c], 2 * COMPS * size)


def inner_kernel(plan, refs):
    size, radial, depth = plan.size, plan.radial, plan.depth
    scalars, eddy, prev, now, inner, strip = (refs.pop(0) for _ in range(6))
    place = place_of(plan.depth)
    coef = [coefficients(scalars, row, plan.weight) for row in range(2)]
    if plan.n == 1:
        inner = now
    outer = [refs.pop(0) for _ in range(PARTS)]
    partner = [refs.pop(0) for _ in range(1 if plan.n == 1 else len(PIECES))]
    base = None if plan.early else refs.pop(0)
    if plan.strips:
        edges = refs.pop(0) if plan.n == 1 else partner[-1]
        strip_outer, strip_now, strip_prev, strip_eddy, strip_base = (refs.pop(0) for _ in range(5))
    if plan.strips:
        refs.pop(0)
    made = refs.pop(0)
    if plan.strips:
        border, strip_out = [refs.pop(0) for _ in PIECES], refs.pop(0)
    tile, columns = refs.pop(0), refs.pop(0)
    if plan.final:
        out, made, sem = made, refs.pop(0), refs.pop(0)
    ghost_columns(
        tile, columns, [(strip.at[side, c, j], side) for side in range(2) for c in range(COMPS) for j in range(depth)]
    )
    copies = []
    at = lambda j: place[0] + place[1] * (j + 1)
    own = lambda j: at(j) if plan.n == 1 else j
    for j in range(depth):
        for row in range(2):
            for r0 in range(0, radial, CHUNK):

                def store(c, r, value):
                    made[c, row, j, pl.ds(r, CHUNK), :] = value
                    if plan.strips and j == depth - 1:
                        piece, index = piece_of(c * 2 + row)
                        border[piece][pl.ds(index * radial + r, CHUNK), :] = value

                before = joined(outer, row, size) if j == 0 else plain_rows(inner, row, own(j - 1))
                after = pieces(partner, row, radial) if j == depth - 1 else plain_rows(inner, row, own(j + 1))
                update_rows(
                    row, r0, radial, lambda c: (row * COMPS + c) * depth + j, plain_rows(inner, row, own(j)), before,
                    after, None if plan.early else plain_rows(base, row, j), plain_rows(now, row, at(j)),
                    plain_rows(prev, row, at(j)), lambda r, n: eddy[row, at(j), pl.ds(r, n), :], columns, coef, store,
                )
        if plan.final:
            copies.append(pltpu.make_async_copy(made.at[:, :, j], out.at[:, :, at(j)], sem.at[j]))
            copies[-1].start()
    for copy in copies:
        copy.wait()
    if plan.strips:
        lines = tile
        pack_columns(
            columns, lines, radial,
            [(row, c, plain_rows(inner, row, own(j))) for row in range(2) for c in range(COMPS) for j in range(depth)],
        )
        every = range(COMPS)
        for side in range(2):
            for j in range(depth):
                if j < depth - 1:
                    down = [strip[side, c, j + 1] for c in every]
                else:
                    down = [edge_of(edges, side, c, plan.n == 1, plan.piece) for c in every]
                result = strip_layer(
                    coef, side, [strip[side, c, j] for c in every],
                    [strip_outer[side, c] if j == 0 else strip[side, c, j - 1] for c in every], down,
                    [lines[pl.ds((side * COMPS + c) * depth + j, 1), :] for c in every],
                    [strip_base[side, c, j] for c in every], [strip_now[side, c, j] for c in every],
                    [strip_prev[side, c, j] for c in every], strip_eddy[side, j],
                )
                for c in every:
                    strip_out[side, c, j] = result[c]
                    if j == depth - 1 and plan.edges:
                        put_edge(border[-1], side, c, result[c], plan.piece)


def strip_items():
    now = [(0, c, NEED, c * NEED) for c in range(COMPS)]
    rest = [(1, c, NEED - 1, c * (NEED - 1)) for c in range(COMPS)]
    return now + rest + [(2, 0, NEED - 1, COMPS * (NEED - 1))]


def border_kernel(now, out, sems):
    _, _, cells, radial, _ = now.shape
    first, size = place_of(cells - 1)[0], radial // PARTS
    copies = []
    for i in range(2 * COMPS):
        source = now.at[i // 2, i % 2, first, pl.ds(0, size), :]
        copies.append(pltpu.make_async_copy(source, out.at[pl.ds(i * size, size), :], sems.at[i]))
        copies[-1].start()
    for copy in copies:
        copy.wait()


def gather_kernel(now, prev, eddy, _, *outs):
    _, _, cells, radial, axial = now.shape
    rotor, stator, *parts = outs[: 2 + PARTS]
    next_parts, prev_parts = outs[2 + PARTS : 2 + 2 * PARTS], outs[2 + 2 * PARTS : 2 + 3 * PARTS]
    border, eddy_outer, now_held, prev_held, eddy_held, in_sems, out_sems = outs[2 + 3 * PARTS :]
    size = radial // PARTS
    _, _, cells, radial, axial = now.shape
    depth = cells - 1
    first, step = place_of(depth)
    per_tile = axial // STRIP
    block = lax.broadcasted_iota(jnp.int32, (radial, axial), 1) // STRIP
    items = [(item, t) for item in strip_items() for t in range(cells)]
    arrays = ((now, now_held), (prev, prev_held), (eddy, eddy_held))
    reads, writes = {}, []
    order = [(row, kind, c) for row in range(2) for kind, c, _, _ in strip_items()]
    for i, (row, kind, c) in enumerate(order):
        at = (row,) if kind == 2 else (c, row)
        source, held = arrays[kind]
        reads[row, kind, c] = pltpu.make_async_copy(source.at[at], held.at[at], in_sems.at[i])
        reads[row, kind, c].start()
    rotor[...] = jnp.zeros_like(rotor)
    stator[...] = jnp.zeros_like(stator)

    def write(source, target):
        writes.append(pltpu.make_async_copy(source, target, out_sems.at[len(writes)]))
        writes[-1].start()

    for row in range(2):
        mine, other = (rotor, stator) if row == 0 else (stator, rotor)
        begin = axial - STRIP if row == 0 else 0
        for p in range(0, len(items), per_tile):
            tile = jnp.zeros((radial, axial), jnp.float32)
            for q, ((kind, c, _, _), t) in enumerate(items[p : p + per_tile]):
                if t == 0:
                    reads[row, kind, c].wait()
                    rows = pl.ds((c * 2 + row) * radial, radial)
                    if kind == 0:
                        write(now_held.at[c, row, first + step * depth], border.at[rows, :])
                    if kind < 2:
                        sources = ((now_held, first, parts), (now_held, first + step, next_parts)) if kind == 0 else ()
                        for held, at_layer, targets in sources or ((prev_held, first, prev_parts),):
                            for part, ref in enumerate(targets):
                                source = held.at[c, row, at_layer, pl.ds(part * size, size), :]
                                write(source, ref.at[pl.ds((c * 2 + row) * size, size), :])
                    else:
                        write(eddy_held.at[row, first], eddy_outer.at[row])
                value = eddy_held[row, t] if kind == 2 else arrays[kind][1][c, row, t]
                shift = (q * STRIP - begin) % axial
                tile = jnp.where(block == q, pltpu.roll(value, shift, 1) if shift else value, tile)
            turned = tile.T
            for q, ((kind, _, count, at), t) in enumerate(items[p : p + per_tile]):
                start = q * STRIP + (STRIP - count if row == 0 else 0)
                value = turned[start : start + count]
                mine[pl.ds((2 * t + (kind > 0)) * HALF + at, count), :] = value
                if kind == 0 and t == (0 if row == 0 else depth):
                    other[pl.ds(2 * cells * HALF + at, count), :] = value
    for copy in writes:
        copy.wait()


def align_kernel(depth, within, rotor, stator, rotor_behind, stator_ahead, *outs):
    cells = depth + 1
    edge = 2 * cells * HALF

    def block(own, side, sidestart, far, theta, half):
        at = lambda x: pl.multiple_of((2 * jnp.clip(x, 0, depth) + half) * HALF, HALF)
        near = own[pl.ds(at(theta), HALF), :]
        beside = side[pl.ds(at(theta - sidestart), HALF), :]
        value = jnp.where((theta >= 0) & (theta < cells), near, beside)
        if half == 0:
            value = jnp.where(theta == (cells if sidestart < 0 else -1), far[pl.ds(edge, HALF), :], value)
        return value

    for row, out in enumerate(outs):
        own, side, far = (rotor, rotor_behind, stator_ahead) if row == 0 else (stator, stator_ahead, rotor_behind)
        start = -within[0] if row == 0 else within[0]
        sidestart = -cells if row == 0 else cells
        for k in range(-1, cells + 1):
            for half in range(2):
                if half and k in (-1, cells):
                    continue
                at_row = 0 if k < 0 else (1 + 2 * k + half) * HALF
                out[pl.ds(at_row, HALF), :] = block(own, side, sidestart, far, start + k, half)


def scatter_kernel(depth, rotor, stator, *outs):
    cells = depth + 1
    radial = rotor.shape[-1]
    now_out, now_in, prev_out, prev_in, eddy_out, eddy_in, across, partner = outs
    first, step = place_of(depth)
    for side, ref in enumerate((stator, rotor)):
        for kind, c, count, at in strip_items():

            def read(row):
                value = ref[pl.ds(row, count), :]
                rest = jnp.zeros((STRIP - count, radial), jnp.float32)
                return jnp.concatenate([value, rest] if side == 0 else [rest, value], axis=0)

            for j in range(cells):
                start = (1 + 2 * (first + step * j) + (kind > 0)) * HALF
                value = read(pl.multiple_of(start, HALF) + at)
                if kind == 2 and j == 0:
                    eddy_out[side] = value
                elif kind == 2:
                    eddy_in[side, j - 1] = value
                elif j == 0:
                    (now_out, prev_out)[kind][side, c] = value
                else:
                    (now_in, prev_in)[kind][side, c, j - 1] = value
            if kind == 0:
                low, high = read(at), read((1 + 2 * cells) * HALF + at)
                across[side, c] = jnp.where(step > 0, low, high)
                partner[side, c] = jnp.where(step > 0, high, low)


VMEM = pl.BlockSpec(memory_space=pltpu.VMEM)
SMEM = pl.BlockSpec(memory_space=pltpu.SMEM)
ANY = pl.BlockSpec(memory_space=pl.ANY)


def in_hbm(x):
    return pltpu.with_memory_space_constraint(x, pltpu.HBM)


def in_vmem(x):
    return pltpu.with_memory_space_constraint(x, pltpu.VMEM)


def run(kernel, scalars, arrays, outs, scratch, name, final=None, out_shape=None, pinned=0):
    scalars, arrays = list(scalars), list(arrays)
    if pinned is not None:
        arrays = [in_hbm(x) if i < pinned else in_vmem(x) for i, x in enumerate(arrays)]
    in_specs = [SMEM] * len(scalars) + [VMEM] * len(arrays)
    if out_shape is not None:
        outs, out_specs = jax.ShapeDtypeStruct(out_shape, jnp.float32), ANY
    else:
        out_specs = (VMEM,) * len(outs)
    aliases = {}
    if final is not None:
        aliases = {len(in_specs): 0}
        in_specs, arrays = in_specs + [ANY], arrays + [final]
    return pl.pallas_call(
        lambda *refs: kernel(list(refs)),
        out_shape=outs,
        in_specs=in_specs,
        out_specs=out_specs,
        input_output_aliases=aliases,
        scratch_shapes=scratch,
        compiler_params=pltpu.CompilerParams(vmem_limit_bytes=16 << 20),
        cost_estimate=pl.CostEstimate(flops=1, bytes_accessed=1, transcendentals=0),
        name=name,
    )(*scalars, *arrays)


def call_border(now):
    radial, axial = now.shape[3:]
    return pl.pallas_call(
        border_kernel,
        out_shape=pltpu.VMEM((2 * COMPS * radial // PARTS, axial), jnp.float32),
        in_specs=[ANY],
        out_specs=VMEM,
        scratch_shapes=[pltpu.SemaphoreType.DMA((2 * COMPS,))],
        compiler_params=pltpu.CompilerParams(vmem_limit_bytes=16 << 20),
        cost_estimate=pl.CostEstimate(flops=1, bytes_accessed=1, transcendentals=0),
        name="outer_layer",
    )(in_hbm(now))


def call_gather(now, prev, eddy, ordered):
    cells, radial, axial = now.shape[2:]
    strips = pltpu.VMEM((2 * HALF * cells + HALF, radial), jnp.float32)
    part = pltpu.HBM((2 * COMPS * radial // PARTS, axial), jnp.float32)
    layer = pltpu.HBM((2 * COMPS * radial, axial), jnp.float32)
    plane = pltpu.HBM((2, radial, axial), jnp.float32)
    reads = pltpu.SemaphoreType.DMA((2 * (2 * COMPS + 1),))
    writes = pltpu.SemaphoreType.DMA((2 * (COMPS + 1 + 3 * COMPS * PARTS),))
    held = [pltpu.VMEM(x.shape, jnp.float32) for x in (now, prev, eddy)]
    got = pl.pallas_call(
        gather_kernel,
        out_shape=(strips,) * 2 + (part,) * (3 * PARTS) + (layer, plane),
        in_specs=[ANY] * 4,
        out_specs=(VMEM,) * 2 + (ANY,) * (3 * PARTS + 2),
        scratch_shapes=[*held, reads, writes],
        compiler_params=pltpu.CompilerParams(vmem_limit_bytes=16 << 20),
        cost_estimate=pl.CostEstimate(flops=1, bytes_accessed=1, transcendentals=0),
        name="gather_strips",
    )(*(in_hbm(x) for x in (now, prev, eddy)), ordered)
    at = [2 + i * PARTS for i in range(4)]
    return got[:2], *(got[i : i + PARTS] for i in at[:3]), *got[at[3] :]


def call_align(within, strips, cells):
    rotor, stator = strips
    moved = [shifted(rotor, 1), shifted(stator, -1)]
    rows = jax.ShapeDtypeStruct((2 * HALF * (cells + 1), rotor.shape[1]), jnp.float32)
    return run(
        lambda refs: align_kernel(cells - 1, *refs), [within.reshape(1)], [rotor, stator, *moved], (rows, rows), [],
        "align_strips",
    )


def call_scatter(rotor, stator, cells):
    radial = rotor.shape[1]
    shape = lambda *lead: pltpu.VMEM((2, *lead, STRIP, radial), jnp.float32)
    both = [shape(COMPS), shape(COMPS, cells - 1)]
    outs = (*both, *both, shape(), shape(cells - 1), shape(COMPS), shape(COMPS))
    return run(
        lambda refs: scatter_kernel(cells - 1, *refs), [], [rotor, stator], outs, [], "scatter_strips",
        pinned=None,
    )


def shifted(value, steps):
    count = lax.axis_size("theta")
    return lax.ppermute(value, "theta", [(i, (i + steps) % count) for i in range(count)])


def across_chips(value):
    count = lax.axis_size("theta")
    pairs = [(i, (i - 1 if i % 2 == 0 else i + 1) % count) for i in range(count)]
    return lax.ppermute(value, "theta", pairs)


def within_chip(value):
    count = lax.axis_size("theta")
    return lax.ppermute(value, "theta", [(i, i ^ 1) for i in range(count)])


def faced(outer, border, rotor, stator, sectors):
    count = lax.axis_size("theta")
    if count <= 16:

        def branch(steps):
            def exchange(outer, border, rotor, stator):
                return across_chips(outer), within_chip(border), shifted(rotor, steps), shifted(stator, -steps)

            return exchange

        return lax.switch(sectors, [branch(i) for i in range(count)], outer, border, rotor, stator)
    amounts = jnp.stack([sectors, count - sectors]) % count
    stacked = jnp.stack([rotor, stator])
    for level in range((count - 1).bit_length()):
        taken = ((amounts >> level) & 1) == 1
        stacked = jnp.where(taken[:, None, None], shifted(stacked, 1 << level), stacked)
    return across_chips(outer), within_chip(border), stacked[0], stacked[1]


def per_device(state_now, state_prev, eddy_visc, mean_flow, offset):
    shape = state_now.shape
    cells, radial, axial = shape[2:]
    count = lax.axis_size("theta")
    core = lax.axis_index("theta") % 2
    scalars = scalars_of(mean_flow, jnp.where(core == 1, -1.0, 1.0).astype(jnp.float32))
    shift_cells = offset[0] % (cells * count)
    depth, size = cells - 1, radial // PARTS

    early = call_border(state_now)
    across = [across_chips(early)]
    strips, outer, next_layer, prev_outer, border, eddy_outer = call_gather(state_now, state_prev, eddy_visc, early)
    rotor, stator = call_align(shift_cells % cells, strips, cells)
    sectors = lax.optimization_barrier((shift_cells // cells, across))[0]
    late, border, rotor, stator = faced(outer[-1], border, rotor, stator, sectors)
    across.append(late)
    partner = [border]
    now_out, now_in, prev_out, prev_in, eddy_out, eddy_in, edge_across, edge_within = call_scatter(
        rotor, stator, cells
    )

    now_outer, inner, strip_out, strip_in = outer, state_now, now_out, now_in
    f32 = jnp.float32
    square = pltpu.VMEM((radial, axial), f32)
    n = 0
    for _ in range(ITERS):
        base_outer, base_inner, base_out, base_in = outer, inner, strip_out, strip_in
        for _ in SECTION_WEIGHTS:
            n += 1
            plan = Plan(n, shape)

            def outer_call(p, ordered):
                arrays = [eddy_outer, prev_outer[p], next_layer[p] if n == 1 else inner, *outer, now_outer[p]]
                arrays += [across[p]] if plan.early else [base_outer[p], across[p]]
                held, arrays = len(arrays), arrays + [strip_out]
                outs = [pltpu.VMEM((2 * COMPS * size, axial), f32)]
                if p == 0 and plan.edges:
                    outs = [pltpu.VMEM((2 * COMPS * (size + EDGE), axial), f32)]
                if p == 0 and plan.strips:
                    arrays += [edge_across] if n == 1 else []
                    arrays += [strip_in, now_out, prev_out, eddy_out, base_out]
                    outs.append(pltpu.VMEM(strip_out.shape, f32))
                scratch = [square, square]
                if plan.final:
                    scratch += [pltpu.VMEM((2 * COMPS * size, axial), f32), pltpu.SemaphoreType.DMA((2 * COMPS,))]
                elif p > 0:
                    arrays.append(ordered)
                return run(
                    lambda refs: outer_kernel(plan, p, refs), [scalars], arrays, tuple(outs), scratch, "outer",
                    ordered if plan.final else None, shape if plan.final else None, held if n == 1 else 0,
                )

            def inner_call(ordered):
                arrays = [eddy_visc, state_prev, state_now, inner, strip_in, *outer, *partner]
                arrays += [] if plan.early else [base_inner]
                outs = [pltpu.VMEM((COMPS, 2, depth, radial, axial), f32)]
                if plan.strips:
                    arrays += [edge_within] if n == 1 else []
                    arrays += [strip_out, now_in, prev_in, eddy_in, base_in, ordered]
                    outs += [pltpu.VMEM((count * radial, axial), f32) for count in PIECES[:-1]]
                    rows = plan.piece + (2 * COMPS * EDGE if plan.edges else 0)
                    outs += [pltpu.VMEM((rows, axial), f32), pltpu.VMEM(strip_in.shape, f32)]
                scratch = [square, square]
                if plan.final:
                    scratch += [pltpu.VMEM((COMPS, 2, depth, radial, axial), f32), pltpu.SemaphoreType.DMA((depth,))]
                return run(
                    lambda refs: inner_kernel(plan, refs), [scalars], arrays, tuple(outs), scratch, "inner", None,
                    shape if plan.final else None, None if n == 1 else 0,
                )

            if plan.final:
                made = inner_call(None)
                for p in range(PARTS):
                    made = outer_call(p, made)
                return made
            new_outer = []
            for p in range(PARTS):
                got = outer_call(p, new_outer[-1] if p else None)
                new_outer.append(got[0])
                if p == 0:
                    new_strip_out = got[1]
            made = inner_call(new_outer[-1])
            across = [across_chips(x) for x in new_outer]
            partner = [within_chip(x) for x in made[1:-1]]
            inner, strip_in = made[0], made[-1]
            outer, strip_out = new_outer, new_strip_out


def solution(mesh):
    placed = (
        P(None, None, "theta", "groups", None),
        P(None, None, "theta", "groups", None),
        P(None, "theta", "groups", None),
        P(),
        P("groups"),
    )
    return jax.shard_map(
        per_device,
        mesh=mesh,
        in_specs=placed,
        out_specs=P(None, None, "theta", "groups", None),
        check_vma=False,
    )
```

```python
import jax
import jax.numpy as jnp
from jax import lax
from jax.experimental import pallas as pl
from jax.experimental.pallas import tpu as pltpu
from jax.sharding import PartitionSpec as P

ITERS = 2
PSEUDO_STEP = 0.2
PHYS_STEP = 1.0
SECTION_WEIGHTS = (0.6, 0.6, 1.0)
COMPS = 5
CHUNK = 32
STRIP = 8
NEED = 6
HALF = 32
PARTS = 2
PIECES = (4, 3, 3)


def scalars_of(mean_flow, sign):
    flow = jnp.concatenate([mean_flow, 1.0 / mean_flow[:, 2:3]], axis=1).reshape(-1)
    return jnp.concatenate([flow, jnp.broadcast_to(sign, (6,))])


def coefficients(scalars, row, weight):
    a = weight * PSEUDO_STEP
    axial, swirl, density, sound, inverse = (scalars[row * 5 + i] for i in range(5))
    sign = scalars[10]
    half = 0.5 * a
    mass, lift = half * density, half * inverse
    return half * axial, half * swirl * sign, mass, mass * sound * sound, lift, lift * sign, sign, a


def advance(k, f, up, down, low, high, behind, ahead, kept, eddy):
    e = k[7] * eddy
    damp = 6.0 * e + (1.5 / PHYS_STEP) * k[7]
    da = [ahead[c] - behind[c] for c in range(COMPS)]
    dt = [down[c] - up[c] for c in range(COMPS)]
    dr = [high[c] - low[c] if c >= 3 else None for c in range(COMPS)]
    div = da[1] + k[6] * dt[2] + dr[3]
    push = (k[2] * div, k[4] * da[4], k[5] * dt[4], k[4] * dr[4], k[3] * div)
    new = []
    for c in range(COMPS):
        around = ((up[c] + down[c]) + (low[c] + high[c])) + (behind[c] + ahead[c])
        new.append((kept[c] - damp * f[c]) + e * around - k[0] * da[c] - k[1] * dt[c] - push[c])
    return new


def kept_part(a, base, now, prev):
    a = a * (0.5 / PHYS_STEP)
    if base is None:
        return (1.0 + 4.0 * a) * now - a * prev
    return (base + (4.0 * a) * now) - a * prev


def layer_rows(ref, row, size, first=0):
    return lambda c, r, n: ref[pl.ds((c * 2 + row) * size + r - first, n), :]


def part_rows(ref, row, plan, p):
    whole = ref.shape[0] == 2 * COMPS * plan.radial
    return layer_rows(ref, row, plan.radial) if whole else layer_rows(ref, row, plan.size, p * plan.size)


def joined(refs, row, size):
    def read(c, r, n):
        p, q = r // size, (r + n - 1) // size
        if p == q:
            return layer_rows(refs[p], row, size, p * size)(c, r, n)
        cut = q * size - r
        return jnp.concatenate(
            [layer_rows(refs[p], row, size, p * size)(c, r, cut), layer_rows(refs[q], row, size, q * size)(c, r + cut, n - cut)]
        )

    return read


def piece_of(index):
    for at, count in enumerate(PIECES):
        if index < count:
            return at, index
        index -= count


def pieces(refs, row, size, first=0):
    def read(c, r, n):
        at, index = piece_of(c * 2 + row)
        return refs[at][pl.ds(index * size + r - first, n), :]

    return read


def plain_rows(ref, row, layer):
    return lambda c, r, n: ref[c, row, layer, pl.ds(r, n), :]


def update_rows(row, r0, radial, ghost_at, center, before, after, base, now, prev, eddy, ghosts, coef, store):
    ghost = ghosts[pl.ds(r0, CHUNK), :]
    axial = ghost.shape[-1]
    lane = lax.broadcasted_iota(jnp.int32, ghost.shape, 1)
    first, last = lane == 0, lane == axial - 1
    f, low, high, behind, ahead = [], [], [], [], []
    for c in range(COMPS):
        f.append(center(c, r0, CHUNK))
        wall = -1.0 if c == 3 else 1.0
        if r0 == 0:
            low.append(jnp.concatenate([f[c][:1] * wall, center(c, 0, CHUNK - 1)], axis=0))
        else:
            low.append(center(c, r0 - 1, CHUNK))
        if r0 + CHUNK == radial:
            high.append(jnp.concatenate([center(c, r0 + 1, CHUNK - 1), f[c][-1:] * wall], axis=0))
        else:
            high.append(center(c, r0 + 1, CHUNK))
        at = ghost_at(c)
        lower, upper = pltpu.roll(f[c], 1, 1), pltpu.roll(f[c], axial - 1, 1)
        if row == 0:
            lower = jnp.where(first, 0.0, lower)
            upper = jnp.where(last, pltpu.roll(ghost, (axial - 1 - at) % axial, 1), upper)
        else:
            lower = jnp.where(first, pltpu.roll(ghost, (axial - at) % axial, 1), lower)
            upper = jnp.where(last, f[c], upper)
        behind.append(lower)
        ahead.append(upper)
    every = range(COMPS)
    read = lambda source: [source(c, r0, CHUNK) for c in every]
    new = advance(
        coef[row], f, read(before), read(after), low, high, behind, ahead,
        [kept_part(coef[row][7], base and base(c, r0, CHUNK), now(c, r0, CHUNK), prev(c, r0, CHUNK)) for c in every],
        eddy(r0, CHUNK),
    )
    for c in every:
        store(c, r0, new[c])


def pack_columns(tile, lines, radial, columns):
    axial = tile.shape[-1]
    lane = lax.broadcasted_iota(jnp.int32, (CHUNK, axial), 1)
    for r0 in range(0, radial, CHUNK):
        packed = jnp.zeros((CHUNK, axial), jnp.float32)
        for i, (row, c, center) in enumerate(columns):
            value, shift = center(c, r0, CHUNK), (i - (axial - 1 if row == 0 else 0)) % axial
            packed = jnp.where(lane == i, pltpu.roll(value, shift, 1) if shift else value, packed)
        tile[pl.ds(r0, CHUNK), :] = packed
    lines[...] = tile[...].T


def ghost_columns(tile, columns, faces):
    tile[...] = jnp.zeros_like(tile)
    for i, (strip, side) in enumerate(faces):
        face = 0 if side == 0 else STRIP - 1
        tile[pl.ds(i, 1), :] = strip[pl.ds(face, 1), :]
    columns[...] = tile[...].T


def strip_layer(coef, side, cur, up, down, lines, base, now, prev, eddy):
    radial = eddy.shape[-1]
    sub = lax.broadcasted_iota(jnp.int32, (STRIP, radial), 0)
    lane = lax.broadcasted_iota(jnp.int32, (STRIP, radial), 1)
    low, high, behind, ahead = [], [], [], []
    for c in range(COMPS):
        value = cur[c]
        wall = -value if c == 3 else value
        lower, upper = pltpu.roll(value, 1, 0), pltpu.roll(value, STRIP - 1, 0)
        if side == 0:
            lower = jnp.where(sub == 0, lines[c], lower)
        else:
            upper = jnp.where(sub == STRIP - 1, lines[c], upper)
        low.append(jnp.where(lane == 0, wall, pltpu.roll(value, 1, 1)))
        high.append(jnp.where(lane == radial - 1, wall, pltpu.roll(value, radial - 1, 1)))
        behind.append(lower)
        ahead.append(upper)
    kept = [kept_part(coef[0][7], base[c], now[c], prev[c]) for c in range(COMPS)]
    return advance(coef[1 - side], cur, up, down, low, high, behind, ahead, kept, eddy)


def edge_of(ref, side, c, plan, offset):
    if plan.n == 1:
        return ref[side, c]
    got = ref[pl.ds(offset + (plan.edge + 1) * (side * COMPS + c), plan.edge + 1), :]
    rest = jnp.zeros((STRIP - got.shape[0], got.shape[1]), jnp.float32)
    return jnp.concatenate([got, rest] if side == 0 else [rest, got], axis=0)


def put_edge(ref, side, c, value, plan, offset):
    start = 0 if side == 0 else STRIP - plan.edge
    ref[pl.ds(offset + plan.edge * (side * COMPS + c), plan.edge), :] = value[start : start + plan.edge]


class Plan:
    def __init__(self, n, shape):
        self.weight = SECTION_WEIGHTS[(n - 1) % len(SECTION_WEIGHTS)]
        self.n, self.total = n, ITERS * len(SECTION_WEIGHTS)
        self.cells, self.radial, self.axial = shape[2:]
        self.depth, self.size = self.cells - 1, self.radial // PARTS
        self.piece = PIECES[-1] * self.radial
        self.early = n <= len(SECTION_WEIGHTS)
        self.final = n == self.total
        self.strips = n < self.total
        self.edge = self.total - 1 - n
        self.edges = self.edge > 0


def place_of(depth):
    odd = lax.axis_index("theta") % 2 == 1
    return jnp.where(odd, depth, 0), jnp.where(odd, -1, 1)


def outer_kernel(plan, p, refs):
    size, radial = plan.size, plan.radial
    scalars, eddy, prev, inner = (refs.pop(0) for _ in range(4))
    place = place_of(plan.depth)
    coef = [coefficients(scalars, row, plan.weight) for row in range(2)]
    mine = [refs.pop(0) for _ in range(PARTS)]
    now = refs.pop(0)
    base = None if plan.early else refs.pop(0)
    split = plan.n == 1 and p == PARTS - 1
    across = [refs.pop(0) for _ in PIECES] if split else refs.pop(0)
    strip = refs.pop(0)
    works = p == 0 and plan.strips
    if works:
        edges = refs.pop(0) if plan.n == 1 else across
        strip_inner, strip_now, strip_prev, strip_eddy = (refs.pop(0) for _ in range(4))
        strip_base = refs.pop(0)
    if p > 0 and not plan.final:
        refs.pop(0)
    if plan.final:
        refs.pop(0)
    out = refs.pop(0)
    if works:
        strip_out = refs.pop(0)
    tile, columns = refs.pop(0), refs.pop(0)
    if plan.final:
        made, sem = refs.pop(0), refs.pop(0)
    else:
        made = out
    copies = []
    ghost_columns(tile, columns, [(strip.at[side, c], side) for side in range(2) for c in range(COMPS)])
    for row in range(2):
        for r0 in range(p * size, (p + 1) * size, CHUNK):

            def store(c, r, value):
                made[pl.ds((c * 2 + row) * size + r - p * size, CHUNK), :] = value

            part = lambda ref: part_rows(ref, row, plan, p)
            inside = part(inner) if plan.n == 1 else plain_rows(inner, row, 0)
            update_rows(
                row, r0, radial, lambda c: row * COMPS + c, joined(mine, row, size),
                pieces(across, row, size, p * size) if split else part(across), inside,
                None if plan.early else part(base), part(now), part(prev), lambda r, n: eddy[row, pl.ds(r, n), :], columns,
                coef, store,
            )
        if plan.final:
            for c in range(COMPS):
                source = made.at[pl.ds((c * 2 + row) * size, size), :]
                target = out.at[c, row, place[0], pl.ds(p * size, size), :]
                copies.append(pltpu.make_async_copy(source, target, sem.at[len(copies)]))
                copies[-1].start()
    for copy in copies:
        copy.wait()
    if works:
        lines = tile
        pack_columns(
            columns, lines, radial, [(row, c, joined(mine, row, size)) for row in range(2) for c in range(COMPS)]
        )
        every = range(COMPS)
        for side in range(2):
            result = strip_layer(
                coef, side, [strip[side, c] for c in every],
                [edge_of(edges, side, c, plan, 2 * COMPS * size) for c in every],
                [strip_inner[side, c, 0] for c in every], [lines[pl.ds(side * COMPS + c, 1), :] for c in every],
                [strip_base[side, c] for c in every], [strip_now[side, c] for c in every],
                [strip_prev[side, c] for c in every], strip_eddy[side],
            )
            for c in every:
                strip_out[side, c] = result[c]
                if plan.edges:
                    put_edge(out, side, c, result[c], plan, 2 * COMPS * size)


def inner_kernel(plan, refs):
    size, radial, depth = plan.size, plan.radial, plan.depth
    scalars, eddy, prev, now, inner, strip = (refs.pop(0) for _ in range(6))
    place = place_of(plan.depth)
    coef = [coefficients(scalars, row, plan.weight) for row in range(2)]
    if plan.n == 1:
        inner = now
    outer = [refs.pop(0) for _ in range(PARTS)]
    partner = [refs.pop(0) for _ in PIECES]
    base = None if plan.early else refs.pop(0)
    if plan.strips:
        edges = refs.pop(0) if plan.n == 1 else partner[-1]
        strip_outer, strip_now, strip_prev, strip_eddy, strip_base = (refs.pop(0) for _ in range(5))
    if plan.strips:
        refs.pop(0)
    made = refs.pop(0)
    if plan.strips:
        border, strip_out = [refs.pop(0) for _ in PIECES], refs.pop(0)
    tile, columns = refs.pop(0), refs.pop(0)
    if plan.final:
        out, made, sem = made, refs.pop(0), refs.pop(0)
    ghost_columns(
        tile, columns, [(strip.at[side, c, j], side) for side in range(2) for c in range(COMPS) for j in range(depth)]
    )
    copies = []
    at = lambda j: place[0] + place[1] * (j + 1)
    own = lambda j: at(j) if plan.n == 1 else j
    for j in range(depth):
        for row in range(2):
            for r0 in range(0, radial, CHUNK):

                def store(c, r, value):
                    made[c, row, j, pl.ds(r, CHUNK), :] = value
                    if plan.strips and j == depth - 1:
                        piece, index = piece_of(c * 2 + row)
                        border[piece][pl.ds(index * radial + r, CHUNK), :] = value

                before = joined(outer, row, size) if j == 0 else plain_rows(inner, row, own(j - 1))
                after = pieces(partner, row, radial) if j == depth - 1 else plain_rows(inner, row, own(j + 1))
                update_rows(
                    row, r0, radial, lambda c: (row * COMPS + c) * depth + j, plain_rows(inner, row, own(j)), before,
                    after, None if plan.early else plain_rows(base, row, j), plain_rows(now, row, at(j)),
                    plain_rows(prev, row, at(j)), lambda r, n: eddy[row, at(j), pl.ds(r, n), :], columns, coef, store,
                )
        if plan.final:
            copies.append(pltpu.make_async_copy(made.at[:, :, j], out.at[:, :, at(j)], sem.at[j]))
            copies[-1].start()
    for copy in copies:
        copy.wait()
    if plan.strips:
        lines = tile
        pack_columns(
            columns, lines, radial,
            [(row, c, plain_rows(inner, row, own(j))) for row in range(2) for c in range(COMPS) for j in range(depth)],
        )
        every = range(COMPS)
        for side in range(2):
            for j in range(depth):
                if j < depth - 1:
                    down = [strip[side, c, j + 1] for c in every]
                else:
                    down = [edge_of(edges, side, c, plan, plan.piece) for c in every]
                result = strip_layer(
                    coef, side, [strip[side, c, j] for c in every],
                    [strip_outer[side, c] if j == 0 else strip[side, c, j - 1] for c in every], down,
                    [lines[pl.ds((side * COMPS + c) * depth + j, 1), :] for c in every],
                    [strip_base[side, c, j] for c in every], [strip_now[side, c, j] for c in every],
                    [strip_prev[side, c, j] for c in every], strip_eddy[side, j],
                )
                for c in every:
                    strip_out[side, c, j] = result[c]
                    if j == depth - 1 and plan.edges:
                        put_edge(border[-1], side, c, result[c], plan, plan.piece)


def strip_items():
    now = [(0, c, NEED, c * NEED) for c in range(COMPS)]
    rest = [(1, c, NEED - 1, c * (NEED - 1)) for c in range(COMPS)]
    return now + rest + [(2, 0, NEED - 1, COMPS * (NEED - 1))]


def border_kernel(now, out, sems):
    _, _, cells, radial, _ = now.shape
    first, size = place_of(cells - 1)[0], radial // PARTS
    copies = []
    for i in range(2 * COMPS):
        source = now.at[i // 2, i % 2, first, pl.ds(0, size), :]
        copies.append(pltpu.make_async_copy(source, out.at[pl.ds(i * size, size), :], sems.at[i]))
        copies[-1].start()
    for copy in copies:
        copy.wait()


def gather_kernel(now, prev, eddy, _, *outs):
    _, _, cells, radial, axial = now.shape
    rotor, stator, *parts = outs[: 2 + PARTS]
    next_parts, prev_parts = outs[2 + PARTS : 2 + 2 * PARTS], outs[2 + 2 * PARTS : 2 + 3 * PARTS]
    border, rest = outs[2 + 3 * PARTS :][: len(PIECES)], outs[2 + 3 * PARTS + len(PIECES) :]
    late, (eddy_outer, now_held, prev_held, eddy_held, in_sems, out_sems) = rest[: len(PIECES)], rest[len(PIECES) :]
    size = radial // PARTS
    _, _, cells, radial, axial = now.shape
    depth = cells - 1
    first, step = place_of(depth)
    per_tile = axial // STRIP
    block = lax.broadcasted_iota(jnp.int32, (radial, axial), 1) // STRIP
    items = [(item, t) for item in strip_items() for t in range(cells)]
    arrays = ((now, now_held), (prev, prev_held), (eddy, eddy_held))
    reads, writes = {}, []
    order = [(row, kind, c) for row in range(2) for kind, c, _, _ in strip_items()]
    for i, (row, kind, c) in enumerate(order):
        at = (row,) if kind == 2 else (c, row)
        source, held = arrays[kind]
        reads[row, kind, c] = pltpu.make_async_copy(source.at[at], held.at[at], in_sems.at[i])
        reads[row, kind, c].start()
    rotor[...] = jnp.zeros_like(rotor)
    stator[...] = jnp.zeros_like(stator)

    def write(source, target):
        writes.append(pltpu.make_async_copy(source, target, out_sems.at[len(writes)]))
        writes[-1].start()

    for row in range(2):
        mine, other = (rotor, stator) if row == 0 else (stator, rotor)
        begin = axial - STRIP if row == 0 else 0
        for p in range(0, len(items), per_tile):
            tile = jnp.zeros((radial, axial), jnp.float32)
            for q, ((kind, c, _, _), t) in enumerate(items[p : p + per_tile]):
                if t == 0:
                    reads[row, kind, c].wait()
                    if kind == 0:
                        at_piece, index = piece_of(c * 2 + row)
                        target = border[at_piece].at[pl.ds(index * radial, radial), :]
                        write(now_held.at[c, row, first + step * depth], target)
                        target = late[at_piece].at[pl.ds(index * size, size), :]
                        write(now_held.at[c, row, first, pl.ds(radial - size, size), :], target)
                    if kind < 2:
                        sources = ((now_held, first, parts), (now_held, first + step, next_parts)) if kind == 0 else ()
                        for held, at_layer, targets in sources or ((prev_held, first, prev_parts),):
                            for part, ref in enumerate(targets):
                                source = held.at[c, row, at_layer, pl.ds(part * size, size), :]
                                write(source, ref.at[pl.ds((c * 2 + row) * size, size), :])
                    else:
                        write(eddy_held.at[row, first], eddy_outer.at[row])
                value = eddy_held[row, t] if kind == 2 else arrays[kind][1][c, row, t]
                shift = (q * STRIP - begin) % axial
                tile = jnp.where(block == q, pltpu.roll(value, shift, 1) if shift else value, tile)
            turned = tile.T
            for q, ((kind, _, count, at), t) in enumerate(items[p : p + per_tile]):
                start = q * STRIP + (STRIP - count if row == 0 else 0)
                value = turned[start : start + count]
                mine[pl.ds((2 * t + (kind > 0)) * HALF + at, count), :] = value
                if kind == 0 and t == (0 if row == 0 else depth):
                    other[pl.ds(2 * cells * HALF + at, count), :] = value
    for copy in writes:
        copy.wait()


def align_kernel(depth, within, rotor, stator, rotor_behind, stator_ahead, *outs):
    cells = depth + 1
    edge = 2 * cells * HALF

    def block(own, side, sidestart, far, theta, half):
        at = lambda x: pl.multiple_of((2 * jnp.clip(x, 0, depth) + half) * HALF, HALF)
        near = own[pl.ds(at(theta), HALF), :]
        beside = side[pl.ds(at(theta - sidestart), HALF), :]
        value = jnp.where((theta >= 0) & (theta < cells), near, beside)
        if half == 0:
            value = jnp.where(theta == (cells if sidestart < 0 else -1), far[pl.ds(edge, HALF), :], value)
        return value

    for row, out in enumerate(outs):
        own, side, far = (rotor, rotor_behind, stator_ahead) if row == 0 else (stator, stator_ahead, rotor_behind)
        start = -within[0] if row == 0 else within[0]
        sidestart = -cells if row == 0 else cells
        for k in range(-1, cells + 1):
            for half in range(2):
                if half and k in (-1, cells):
                    continue
                at_row = 0 if k < 0 else (1 + 2 * k + half) * HALF
                out[pl.ds(at_row, HALF), :] = block(own, side, sidestart, far, start + k, half)


def scatter_kernel(depth, rotor, stator, *outs):
    cells = depth + 1
    radial = rotor.shape[-1]
    now_out, now_in, prev_out, prev_in, eddy_out, eddy_in, across, partner = outs
    first, step = place_of(depth)
    for side, ref in enumerate((stator, rotor)):
        for kind, c, count, at in strip_items():

            def read(row):
                value = ref[pl.ds(row, count), :]
                rest = jnp.zeros((STRIP - count, radial), jnp.float32)
                return jnp.concatenate([value, rest] if side == 0 else [rest, value], axis=0)

            for j in range(cells):
                start = (1 + 2 * (first + step * j) + (kind > 0)) * HALF
                value = read(pl.multiple_of(start, HALF) + at)
                if kind == 2 and j == 0:
                    eddy_out[side] = value
                elif kind == 2:
                    eddy_in[side, j - 1] = value
                elif j == 0:
                    (now_out, prev_out)[kind][side, c] = value
                else:
                    (now_in, prev_in)[kind][side, c, j - 1] = value
            if kind == 0:
                low, high = read(at), read((1 + 2 * cells) * HALF + at)
                across[side, c] = jnp.where(step > 0, low, high)
                partner[side, c] = jnp.where(step > 0, high, low)


VMEM = pl.BlockSpec(memory_space=pltpu.VMEM)
SMEM = pl.BlockSpec(memory_space=pltpu.SMEM)
ANY = pl.BlockSpec(memory_space=pl.ANY)


def in_hbm(x):
    return pltpu.with_memory_space_constraint(x, pltpu.HBM)


def in_vmem(x):
    return pltpu.with_memory_space_constraint(x, pltpu.VMEM)


def run(kernel, scalars, arrays, outs, scratch, name, final=None, out_shape=None, pinned=0):
    scalars, arrays = list(scalars), list(arrays)
    if pinned is not None:
        arrays = [in_hbm(x) if i < pinned else in_vmem(x) for i, x in enumerate(arrays)]
    in_specs = [SMEM] * len(scalars) + [VMEM] * len(arrays)
    if out_shape is not None:
        outs, out_specs = jax.ShapeDtypeStruct(out_shape, jnp.float32), ANY
    else:
        out_specs = (VMEM,) * len(outs)
    aliases = {}
    if final is not None:
        aliases = {len(in_specs): 0}
        in_specs, arrays = in_specs + [ANY], arrays + [final]
    return pl.pallas_call(
        lambda *refs: kernel(list(refs)),
        out_shape=outs,
        in_specs=in_specs,
        out_specs=out_specs,
        input_output_aliases=aliases,
        scratch_shapes=scratch,
        compiler_params=pltpu.CompilerParams(vmem_limit_bytes=16 << 20),
        cost_estimate=pl.CostEstimate(flops=1, bytes_accessed=1, transcendentals=0),
        name=name,
    )(*scalars, *arrays)


def call_border(now):
    radial, axial = now.shape[3:]
    return pl.pallas_call(
        border_kernel,
        out_shape=pltpu.VMEM((2 * COMPS * radial // PARTS, axial), jnp.float32),
        in_specs=[ANY],
        out_specs=VMEM,
        scratch_shapes=[pltpu.SemaphoreType.DMA((2 * COMPS,))],
        compiler_params=pltpu.CompilerParams(vmem_limit_bytes=16 << 20),
        cost_estimate=pl.CostEstimate(flops=1, bytes_accessed=1, transcendentals=0),
        name="outer_layer",
    )(in_hbm(now))


def call_gather(now, prev, eddy, ordered):
    cells, radial, axial = now.shape[2:]
    strips = pltpu.VMEM((2 * HALF * cells + HALF, radial), jnp.float32)
    part = pltpu.HBM((2 * COMPS * radial // PARTS, axial), jnp.float32)
    border = [pltpu.HBM((count * radial, axial), jnp.float32) for count in PIECES]
    late = [pltpu.HBM((count * radial // PARTS, axial), jnp.float32) for count in PIECES]
    plane = pltpu.HBM((2, radial, axial), jnp.float32)
    reads = pltpu.SemaphoreType.DMA((2 * (2 * COMPS + 1),))
    writes = pltpu.SemaphoreType.DMA((2 * (2 * COMPS + 1 + 3 * COMPS * PARTS),))
    held = [pltpu.VMEM(x.shape, jnp.float32) for x in (now, prev, eddy)]
    got = pl.pallas_call(
        gather_kernel,
        out_shape=(strips,) * 2 + (part,) * (3 * PARTS) + (*border, *late, plane),
        in_specs=[ANY] * 4,
        out_specs=(VMEM,) * 2 + (ANY,) * (3 * PARTS + 1 + 2 * len(PIECES)),
        scratch_shapes=[*held, reads, writes],
        compiler_params=pltpu.CompilerParams(vmem_limit_bytes=16 << 20),
        cost_estimate=pl.CostEstimate(flops=1, bytes_accessed=1, transcendentals=0),
        name="gather_strips",
    )(*(in_hbm(x) for x in (now, prev, eddy)), ordered)
    at = [2 + i * PARTS for i in range(4)]
    ends = at[3] + len(PIECES)
    return got[:2], *(got[i : i + PARTS] for i in at[:3]), got[at[3] : ends], got[ends:-1], got[-1]


def call_align(within, strips, cells):
    rotor, stator = strips
    moved = [shifted(rotor, 1), shifted(stator, -1)]
    rows = jax.ShapeDtypeStruct((2 * HALF * (cells + 1), rotor.shape[1]), jnp.float32)
    return run(
        lambda refs: align_kernel(cells - 1, *refs), [within.reshape(1)], [rotor, stator, *moved], (rows, rows), [],
        "align_strips",
    )


def call_scatter(rotor, stator, cells):
    radial = rotor.shape[1]
    shape = lambda *lead: pltpu.VMEM((2, *lead, STRIP, radial), jnp.float32)
    both = [shape(COMPS), shape(COMPS, cells - 1)]
    outs = (*both, *both, shape(), shape(cells - 1), shape(COMPS), shape(COMPS))
    return run(
        lambda refs: scatter_kernel(cells - 1, *refs), [], [rotor, stator], outs, [], "scatter_strips",
        pinned=None,
    )


def shifted(value, steps):
    count = lax.axis_size("theta")
    return lax.ppermute(value, "theta", [(i, (i + steps) % count) for i in range(count)])


def across_chips(value):
    count = lax.axis_size("theta")
    pairs = [(i, (i - 1 if i % 2 == 0 else i + 1) % count) for i in range(count)]
    return lax.ppermute(value, "theta", pairs)


def within_chip(value):
    count = lax.axis_size("theta")
    return lax.ppermute(value, "theta", [(i, i ^ 1) for i in range(count)])


def faced(outer, rotor, stator, sectors):
    count = lax.axis_size("theta")
    if count <= 16:

        def branch(steps):
            def exchange(outer, rotor, stator):
                return [across_chips(x) for x in outer], shifted(rotor, steps), shifted(stator, -steps)

            return exchange

        return lax.switch(sectors, [branch(i) for i in range(count)], outer, rotor, stator)
    amounts = jnp.stack([sectors, count - sectors]) % count
    stacked = jnp.stack([rotor, stator])
    for level in range((count - 1).bit_length()):
        taken = ((amounts >> level) & 1) == 1
        stacked = jnp.where(taken[:, None, None], shifted(stacked, 1 << level), stacked)
    return [across_chips(x) for x in outer], stacked[0], stacked[1]


def per_device(state_now, state_prev, eddy_visc, mean_flow, offset):
    shape = state_now.shape
    cells, radial, axial = shape[2:]
    count = lax.axis_size("theta")
    core = lax.axis_index("theta") % 2
    scalars = scalars_of(mean_flow, jnp.where(core == 1, -1.0, 1.0).astype(jnp.float32))
    shift_cells = offset[0] % (cells * count)
    depth, size = cells - 1, radial // PARTS

    early = call_border(state_now)
    across = [across_chips(early)]
    strips, outer, next_layer, prev_outer, border, late, eddy_outer = call_gather(
        state_now, state_prev, eddy_visc, early
    )
    rotor, stator = call_align(shift_cells % cells, strips, cells)
    sectors = lax.optimization_barrier((shift_cells // cells, across))[0]
    late, rotor, stator = faced(late, rotor, stator, sectors)
    across.append(late)
    partner = [within_chip(x) for x in border]
    now_out, now_in, prev_out, prev_in, eddy_out, eddy_in, edge_across, edge_within = call_scatter(
        rotor, stator, cells
    )

    now_outer, inner, strip_out, strip_in = outer, state_now, now_out, now_in
    f32 = jnp.float32
    square = pltpu.VMEM((radial, axial), f32)
    n = 0
    for _ in range(ITERS):
        base_outer, base_inner, base_out, base_in = outer, inner, strip_out, strip_in
        for _ in SECTION_WEIGHTS:
            n += 1
            plan = Plan(n, shape)

            def outer_call(p, ordered):
                arrays = [eddy_outer, prev_outer[p], next_layer[p] if n == 1 else inner, *outer, now_outer[p]]
                arrays += [] if plan.early else [base_outer[p]]
                arrays += across[p] if n == 1 and p == PARTS - 1 else [across[p]]
                held, arrays = len(arrays), arrays + [strip_out]
                outs = [pltpu.VMEM((2 * COMPS * size, axial), f32)]
                if p == 0 and plan.edges:
                    outs = [pltpu.VMEM((2 * COMPS * (size + plan.edge), axial), f32)]
                if p == 0 and plan.strips:
                    arrays += [edge_across] if n == 1 else []
                    arrays += [strip_in, now_out, prev_out, eddy_out, base_out]
                    outs.append(pltpu.VMEM(strip_out.shape, f32))
                scratch = [square, square]
                if plan.final:
                    scratch += [pltpu.VMEM((2 * COMPS * size, axial), f32), pltpu.SemaphoreType.DMA((2 * COMPS,))]
                elif p > 0:
                    arrays.append(ordered)
                return run(
                    lambda refs: outer_kernel(plan, p, refs), [scalars], arrays, tuple(outs), scratch, "outer",
                    ordered if plan.final else None, shape if plan.final else None, held if n == 1 else 0,
                )

            def inner_call(ordered):
                arrays = [eddy_visc, state_prev, state_now, inner, strip_in, *outer, *partner]
                arrays += [] if plan.early else [base_inner]
                outs = [pltpu.VMEM((COMPS, 2, depth, radial, axial), f32)]
                if plan.strips:
                    arrays += [edge_within] if n == 1 else []
                    arrays += [strip_out, now_in, prev_in, eddy_in, base_in, ordered]
                    outs += [pltpu.VMEM((count * radial, axial), f32) for count in PIECES[:-1]]
                    rows = plan.piece + 2 * COMPS * plan.edge
                    outs += [pltpu.VMEM((rows, axial), f32), pltpu.VMEM(strip_in.shape, f32)]
                scratch = [square, square]
                if plan.final:
                    scratch += [pltpu.VMEM((COMPS, 2, depth, radial, axial), f32), pltpu.SemaphoreType.DMA((depth,))]
                return run(
                    lambda refs: inner_kernel(plan, refs), [scalars], arrays, tuple(outs), scratch, "inner", None,
                    shape if plan.final else None, None if n == 1 else 0,
                )

            if plan.final:
                made = inner_call(None)
                for p in range(PARTS):
                    made = outer_call(p, made)
                return made
            got, new_strip_out = outer_call(0, None)
            new_outer = [got]
            if n > 1:
                made = inner_call(got)
            for p in range(1, PARTS):
                new_outer.append(outer_call(p, made[1] if n > 1 else new_outer[-1])[0])
            if n == 1:
                made = inner_call(new_outer[-1])
            across = [across_chips(x) for x in new_outer]
            partner = [within_chip(x) for x in made[1:-1]]
            inner, strip_in = made[0], made[-1]
            outer, strip_out = new_outer, new_strip_out


def solution(mesh):
    placed = (
        P(None, None, "theta", "groups", None),
        P(None, None, "theta", "groups", None),
        P(None, "theta", "groups", None),
        P(),
        P("groups"),
    )
    return jax.shard_map(
        per_device,
        mesh=mesh,
        in_specs=placed,
        out_specs=P(None, None, "theta", "groups", None),
        check_vma=False,
    )
```

```python
import jax
import jax.numpy as jnp
from jax import lax
from jax.experimental import pallas as pl
from jax.experimental.pallas import tpu as pltpu
from jax.sharding import PartitionSpec as P

ITERS = 2
PSEUDO_STEP = 0.2
PHYS_STEP = 1.0
SECTION_WEIGHTS = (0.6, 0.6, 1.0)
COMPS = 5
CHUNK = 16
STRIP = 8
NEED = 6
HALF = 32
PARTS = 2
PIECES = (4, 3, 3)


def scalars_of(mean_flow, sign, lanes):
    flow = jnp.concatenate([mean_flow, 1.0 / mean_flow[:, 2:3]], axis=1).reshape(-1)
    return jnp.broadcast_to(jnp.concatenate([flow, jnp.broadcast_to(sign, (6,))])[:, None], (16, lanes))


def coefficients(scalars, row, weight):
    a = weight * PSEUDO_STEP
    axial, swirl, density, sound, inverse = (scalars[pl.ds(row * 5 + i, 1), :] for i in range(5))
    sign = scalars[pl.ds(10, 1), :]
    half = 0.5 * a
    mass, lift = half * density, half * inverse
    return half * axial, half * swirl * sign, mass, mass * sound * sound, lift, lift * sign, sign, a


def advance(k, f, up, down, low, high, behind, ahead, kept, eddy):
    e = k[7] * eddy
    damp = 6.0 * e + (1.5 / PHYS_STEP) * k[7]
    to_ahead, to_behind, to_down, to_up = e - k[0], e + k[0], e - k[1], e + k[1]
    div = (ahead[1] - behind[1]) + k[6] * (down[2] - up[2]) + (high[3] - low[3])
    push = (
        k[2] * div, k[4] * (ahead[4] - behind[4]), k[5] * (down[4] - up[4]), k[4] * (high[4] - low[4]), k[3] * div,
    )
    new = []
    for c in range(COMPS):
        axial = to_ahead * ahead[c] + to_behind * behind[c]
        theta = to_down * down[c] + to_up * up[c]
        own = (kept[c] - push[c]) - damp * f[c]
        new.append((own + e * (low[c] + high[c])) + (axial + theta))
    return new


def kept_part(a, base, now, prev):
    a = a * (0.5 / PHYS_STEP)
    if base is None:
        return (1.0 + 4.0 * a) * now - a * prev
    return (base + (4.0 * a) * now) - a * prev


def layer_rows(ref, row, size, first=0):
    return lambda c, r, n: ref[pl.ds((c * 2 + row) * size + r - first, n), :]


def part_rows(ref, row, plan, p):
    whole = ref.shape[0] == 2 * COMPS * plan.radial
    return layer_rows(ref, row, plan.radial) if whole else layer_rows(ref, row, plan.size, p * plan.size)


def joined(refs, row, size):
    def read(c, r, n):
        p, q = r // size, (r + n - 1) // size
        if p == q:
            return layer_rows(refs[p], row, size, p * size)(c, r, n)
        cut = q * size - r
        return jnp.concatenate(
            [layer_rows(refs[p], row, size, p * size)(c, r, cut), layer_rows(refs[q], row, size, q * size)(c, r + cut, n - cut)]
        )

    return read


def piece_of(index):
    for at, count in enumerate(PIECES):
        if index < count:
            return at, index
        index -= count


def pieces(refs, row, size, first=0):
    def read(c, r, n):
        at, index = piece_of(c * 2 + row)
        return refs[at][pl.ds(index * size + r - first, n), :]

    return read


def plain_rows(ref, row, layer):
    return lambda c, r, n: ref[c, row, layer, pl.ds(r, n), :]


def update_rows(row, r0, radial, ghost_at, center, before, after, base, now, prev, eddy, ghosts, coef, store):
    ghost = ghosts[pl.ds(r0, CHUNK), :]
    axial = ghost.shape[-1]
    lane = lax.broadcasted_iota(jnp.int32, ghost.shape, 1)
    first, last = lane == 0, lane == axial - 1
    f, low, high, behind, ahead = [], [], [], [], []
    for c in range(COMPS):
        f.append(center(c, r0, CHUNK))
        wall = -1.0 if c == 3 else 1.0
        if r0 == 0:
            low.append(jnp.concatenate([f[c][:1] * wall, center(c, 0, CHUNK - 1)], axis=0))
        else:
            low.append(center(c, r0 - 1, CHUNK))
        if r0 + CHUNK == radial:
            high.append(jnp.concatenate([center(c, r0 + 1, CHUNK - 1), f[c][-1:] * wall], axis=0))
        else:
            high.append(center(c, r0 + 1, CHUNK))
        at = ghost_at(c)
        lower, upper = pltpu.roll(f[c], 1, 1), pltpu.roll(f[c], axial - 1, 1)
        if row == 0:
            lower = jnp.where(first, 0.0, lower)
            upper = jnp.where(last, pltpu.roll(ghost, (axial - 1 - at) % axial, 1), upper)
        else:
            lower = jnp.where(first, pltpu.roll(ghost, (axial - at) % axial, 1), lower)
            upper = jnp.where(last, f[c], upper)
        behind.append(lower)
        ahead.append(upper)
    every = range(COMPS)
    read = lambda source: [source(c, r0, CHUNK) for c in every]
    new = advance(
        coef[row], f, read(before), read(after), low, high, behind, ahead,
        [kept_part(coef[row][7], base and base(c, r0, CHUNK), now(c, r0, CHUNK), prev(c, r0, CHUNK)) for c in every],
        eddy(r0, CHUNK),
    )
    for c in every:
        store(c, r0, new[c])


def pack_columns(tile, lines, radial, columns):
    axial = tile.shape[-1]
    lane = lax.broadcasted_iota(jnp.int32, (CHUNK, axial), 1)
    for r0 in range(0, radial, CHUNK):
        packed = jnp.zeros((CHUNK, axial), jnp.float32)
        for i, (row, c, center) in enumerate(columns):
            value, shift = center(c, r0, CHUNK), (i - (axial - 1 if row == 0 else 0)) % axial
            packed = jnp.where(lane == i, pltpu.roll(value, shift, 1) if shift else value, packed)
        tile[pl.ds(r0, CHUNK), :] = packed
    lines[...] = tile[...].T


def ghost_columns(tile, columns, faces):
    tile[...] = jnp.zeros_like(tile)
    for i, (strip, side) in enumerate(faces):
        face = 0 if side == 0 else STRIP - 1
        tile[pl.ds(i, 1), :] = strip[pl.ds(face, 1), :]
    columns[...] = tile[...].T


def strip_layer(coef, side, cur, up, down, lines, base, now, prev, eddy):
    radial = eddy.shape[-1]
    sub = lax.broadcasted_iota(jnp.int32, (STRIP, radial), 0)
    lane = lax.broadcasted_iota(jnp.int32, (STRIP, radial), 1)
    low, high, behind, ahead = [], [], [], []
    for c in range(COMPS):
        value = cur[c]
        wall = -value if c == 3 else value
        lower, upper = pltpu.roll(value, 1, 0), pltpu.roll(value, STRIP - 1, 0)
        if side == 0:
            lower = jnp.where(sub == 0, lines[c], lower)
        else:
            upper = jnp.where(sub == STRIP - 1, lines[c], upper)
        low.append(jnp.where(lane == 0, wall, pltpu.roll(value, 1, 1)))
        high.append(jnp.where(lane == radial - 1, wall, pltpu.roll(value, radial - 1, 1)))
        behind.append(lower)
        ahead.append(upper)
    kept = [kept_part(coef[0][7], base[c], now[c], prev[c]) for c in range(COMPS)]
    return advance(coef[1 - side], cur, up, down, low, high, behind, ahead, kept, eddy)


def edge_of(ref, side, c, plan, offset):
    if plan.n == 1:
        return ref[side, c]
    got = ref[pl.ds(offset + (plan.edge + 1) * (side * COMPS + c), plan.edge + 1), :]
    rest = jnp.zeros((STRIP - got.shape[0], got.shape[1]), jnp.float32)
    return jnp.concatenate([got, rest] if side == 0 else [rest, got], axis=0)


def put_edge(ref, side, c, value, plan, offset):
    start = 0 if side == 0 else STRIP - plan.edge
    ref[pl.ds(offset + plan.edge * (side * COMPS + c), plan.edge), :] = value[start : start + plan.edge]


class Plan:
    def __init__(self, n, shape):
        self.weight = SECTION_WEIGHTS[(n - 1) % len(SECTION_WEIGHTS)]
        self.n, self.total = n, ITERS * len(SECTION_WEIGHTS)
        self.cells, self.radial, self.axial = shape[2:]
        self.depth, self.size = self.cells - 1, self.radial // PARTS
        self.piece = PIECES[-1] * self.radial
        self.early = n <= len(SECTION_WEIGHTS)
        self.final = n == self.total
        self.strips = n < self.total
        self.edge = self.total - 1 - n
        self.edges = self.edge > 0


def place_of(depth):
    odd = lax.axis_index("theta") % 2 == 1
    return jnp.where(odd, depth, 0), jnp.where(odd, -1, 1)


def outer_kernel(plan, p, refs):
    size, radial = plan.size, plan.radial
    scalars, eddy, prev, inner = (refs.pop(0) for _ in range(4))
    place = place_of(plan.depth)
    coef = [coefficients(scalars, row, plan.weight) for row in range(2)]
    mine = [refs.pop(0) for _ in range(PARTS)]
    now = refs.pop(0)
    base = None if plan.early else refs.pop(0)
    split = plan.n == 1 and p == PARTS - 1
    across = [refs.pop(0) for _ in PIECES] if split else refs.pop(0)
    strip = refs.pop(0)
    works = p == 0 and plan.strips
    if works:
        edges = refs.pop(0) if plan.n == 1 else across
        strip_inner, strip_now, strip_prev, strip_eddy = (refs.pop(0) for _ in range(4))
        strip_base = refs.pop(0)
    if p > 0 and not plan.final:
        refs.pop(0)
    if plan.final:
        refs.pop(0)
    out = refs.pop(0)
    if works:
        strip_out = refs.pop(0)
    tile, columns = refs.pop(0), refs.pop(0)
    if plan.final:
        made, sem = refs.pop(0), refs.pop(0)
    else:
        made = out
    copies = []
    ghost_columns(tile, columns, [(strip.at[side, c], side) for side in range(2) for c in range(COMPS)])
    for row in range(2):
        for r0 in range(p * size, (p + 1) * size, CHUNK):

            def store(c, r, value):
                made[pl.ds((c * 2 + row) * size + r - p * size, CHUNK), :] = value

            part = lambda ref: part_rows(ref, row, plan, p)
            inside = part(inner) if plan.n == 1 else plain_rows(inner, row, 0)
            update_rows(
                row, r0, radial, lambda c: row * COMPS + c, joined(mine, row, size),
                pieces(across, row, size, p * size) if split else part(across), inside,
                None if plan.early else part(base), part(now), part(prev), lambda r, n: eddy[row, pl.ds(r, n), :], columns,
                coef, store,
            )
        if plan.final:
            for c in range(COMPS):
                source = made.at[pl.ds((c * 2 + row) * size, size), :]
                target = out.at[c, row, place[0], pl.ds(p * size, size), :]
                copies.append(pltpu.make_async_copy(source, target, sem.at[len(copies)]))
                copies[-1].start()
    for copy in copies:
        copy.wait()
    if works:
        lines = tile
        pack_columns(
            columns, lines, radial, [(row, c, joined(mine, row, size)) for row in range(2) for c in range(COMPS)]
        )
        every = range(COMPS)
        for side in range(2):
            result = strip_layer(
                coef, side, [strip[side, c] for c in every],
                [edge_of(edges, side, c, plan, 2 * COMPS * size) for c in every],
                [strip_inner[side, c, 0] for c in every], [lines[pl.ds(side * COMPS + c, 1), :] for c in every],
                [strip_base[side, c] for c in every], [strip_now[side, c] for c in every],
                [strip_prev[side, c] for c in every], strip_eddy[side],
            )
            for c in every:
                strip_out[side, c] = result[c]
                if plan.edges:
                    put_edge(out, side, c, result[c], plan, 2 * COMPS * size)


def inner_kernel(plan, refs):
    size, radial, depth = plan.size, plan.radial, plan.depth
    scalars, eddy, prev, now, inner, strip = (refs.pop(0) for _ in range(6))
    place = place_of(plan.depth)
    coef = [coefficients(scalars, row, plan.weight) for row in range(2)]
    if plan.n == 1:
        inner = now
    outer = [refs.pop(0) for _ in range(PARTS)]
    partner = [refs.pop(0) for _ in PIECES]
    base = None if plan.early else refs.pop(0)
    if plan.strips:
        edges = refs.pop(0) if plan.n == 1 else partner[-1]
        strip_outer, strip_now, strip_prev, strip_eddy, strip_base = (refs.pop(0) for _ in range(5))
    if plan.strips:
        refs.pop(0)
    made = refs.pop(0)
    if plan.strips:
        border, strip_out = [refs.pop(0) for _ in PIECES], refs.pop(0)
    tile, columns = refs.pop(0), refs.pop(0)
    if plan.final:
        out, made, sem = made, refs.pop(0), refs.pop(0)
    ghost_columns(
        tile, columns, [(strip.at[side, c, j], side) for side in range(2) for c in range(COMPS) for j in range(depth)]
    )
    copies = []
    at = lambda j: place[0] + place[1] * (j + 1)
    own = lambda j: at(j) if plan.n == 1 else j
    for j in range(depth):
        for row in range(2):
            for r0 in range(0, radial, CHUNK):

                def store(c, r, value):
                    made[c, row, j, pl.ds(r, CHUNK), :] = value
                    if plan.strips and j == depth - 1:
                        piece, index = piece_of(c * 2 + row)
                        border[piece][pl.ds(index * radial + r, CHUNK), :] = value

                before = joined(outer, row, size) if j == 0 else plain_rows(inner, row, own(j - 1))
                after = pieces(partner, row, radial) if j == depth - 1 else plain_rows(inner, row, own(j + 1))
                update_rows(
                    row, r0, radial, lambda c: (row * COMPS + c) * depth + j, plain_rows(inner, row, own(j)), before,
                    after, None if plan.early else plain_rows(base, row, j), plain_rows(now, row, at(j)),
                    plain_rows(prev, row, at(j)), lambda r, n: eddy[row, at(j), pl.ds(r, n), :], columns, coef, store,
                )
        if plan.final:
            copies.append(pltpu.make_async_copy(made.at[:, :, j], out.at[:, :, at(j)], sem.at[j]))
            copies[-1].start()
    for copy in copies:
        copy.wait()
    if plan.strips:
        lines = tile
        pack_columns(
            columns, lines, radial,
            [(row, c, plain_rows(inner, row, own(j))) for row in range(2) for c in range(COMPS) for j in range(depth)],
        )
        every = range(COMPS)
        for side in range(2):
            for j in range(depth):
                if j < depth - 1:
                    down = [strip[side, c, j + 1] for c in every]
                else:
                    down = [edge_of(edges, side, c, plan, plan.piece) for c in every]
                result = strip_layer(
                    coef, side, [strip[side, c, j] for c in every],
                    [strip_outer[side, c] if j == 0 else strip[side, c, j - 1] for c in every], down,
                    [lines[pl.ds((side * COMPS + c) * depth + j, 1), :] for c in every],
                    [strip_base[side, c, j] for c in every], [strip_now[side, c, j] for c in every],
                    [strip_prev[side, c, j] for c in every], strip_eddy[side, j],
                )
                for c in every:
                    strip_out[side, c, j] = result[c]
                    if j == depth - 1 and plan.edges:
                        put_edge(border[-1], side, c, result[c], plan, plan.piece)


def strip_items():
    now = [(0, c, NEED, c * NEED) for c in range(COMPS)]
    rest = [(1, c, NEED - 1, c * (NEED - 1)) for c in range(COMPS)]
    return now + rest + [(2, 0, NEED - 1, COMPS * (NEED - 1))]


def border_kernel(now, out, sems):
    _, _, cells, radial, _ = now.shape
    first, size = place_of(cells - 1)[0], radial // PARTS
    copies = []
    for i in range(2 * COMPS):
        source = now.at[i // 2, i % 2, first, pl.ds(0, size), :]
        copies.append(pltpu.make_async_copy(source, out.at[pl.ds(i * size, size), :], sems.at[i]))
        copies[-1].start()
    for copy in copies:
        copy.wait()


def gather_kernel(now, prev, eddy, _, *outs):
    _, _, cells, radial, axial = now.shape
    rotor, stator, *parts = outs[: 2 + PARTS]
    next_parts, prev_parts = outs[2 + PARTS : 2 + 2 * PARTS], outs[2 + 2 * PARTS : 2 + 3 * PARTS]
    border, rest = outs[2 + 3 * PARTS :][: len(PIECES)], outs[2 + 3 * PARTS + len(PIECES) :]
    late, (eddy_outer, now_held, prev_held, eddy_held, in_sems, out_sems) = rest[: len(PIECES)], rest[len(PIECES) :]
    size = radial // PARTS
    _, _, cells, radial, axial = now.shape
    depth = cells - 1
    first, step = place_of(depth)
    per_tile = axial // STRIP
    block = lax.broadcasted_iota(jnp.int32, (radial, axial), 1) // STRIP
    items = [(item, t) for item in strip_items() for t in range(cells)]
    arrays = ((now, now_held), (prev, prev_held), (eddy, eddy_held))
    reads, writes = {}, []
    order = [(row, kind, c) for row in range(2) for kind, c, _, _ in strip_items()]
    for i, (row, kind, c) in enumerate(order):
        at = (row,) if kind == 2 else (c, row)
        source, held = arrays[kind]
        reads[row, kind, c] = pltpu.make_async_copy(source.at[at], held.at[at], in_sems.at[i])
        reads[row, kind, c].start()
    rotor[...] = jnp.zeros_like(rotor)
    stator[...] = jnp.zeros_like(stator)

    def write(source, target):
        writes.append(pltpu.make_async_copy(source, target, out_sems.at[len(writes)]))
        writes[-1].start()

    for row in range(2):
        mine, other = (rotor, stator) if row == 0 else (stator, rotor)
        begin = axial - STRIP if row == 0 else 0
        for p in range(0, len(items), per_tile):
            tile = jnp.zeros((radial, axial), jnp.float32)
            for q, ((kind, c, _, _), t) in enumerate(items[p : p + per_tile]):
                if t == 0:
                    reads[row, kind, c].wait()
                    if kind == 0:
                        at_piece, index = piece_of(c * 2 + row)
                        target = border[at_piece].at[pl.ds(index * radial, radial), :]
                        write(now_held.at[c, row, first + step * depth], target)
                        target = late[at_piece].at[pl.ds(index * size, size), :]
                        write(now_held.at[c, row, first, pl.ds(radial - size, size), :], target)
                    if kind < 2:
                        sources = ((now_held, first, parts), (now_held, first + step, next_parts)) if kind == 0 else ()
                        for held, at_layer, targets in sources or ((prev_held, first, prev_parts),):
                            for part, ref in enumerate(targets):
                                source = held.at[c, row, at_layer, pl.ds(part * size, size), :]
                                write(source, ref.at[pl.ds((c * 2 + row) * size, size), :])
                    else:
                        write(eddy_held.at[row, first], eddy_outer.at[row])
                value = eddy_held[row, t] if kind == 2 else arrays[kind][1][c, row, t]
                shift = (q * STRIP - begin) % axial
                tile = jnp.where(block == q, pltpu.roll(value, shift, 1) if shift else value, tile)
            turned = tile.T
            for q, ((kind, _, count, at), t) in enumerate(items[p : p + per_tile]):
                start = q * STRIP + (STRIP - count if row == 0 else 0)
                value = turned[start : start + count]
                mine[pl.ds((2 * t + (kind > 0)) * HALF + at, count), :] = value
                if kind == 0 and t == (0 if row == 0 else depth):
                    other[pl.ds(2 * cells * HALF + at, count), :] = value
    for copy in writes:
        copy.wait()


def align_kernel(depth, within, rotor, stator, rotor_behind, stator_ahead, *outs):
    cells = depth + 1
    edge = 2 * cells * HALF

    def block(own, side, sidestart, far, theta, half):
        at = lambda x: pl.multiple_of((2 * jnp.clip(x, 0, depth) + half) * HALF, HALF)
        near = own[pl.ds(at(theta), HALF), :]
        beside = side[pl.ds(at(theta - sidestart), HALF), :]
        value = jnp.where((theta >= 0) & (theta < cells), near, beside)
        if half == 0:
            value = jnp.where(theta == (cells if sidestart < 0 else -1), far[pl.ds(edge, HALF), :], value)
        return value

    for row, out in enumerate(outs):
        own, side, far = (rotor, rotor_behind, stator_ahead) if row == 0 else (stator, stator_ahead, rotor_behind)
        start = -within[0] if row == 0 else within[0]
        sidestart = -cells if row == 0 else cells
        for k in range(-1, cells + 1):
            for half in range(2):
                if half and k in (-1, cells):
                    continue
                at_row = 0 if k < 0 else (1 + 2 * k + half) * HALF
                out[pl.ds(at_row, HALF), :] = block(own, side, sidestart, far, start + k, half)


def scatter_kernel(depth, rotor, stator, *outs):
    cells = depth + 1
    radial = rotor.shape[-1]
    now_out, now_in, prev_out, prev_in, eddy_out, eddy_in, across, partner = outs
    first, step = place_of(depth)
    for side, ref in enumerate((stator, rotor)):
        for kind, c, count, at in strip_items():

            def read(row):
                value = ref[pl.ds(row, count), :]
                rest = jnp.zeros((STRIP - count, radial), jnp.float32)
                return jnp.concatenate([value, rest] if side == 0 else [rest, value], axis=0)

            for j in range(cells):
                start = (1 + 2 * (first + step * j) + (kind > 0)) * HALF
                value = read(pl.multiple_of(start, HALF) + at)
                if kind == 2 and j == 0:
                    eddy_out[side] = value
                elif kind == 2:
                    eddy_in[side, j - 1] = value
                elif j == 0:
                    (now_out, prev_out)[kind][side, c] = value
                else:
                    (now_in, prev_in)[kind][side, c, j - 1] = value
            if kind == 0:
                low, high = read(at), read((1 + 2 * cells) * HALF + at)
                across[side, c] = jnp.where(step > 0, low, high)
                partner[side, c] = jnp.where(step > 0, high, low)


VMEM = pl.BlockSpec(memory_space=pltpu.VMEM)
SMEM = pl.BlockSpec(memory_space=pltpu.SMEM)
ANY = pl.BlockSpec(memory_space=pl.ANY)


def in_hbm(x):
    return pltpu.with_memory_space_constraint(x, pltpu.HBM)


def in_vmem(x):
    return pltpu.with_memory_space_constraint(x, pltpu.VMEM)


def run(kernel, scalars, arrays, outs, scratch, name, final=None, out_shape=None, pinned=0):
    scalars, arrays = list(scalars), list(arrays)
    if pinned is not None:
        scalars = [x if x.dtype == jnp.int32 else in_vmem(x) for x in scalars]
        arrays = [in_hbm(x) if i < pinned else in_vmem(x) for i, x in enumerate(arrays)]
    in_specs = [SMEM if x.dtype == jnp.int32 else VMEM for x in scalars] + [VMEM] * len(arrays)
    if out_shape is not None:
        outs, out_specs = jax.ShapeDtypeStruct(out_shape, jnp.float32), ANY
    else:
        out_specs = (VMEM,) * len(outs)
    aliases = {}
    if final is not None:
        aliases = {len(in_specs): 0}
        in_specs, arrays = in_specs + [ANY], arrays + [final]
    return pl.pallas_call(
        lambda *refs: kernel(list(refs)),
        out_shape=outs,
        in_specs=in_specs,
        out_specs=out_specs,
        input_output_aliases=aliases,
        scratch_shapes=scratch,
        compiler_params=pltpu.CompilerParams(vmem_limit_bytes=16 << 20),
        cost_estimate=pl.CostEstimate(flops=1, bytes_accessed=1, transcendentals=0),
        name=name,
    )(*scalars, *arrays)


def call_border(now):
    radial, axial = now.shape[3:]
    return pl.pallas_call(
        border_kernel,
        out_shape=pltpu.VMEM((2 * COMPS * radial // PARTS, axial), jnp.float32),
        in_specs=[ANY],
        out_specs=VMEM,
        scratch_shapes=[pltpu.SemaphoreType.DMA((2 * COMPS,))],
        compiler_params=pltpu.CompilerParams(vmem_limit_bytes=16 << 20),
        cost_estimate=pl.CostEstimate(flops=1, bytes_accessed=1, transcendentals=0),
        name="outer_layer",
    )(in_hbm(now))


def call_gather(now, prev, eddy, ordered):
    cells, radial, axial = now.shape[2:]
    strips = pltpu.VMEM((2 * HALF * cells + HALF, radial), jnp.float32)
    part = pltpu.HBM((2 * COMPS * radial // PARTS, axial), jnp.float32)
    border = [pltpu.HBM((count * radial, axial), jnp.float32) for count in PIECES]
    late = [pltpu.HBM((count * radial // PARTS, axial), jnp.float32) for count in PIECES]
    plane = pltpu.HBM((2, radial, axial), jnp.float32)
    reads = pltpu.SemaphoreType.DMA((2 * (2 * COMPS + 1),))
    writes = pltpu.SemaphoreType.DMA((2 * (2 * COMPS + 1 + 3 * COMPS * PARTS),))
    held = [pltpu.VMEM(x.shape, jnp.float32) for x in (now, prev, eddy)]
    got = pl.pallas_call(
        gather_kernel,
        out_shape=(strips,) * 2 + (part,) * (3 * PARTS) + (*border, *late, plane),
        in_specs=[ANY] * 4,
        out_specs=(VMEM,) * 2 + (ANY,) * (3 * PARTS + 1 + 2 * len(PIECES)),
        scratch_shapes=[*held, reads, writes],
        compiler_params=pltpu.CompilerParams(vmem_limit_bytes=16 << 20),
        cost_estimate=pl.CostEstimate(flops=1, bytes_accessed=1, transcendentals=0),
        name="gather_strips",
    )(*(in_hbm(x) for x in (now, prev, eddy)), ordered)
    at = [2 + i * PARTS for i in range(4)]
    ends = at[3] + len(PIECES)
    return got[:2], *(got[i : i + PARTS] for i in at[:3]), got[at[3] : ends], got[ends:-1], got[-1]


def call_align(within, strips, cells):
    rotor, stator = strips
    moved = [shifted(rotor, 1), shifted(stator, -1)]
    rows = jax.ShapeDtypeStruct((2 * HALF * (cells + 1), rotor.shape[1]), jnp.float32)
    return run(
        lambda refs: align_kernel(cells - 1, *refs), [within.reshape(1)], [rotor, stator, *moved], (rows, rows), [],
        "align_strips",
    )


def call_scatter(rotor, stator, cells):
    radial = rotor.shape[1]
    shape = lambda *lead: pltpu.VMEM((2, *lead, STRIP, radial), jnp.float32)
    both = [shape(COMPS), shape(COMPS, cells - 1)]
    outs = (*both, *both, shape(), shape(cells - 1), shape(COMPS), shape(COMPS))
    return run(
        lambda refs: scatter_kernel(cells - 1, *refs), [], [rotor, stator], outs, [], "scatter_strips",
        pinned=None,
    )


def shifted(value, steps):
    count = lax.axis_size("theta")
    return lax.ppermute(value, "theta", [(i, (i + steps) % count) for i in range(count)])


def across_chips(value):
    count = lax.axis_size("theta")
    pairs = [(i, (i - 1 if i % 2 == 0 else i + 1) % count) for i in range(count)]
    return lax.ppermute(value, "theta", pairs)


def within_chip(value):
    count = lax.axis_size("theta")
    return lax.ppermute(value, "theta", [(i, i ^ 1) for i in range(count)])


def faced(outer, rotor, stator, sectors):
    count = lax.axis_size("theta")
    if count <= 16:

        def branch(steps):
            def exchange(outer, rotor, stator):
                return [across_chips(x) for x in outer], shifted(rotor, steps), shifted(stator, -steps)

            return exchange

        return lax.switch(sectors, [branch(i) for i in range(count)], outer, rotor, stator)
    amounts = jnp.stack([sectors, count - sectors]) % count
    stacked = jnp.stack([rotor, stator])
    for level in range((count - 1).bit_length()):
        taken = ((amounts >> level) & 1) == 1
        stacked = jnp.where(taken[:, None, None], shifted(stacked, 1 << level), stacked)
    return [across_chips(x) for x in outer], stacked[0], stacked[1]


def per_device(state_now, state_prev, eddy_visc, mean_flow, offset):
    shape = state_now.shape
    cells, radial, axial = shape[2:]
    count = lax.axis_size("theta")
    core = lax.axis_index("theta") % 2
    scalars = scalars_of(mean_flow, jnp.where(core == 1, -1.0, 1.0).astype(jnp.float32), axial)
    shift_cells = offset[0] % (cells * count)
    depth, size = cells - 1, radial // PARTS

    early = call_border(state_now)
    across = [across_chips(early)]
    strips, outer, next_layer, prev_outer, border, late, eddy_outer = call_gather(
        state_now, state_prev, eddy_visc, early
    )
    rotor, stator = call_align(shift_cells % cells, strips, cells)
    sectors = lax.optimization_barrier((shift_cells // cells, across))[0]
    late, rotor, stator = faced(late, rotor, stator, sectors)
    across.append(late)
    partner = [within_chip(x) for x in border]
    now_out, now_in, prev_out, prev_in, eddy_out, eddy_in, edge_across, edge_within = call_scatter(
        rotor, stator, cells
    )

    now_outer, inner, strip_out, strip_in = outer, state_now, now_out, now_in
    f32 = jnp.float32
    square = pltpu.VMEM((radial, axial), f32)
    n = 0
    for _ in range(ITERS):
        base_outer, base_inner, base_out, base_in = outer, inner, strip_out, strip_in
        for _ in SECTION_WEIGHTS:
            n += 1
            plan = Plan(n, shape)

            def outer_call(p, ordered):
                arrays = [eddy_outer, prev_outer[p], next_layer[p] if n == 1 else inner, *outer, now_outer[p]]
                arrays += [] if plan.early else [base_outer[p]]
                arrays += across[p] if n == 1 and p == PARTS - 1 else [across[p]]
                held, arrays = len(arrays), arrays + [strip_out]
                outs = [pltpu.VMEM((2 * COMPS * size, axial), f32)]
                if p == 0 and plan.edges:
                    outs = [pltpu.VMEM((2 * COMPS * (size + plan.edge), axial), f32)]
                if p == 0 and plan.strips:
                    arrays += [edge_across] if n == 1 else []
                    arrays += [strip_in, now_out, prev_out, eddy_out, base_out]
                    outs.append(pltpu.VMEM(strip_out.shape, f32))
                scratch = [square, square]
                if plan.final:
                    scratch += [pltpu.VMEM((2 * COMPS * size, axial), f32), pltpu.SemaphoreType.DMA((2 * COMPS,))]
                elif p > 0:
                    arrays.append(ordered)
                return run(
                    lambda refs: outer_kernel(plan, p, refs), [scalars], arrays, tuple(outs), scratch, "outer",
                    ordered if plan.final else None, shape if plan.final else None, held if n == 1 else 0,
                )

            def inner_call(ordered):
                arrays = [eddy_visc, state_prev, state_now, inner, strip_in, *outer, *partner]
                arrays += [] if plan.early else [base_inner]
                outs = [pltpu.VMEM((COMPS, 2, depth, radial, axial), f32)]
                if plan.strips:
                    arrays += [edge_within] if n == 1 else []
                    arrays += [strip_out, now_in, prev_in, eddy_in, base_in, ordered]
                    outs += [pltpu.VMEM((count * radial, axial), f32) for count in PIECES[:-1]]
                    rows = plan.piece + 2 * COMPS * plan.edge
                    outs += [pltpu.VMEM((rows, axial), f32), pltpu.VMEM(strip_in.shape, f32)]
                scratch = [square, square]
                if plan.final:
                    scratch += [pltpu.VMEM((COMPS, 2, depth, radial, axial), f32), pltpu.SemaphoreType.DMA((depth,))]
                return run(
                    lambda refs: inner_kernel(plan, refs), [scalars], arrays, tuple(outs), scratch, "inner", None,
                    shape if plan.final else None, None if n == 1 else 0,
                )

            if plan.final:
                made = inner_call(None)
                for p in range(PARTS):
                    made = outer_call(p, made)
                return made
            got, new_strip_out = outer_call(0, None)
            new_outer = [got]
            if n > 1:
                made = inner_call(got)
            for p in range(1, PARTS):
                new_outer.append(outer_call(p, made[1] if n > 1 else new_outer[-1])[0])
            if n == 1:
                made = inner_call(new_outer[-1])
            across = [across_chips(x) for x in new_outer]
            partner = [within_chip(x) for x in made[1:-1]]
            inner, strip_in = made[0], made[-1]
            outer, strip_out = new_outer, new_strip_out


def solution(mesh):
    placed = (
        P(None, None, "theta", "groups", None),
        P(None, None, "theta", "groups", None),
        P(None, "theta", "groups", None),
        P(),
        P("groups"),
    )
    return jax.shard_map(
        per_device,
        mesh=mesh,
        in_specs=placed,
        out_specs=P(None, None, "theta", "groups", None),
        check_vma=False,
    )
```

```python
import jax
import jax.numpy as jnp
from jax import lax
from jax.experimental import pallas as pl
from jax.experimental.pallas import tpu as pltpu
from jax.sharding import PartitionSpec as P

ITERS = 2
PSEUDO_STEP = 0.2
PHYS_STEP = 1.0
SECTION_WEIGHTS = (0.6, 0.6, 1.0)
COMPS = 5
CHUNK = 16
STRIP = 8
NEED = 6
HALF = 30
PARTS = 2
PIECES = (4, 3, 3)


def scalars_of(mean_flow, sign, lanes):
    flow = jnp.concatenate([mean_flow, 1.0 / mean_flow[:, 2:3]], axis=1).reshape(-1)
    return jnp.broadcast_to(jnp.concatenate([flow, jnp.broadcast_to(sign, (6,))])[:, None], (16, lanes))


def coefficients(scalars, row, weight):
    a = weight * PSEUDO_STEP
    axial, swirl, density, sound, inverse = (scalars[pl.ds(row * 5 + i, 1), :] for i in range(5))
    sign = scalars[pl.ds(10, 1), :]
    half = 0.5 * a
    mass, lift = half * density, half * inverse
    return half * axial, half * swirl * sign, mass, mass * sound * sound, lift, lift * sign, sign, a


def advance(k, f, up, down, low, high, behind, ahead, kept, eddy):
    e = k[7] * eddy
    damp = 6.0 * e + (1.5 / PHYS_STEP) * k[7]
    to_ahead, to_behind, to_down, to_up = e - k[0], e + k[0], e - k[1], e + k[1]
    div = (ahead[1] - behind[1]) + k[6] * (down[2] - up[2]) + (high[3] - low[3])
    push = (
        k[2] * div, k[4] * (ahead[4] - behind[4]), k[5] * (down[4] - up[4]), k[4] * (high[4] - low[4]), k[3] * div,
    )
    new = []
    for c in range(COMPS):
        axial = to_ahead * ahead[c] + to_behind * behind[c]
        theta = to_down * down[c] + to_up * up[c]
        own = (kept[c] - push[c]) - damp * f[c]
        new.append((own + e * (low[c] + high[c])) + (axial + theta))
    return new


def kept_part(a, base, now, prev):
    a = a * (0.5 / PHYS_STEP)
    if base is None:
        return (1.0 + 4.0 * a) * now - a * prev
    return (base + (4.0 * a) * now) - a * prev


def layer_rows(ref, row, size, first=0):
    return lambda c, r, n: ref[pl.ds((c * 2 + row) * size + r - first, n), :]


def part_rows(ref, row, plan, p):
    whole = ref.shape[0] == 2 * COMPS * plan.radial
    return layer_rows(ref, row, plan.radial) if whole else layer_rows(ref, row, plan.size, p * plan.size)


def joined(refs, row, size):
    def read(c, r, n):
        p, q = r // size, (r + n - 1) // size
        if p == q:
            return layer_rows(refs[p], row, size, p * size)(c, r, n)
        cut = q * size - r
        return jnp.concatenate(
            [layer_rows(refs[p], row, size, p * size)(c, r, cut), layer_rows(refs[q], row, size, q * size)(c, r + cut, n - cut)]
        )

    return read


def piece_of(index):
    for at, count in enumerate(PIECES):
        if index < count:
            return at, index
        index -= count


def pieces(refs, row, size, first=0):
    def read(c, r, n):
        at, index = piece_of(c * 2 + row)
        return refs[at][pl.ds(index * size + r - first, n), :]

    return read


def plain_rows(ref, row, layer):
    return lambda c, r, n: ref[c, row, layer, pl.ds(r, n), :]


def update_rows(row, r0, radial, ghost_at, center, before, after, base, now, prev, eddy, ghosts, coef, store):
    ghost = ghosts[pl.ds(r0, CHUNK), :]
    axial = ghost.shape[-1]
    lane = lax.broadcasted_iota(jnp.int32, ghost.shape, 1)
    first, last = lane == 0, lane == axial - 1
    f, low, high, behind, ahead = [], [], [], [], []
    for c in range(COMPS):
        f.append(center(c, r0, CHUNK))
        wall = -1.0 if c == 3 else 1.0
        if r0 == 0:
            low.append(jnp.concatenate([f[c][:1] * wall, center(c, 0, CHUNK - 1)], axis=0))
        else:
            low.append(center(c, r0 - 1, CHUNK))
        if r0 + CHUNK == radial:
            high.append(jnp.concatenate([center(c, r0 + 1, CHUNK - 1), f[c][-1:] * wall], axis=0))
        else:
            high.append(center(c, r0 + 1, CHUNK))
        at = ghost_at(c)
        lower, upper = pltpu.roll(f[c], 1, 1), pltpu.roll(f[c], axial - 1, 1)
        if row == 0:
            lower = jnp.where(first, 0.0, lower)
            upper = jnp.where(last, pltpu.roll(ghost, (axial - 1 - at) % axial, 1), upper)
        else:
            lower = jnp.where(first, pltpu.roll(ghost, (axial - at) % axial, 1), lower)
            upper = jnp.where(last, f[c], upper)
        behind.append(lower)
        ahead.append(upper)
    every = range(COMPS)
    read = lambda source: [source(c, r0, CHUNK) for c in every]
    new = advance(
        coef[row], f, read(before), read(after), low, high, behind, ahead,
        [kept_part(coef[row][7], base and base(c, r0, CHUNK), now(c, r0, CHUNK), prev(c, r0, CHUNK)) for c in every],
        eddy(r0, CHUNK),
    )
    for c in every:
        store(c, r0, new[c])


def pack_columns(tile, lines, radial, columns):
    axial = tile.shape[-1]
    lane = lax.broadcasted_iota(jnp.int32, (CHUNK, axial), 1)
    for r0 in range(0, radial, CHUNK):
        packed = jnp.zeros((CHUNK, axial), jnp.float32)
        for i, (row, c, center) in enumerate(columns):
            value, shift = center(c, r0, CHUNK), (i - (axial - 1 if row == 0 else 0)) % axial
            packed = jnp.where(lane == i, pltpu.roll(value, shift, 1) if shift else value, packed)
        tile[pl.ds(r0, CHUNK), :] = packed
    lines[...] = tile[...].T


def ghost_columns(tile, columns, faces):
    tile[...] = jnp.zeros_like(tile)
    for i, (strip, side) in enumerate(faces):
        face = 0 if side == 0 else STRIP - 1
        tile[pl.ds(i, 1), :] = strip[pl.ds(face, 1), :]
    columns[...] = tile[...].T


def strip_layer(coef, side, cur, up, down, lines, base, now, prev, eddy):
    radial = eddy.shape[-1]
    sub = lax.broadcasted_iota(jnp.int32, (STRIP, radial), 0)
    lane = lax.broadcasted_iota(jnp.int32, (STRIP, radial), 1)
    low, high, behind, ahead = [], [], [], []
    for c in range(COMPS):
        value = cur[c]
        wall = -value if c == 3 else value
        lower, upper = pltpu.roll(value, 1, 0), pltpu.roll(value, STRIP - 1, 0)
        if side == 0:
            lower = jnp.where(sub == 0, lines[c], lower)
        else:
            upper = jnp.where(sub == STRIP - 1, lines[c], upper)
        low.append(jnp.where(lane == 0, wall, pltpu.roll(value, 1, 1)))
        high.append(jnp.where(lane == radial - 1, wall, pltpu.roll(value, radial - 1, 1)))
        behind.append(lower)
        ahead.append(upper)
    kept = [kept_part(coef[0][7], base[c], now[c], prev[c]) for c in range(COMPS)]
    return advance(coef[1 - side], cur, up, down, low, high, behind, ahead, kept, eddy)


def edge_of(ref, side, c, plan, offset):
    if plan.n == 1:
        return ref[side, c]
    got = ref[pl.ds(offset + (plan.edge + 1) * (side * COMPS + c), plan.edge + 1), :]
    rest = jnp.zeros((STRIP - got.shape[0], got.shape[1]), jnp.float32)
    return jnp.concatenate([got, rest] if side == 0 else [rest, got], axis=0)


def put_edge(ref, side, c, value, plan, offset):
    start = 0 if side == 0 else STRIP - plan.edge
    ref[pl.ds(offset + plan.edge * (side * COMPS + c), plan.edge), :] = value[start : start + plan.edge]


class Plan:
    def __init__(self, n, shape):
        self.weight = SECTION_WEIGHTS[(n - 1) % len(SECTION_WEIGHTS)]
        self.n, self.total = n, ITERS * len(SECTION_WEIGHTS)
        self.cells, self.radial, self.axial = shape[2:]
        self.depth, self.size = self.cells - 1, self.radial // PARTS
        self.piece = PIECES[-1] * self.radial
        self.early = n <= len(SECTION_WEIGHTS)
        self.final = n == self.total
        self.strips = n < self.total
        self.edge = self.total - 1 - n
        self.edges = self.edge > 0


def place_of(depth):
    odd = lax.axis_index("theta") % 2 == 1
    return jnp.where(odd, depth, 0), jnp.where(odd, -1, 1)


def outer_kernel(plan, p, refs):
    size, radial = plan.size, plan.radial
    scalars, eddy, prev, inner = (refs.pop(0) for _ in range(4))
    place = place_of(plan.depth)
    coef = [coefficients(scalars, row, plan.weight) for row in range(2)]
    mine = [refs.pop(0) for _ in range(PARTS)]
    now = refs.pop(0)
    base = None if plan.early else refs.pop(0)
    split = plan.n == 1 and p == PARTS - 1
    across = [refs.pop(0) for _ in PIECES] if split else refs.pop(0)
    strip = refs.pop(0)
    works = p == 0 and plan.strips
    if works:
        edges = refs.pop(0) if plan.n == 1 else across
        strip_inner, strip_now, strip_prev, strip_eddy = (refs.pop(0) for _ in range(4))
        strip_base = refs.pop(0)
    if p > 0 and not plan.final:
        refs.pop(0)
    if plan.final:
        refs.pop(0)
    out = refs.pop(0)
    if works:
        strip_out = refs.pop(0)
    tile, columns = refs.pop(0), refs.pop(0)
    if plan.final:
        made, sem = refs.pop(0), refs.pop(0)
    else:
        made = out
    copies = []
    ghost_columns(tile, columns, [(strip.at[side, c], side) for side in range(2) for c in range(COMPS)])
    for row in range(2):
        for r0 in range(p * size, (p + 1) * size, CHUNK):

            def store(c, r, value):
                made[pl.ds((c * 2 + row) * size + r - p * size, CHUNK), :] = value

            part = lambda ref: part_rows(ref, row, plan, p)
            inside = part(inner) if plan.n == 1 else plain_rows(inner, row, 0)
            update_rows(
                row, r0, radial, lambda c: row * COMPS + c, joined(mine, row, size),
                pieces(across, row, size, p * size) if split else part(across), inside,
                None if plan.early else part(base), part(now), part(prev), lambda r, n: eddy[row, pl.ds(r, n), :], columns,
                coef, store,
            )
        if plan.final:
            for c in range(COMPS):
                source = made.at[pl.ds((c * 2 + row) * size, size), :]
                target = out.at[c, row, place[0], pl.ds(p * size, size), :]
                copies.append(pltpu.make_async_copy(source, target, sem.at[len(copies)]))
                copies[-1].start()
    for copy in copies:
        copy.wait()
    if works:
        lines = tile
        pack_columns(
            columns, lines, radial, [(row, c, joined(mine, row, size)) for row in range(2) for c in range(COMPS)]
        )
        every = range(COMPS)
        for side in range(2):
            result = strip_layer(
                coef, side, [strip[side, c] for c in every],
                [edge_of(edges, side, c, plan, 2 * COMPS * size) for c in every],
                [strip_inner[side, c, 0] for c in every], [lines[pl.ds(side * COMPS + c, 1), :] for c in every],
                [strip_base[side, c] for c in every], [strip_now[side, c] for c in every],
                [strip_prev[side, c] for c in every], strip_eddy[side],
            )
            for c in every:
                strip_out[side, c] = result[c]
                if plan.edges:
                    put_edge(out, side, c, result[c], plan, 2 * COMPS * size)


def inner_kernel(plan, refs):
    size, radial, depth = plan.size, plan.radial, plan.depth
    scalars, eddy, prev, now, inner, strip = (refs.pop(0) for _ in range(6))
    place = place_of(plan.depth)
    coef = [coefficients(scalars, row, plan.weight) for row in range(2)]
    if plan.n == 1:
        inner = now
    outer = [refs.pop(0) for _ in range(PARTS)]
    partner = [refs.pop(0) for _ in PIECES]
    base = None if plan.early else refs.pop(0)
    if plan.strips:
        edges = refs.pop(0) if plan.n == 1 else partner[-1]
        strip_outer, strip_now, strip_prev, strip_eddy, strip_base = (refs.pop(0) for _ in range(5))
    if plan.strips:
        refs.pop(0)
    made = refs.pop(0)
    if plan.strips:
        border, strip_out = [refs.pop(0) for _ in PIECES], refs.pop(0)
    tile, columns = refs.pop(0), refs.pop(0)
    if plan.final:
        out, made, sem = made, refs.pop(0), refs.pop(0)
    ghost_columns(
        tile, columns, [(strip.at[side, c, j], side) for side in range(2) for c in range(COMPS) for j in range(depth)]
    )
    copies = []
    at = lambda j: place[0] + place[1] * (j + 1)
    own = lambda j: at(j) if plan.n == 1 else j
    for j in range(depth):
        for row in range(2):
            for r0 in range(0, radial, CHUNK):

                def store(c, r, value):
                    made[c, row, j, pl.ds(r, CHUNK), :] = value
                    if plan.strips and j == depth - 1:
                        piece, index = piece_of(c * 2 + row)
                        border[piece][pl.ds(index * radial + r, CHUNK), :] = value

                before = joined(outer, row, size) if j == 0 else plain_rows(inner, row, own(j - 1))
                after = pieces(partner, row, radial) if j == depth - 1 else plain_rows(inner, row, own(j + 1))
                update_rows(
                    row, r0, radial, lambda c: (row * COMPS + c) * depth + j, plain_rows(inner, row, own(j)), before,
                    after, None if plan.early else plain_rows(base, row, j), plain_rows(now, row, at(j)),
                    plain_rows(prev, row, at(j)), lambda r, n: eddy[row, at(j), pl.ds(r, n), :], columns, coef, store,
                )
        if plan.final:
            copies.append(pltpu.make_async_copy(made.at[:, :, j], out.at[:, :, at(j)], sem.at[j]))
            copies[-1].start()
    for copy in copies:
        copy.wait()
    if plan.strips:
        lines = tile
        pack_columns(
            columns, lines, radial,
            [(row, c, plain_rows(inner, row, own(j))) for row in range(2) for c in range(COMPS) for j in range(depth)],
        )
        every = range(COMPS)
        for side in range(2):
            for j in range(depth):
                if j < depth - 1:
                    down = [strip[side, c, j + 1] for c in every]
                else:
                    down = [edge_of(edges, side, c, plan, plan.piece) for c in every]
                result = strip_layer(
                    coef, side, [strip[side, c, j] for c in every],
                    [strip_outer[side, c] if j == 0 else strip[side, c, j - 1] for c in every], down,
                    [lines[pl.ds((side * COMPS + c) * depth + j, 1), :] for c in every],
                    [strip_base[side, c, j] for c in every], [strip_now[side, c, j] for c in every],
                    [strip_prev[side, c, j] for c in every], strip_eddy[side, j],
                )
                for c in every:
                    strip_out[side, c, j] = result[c]
                    if j == depth - 1 and plan.edges:
                        put_edge(border[-1], side, c, result[c], plan, plan.piece)


def strip_items():
    now = [(0, c, NEED, c * NEED) for c in range(COMPS)]
    rest = [(1, c, NEED - 1, c * (NEED - 1)) for c in range(COMPS)]
    return now + rest + [(2, 0, NEED - 1, COMPS * (NEED - 1))]


def border_kernel(now, out, sems):
    _, _, cells, radial, _ = now.shape
    first, size = place_of(cells - 1)[0], radial // PARTS
    copies = []
    for i in range(2 * COMPS):
        source = now.at[i // 2, i % 2, first, pl.ds(0, size), :]
        copies.append(pltpu.make_async_copy(source, out.at[pl.ds(i * size, size), :], sems.at[i]))
        copies[-1].start()
    for copy in copies:
        copy.wait()


def gather_kernel(now, prev, eddy, _, *outs):
    _, _, cells, radial, axial = now.shape
    rotor, stator, *parts = outs[: 2 + PARTS]
    next_parts, prev_parts = outs[2 + PARTS : 2 + 2 * PARTS], outs[2 + 2 * PARTS : 2 + 3 * PARTS]
    border, rest = outs[2 + 3 * PARTS :][: len(PIECES)], outs[2 + 3 * PARTS + len(PIECES) :]
    late, (eddy_outer, now_held, prev_held, eddy_held, in_sems, out_sems) = rest[: len(PIECES)], rest[len(PIECES) :]
    size = radial // PARTS
    _, _, cells, radial, axial = now.shape
    depth = cells - 1
    first, step = place_of(depth)
    per_tile = axial // STRIP
    block = lax.broadcasted_iota(jnp.int32, (radial, axial), 1) // STRIP
    items = [(item, t) for item in strip_items() for t in range(cells)]
    arrays = ((now, now_held), (prev, prev_held), (eddy, eddy_held))
    reads, writes = {}, []
    order = [(row, kind, c) for row in range(2) for kind, c, _, _ in strip_items()]
    for i, (row, kind, c) in enumerate(order):
        at = (row,) if kind == 2 else (c, row)
        source, held = arrays[kind]
        reads[row, kind, c] = pltpu.make_async_copy(source.at[at], held.at[at], in_sems.at[i])
        reads[row, kind, c].start()
    rotor[...] = jnp.zeros_like(rotor)
    stator[...] = jnp.zeros_like(stator)

    def write(source, target):
        writes.append(pltpu.make_async_copy(source, target, out_sems.at[len(writes)]))
        writes[-1].start()

    for row in range(2):
        mine, other = (rotor, stator) if row == 0 else (stator, rotor)
        begin = axial - STRIP if row == 0 else 0
        for p in range(0, len(items), per_tile):
            tile = jnp.zeros((radial, axial), jnp.float32)
            for q, ((kind, c, _, _), t) in enumerate(items[p : p + per_tile]):
                if t == 0:
                    reads[row, kind, c].wait()
                    if kind == 0:
                        at_piece, index = piece_of(c * 2 + row)
                        target = border[at_piece].at[pl.ds(index * radial, radial), :]
                        write(now_held.at[c, row, first + step * depth], target)
                        target = late[at_piece].at[pl.ds(index * size, size), :]
                        write(now_held.at[c, row, first, pl.ds(radial - size, size), :], target)
                    if kind < 2:
                        sources = ((now_held, first, parts), (now_held, first + step, next_parts)) if kind == 0 else ()
                        for held, at_layer, targets in sources or ((prev_held, first, prev_parts),):
                            for part, ref in enumerate(targets):
                                source = held.at[c, row, at_layer, pl.ds(part * size, size), :]
                                write(source, ref.at[pl.ds((c * 2 + row) * size, size), :])
                    else:
                        write(eddy_held.at[row, first], eddy_outer.at[row])
                value = eddy_held[row, t] if kind == 2 else arrays[kind][1][c, row, t]
                shift = (q * STRIP - begin) % axial
                tile = jnp.where(block == q, pltpu.roll(value, shift, 1) if shift else value, tile)
            turned = tile.T
            for q, ((kind, _, count, at), t) in enumerate(items[p : p + per_tile]):
                start = q * STRIP + (STRIP - count if row == 0 else 0)
                value = turned[start : start + count]
                mine[pl.ds((2 * t + (kind > 0)) * HALF + at, count), :] = value
                if kind == 0 and t == (0 if row == 0 else depth):
                    other[pl.ds(2 * cells * HALF + at, count), :] = value
    for copy in writes:
        copy.wait()


def align_kernel(depth, within, rotor, stator, rotor_behind, stator_ahead, *outs):
    cells = depth + 1
    edge = 2 * cells * HALF

    def block(own, side, sidestart, far, theta, half):
        at = lambda x: pl.multiple_of((2 * jnp.clip(x, 0, depth) + half) * HALF, HALF)
        near = own[pl.ds(at(theta), HALF), :]
        beside = side[pl.ds(at(theta - sidestart), HALF), :]
        value = jnp.where((theta >= 0) & (theta < cells), near, beside)
        if half == 0:
            value = jnp.where(theta == (cells if sidestart < 0 else -1), far[pl.ds(edge, HALF), :], value)
        return value

    for row, out in enumerate(outs):
        own, side, far = (rotor, rotor_behind, stator_ahead) if row == 0 else (stator, stator_ahead, rotor_behind)
        start = -within[0] if row == 0 else within[0]
        sidestart = -cells if row == 0 else cells
        for k in range(-1, cells + 1):
            for half in range(2):
                if half and k in (-1, cells):
                    continue
                at_row = 0 if k < 0 else (1 + 2 * k + half) * HALF
                out[pl.ds(at_row, HALF), :] = block(own, side, sidestart, far, start + k, half)


def scatter_kernel(depth, rotor, stator, *outs):
    cells = depth + 1
    radial = rotor.shape[-1]
    now_out, now_in, prev_out, prev_in, eddy_out, eddy_in, across, partner = outs
    first, step = place_of(depth)
    for side, ref in enumerate((stator, rotor)):
        for kind, c, count, at in strip_items():

            def read(row):
                value = ref[pl.ds(row, count), :]
                rest = jnp.zeros((STRIP - count, radial), jnp.float32)
                return jnp.concatenate([value, rest] if side == 0 else [rest, value], axis=0)

            for j in range(cells):
                start = (1 + 2 * (first + step * j) + (kind > 0)) * HALF
                value = read(pl.multiple_of(start, HALF) + at)
                if kind == 2 and j == 0:
                    eddy_out[side] = value
                elif kind == 2:
                    eddy_in[side, j - 1] = value
                elif j == 0:
                    (now_out, prev_out)[kind][side, c] = value
                else:
                    (now_in, prev_in)[kind][side, c, j - 1] = value
            if kind == 0:
                low, high = read(at), read((1 + 2 * cells) * HALF + at)
                across[side, c] = jnp.where(step > 0, low, high)
                partner[side, c] = jnp.where(step > 0, high, low)


VMEM = pl.BlockSpec(memory_space=pltpu.VMEM)
SMEM = pl.BlockSpec(memory_space=pltpu.SMEM)
ANY = pl.BlockSpec(memory_space=pl.ANY)


def in_hbm(x):
    return pltpu.with_memory_space_constraint(x, pltpu.HBM)


def in_vmem(x):
    return pltpu.with_memory_space_constraint(x, pltpu.VMEM)


def run(kernel, scalars, arrays, outs, scratch, name, final=None, out_shape=None, pinned=0):
    scalars, arrays = list(scalars), list(arrays)
    if pinned is not None:
        scalars = [x if x.dtype == jnp.int32 else in_vmem(x) for x in scalars]
        arrays = [in_hbm(x) if i < pinned else in_vmem(x) for i, x in enumerate(arrays)]
    in_specs = [SMEM if x.dtype == jnp.int32 else VMEM for x in scalars] + [VMEM] * len(arrays)
    if out_shape is not None:
        outs, out_specs = jax.ShapeDtypeStruct(out_shape, jnp.float32), ANY
    else:
        out_specs = (VMEM,) * len(outs)
    aliases = {}
    if final is not None:
        aliases = {len(in_specs): 0}
        in_specs, arrays = in_specs + [ANY], arrays + [final]
    return pl.pallas_call(
        lambda *refs: kernel(list(refs)),
        out_shape=outs,
        in_specs=in_specs,
        out_specs=out_specs,
        input_output_aliases=aliases,
        scratch_shapes=scratch,
        compiler_params=pltpu.CompilerParams(vmem_limit_bytes=16 << 20),
        cost_estimate=pl.CostEstimate(flops=1, bytes_accessed=1, transcendentals=0),
        name=name,
    )(*scalars, *arrays)


def call_border(now):
    radial, axial = now.shape[3:]
    return pl.pallas_call(
        border_kernel,
        out_shape=pltpu.VMEM((2 * COMPS * radial // PARTS, axial), jnp.float32),
        in_specs=[ANY],
        out_specs=VMEM,
        scratch_shapes=[pltpu.SemaphoreType.DMA((2 * COMPS,))],
        compiler_params=pltpu.CompilerParams(vmem_limit_bytes=16 << 20),
        cost_estimate=pl.CostEstimate(flops=1, bytes_accessed=1, transcendentals=0),
        name="outer_layer",
    )(in_hbm(now))


def call_gather(now, prev, eddy, ordered):
    cells, radial, axial = now.shape[2:]
    strips = pltpu.VMEM((2 * HALF * cells + HALF, radial), jnp.float32)
    part = pltpu.HBM((2 * COMPS * radial // PARTS, axial), jnp.float32)
    border = [pltpu.HBM((count * radial, axial), jnp.float32) for count in PIECES]
    late = [pltpu.HBM((count * radial // PARTS, axial), jnp.float32) for count in PIECES]
    plane = pltpu.HBM((2, radial, axial), jnp.float32)
    reads = pltpu.SemaphoreType.DMA((2 * (2 * COMPS + 1),))
    writes = pltpu.SemaphoreType.DMA((2 * (2 * COMPS + 1 + 3 * COMPS * PARTS),))
    held = [pltpu.VMEM(x.shape, jnp.float32) for x in (now, prev, eddy)]
    got = pl.pallas_call(
        gather_kernel,
        out_shape=(strips,) * 2 + (part,) * (3 * PARTS) + (*border, *late, plane),
        in_specs=[ANY] * 4,
        out_specs=(VMEM,) * 2 + (ANY,) * (3 * PARTS + 1 + 2 * len(PIECES)),
        scratch_shapes=[*held, reads, writes],
        compiler_params=pltpu.CompilerParams(vmem_limit_bytes=16 << 20),
        cost_estimate=pl.CostEstimate(flops=1, bytes_accessed=1, transcendentals=0),
        name="gather_strips",
    )(*(in_hbm(x) for x in (now, prev, eddy)), ordered)
    at = [2 + i * PARTS for i in range(4)]
    ends = at[3] + len(PIECES)
    return got[:2], *(got[i : i + PARTS] for i in at[:3]), got[at[3] : ends], got[ends:-1], got[-1]


def call_align(within, strips, cells):
    rotor, stator = strips
    moved = [shifted(rotor, 1), shifted(stator, -1)]
    rows = jax.ShapeDtypeStruct((2 * HALF * (cells + 1), rotor.shape[1]), jnp.float32)
    return run(
        lambda refs: align_kernel(cells - 1, *refs), [within.reshape(1)], [rotor, stator, *moved], (rows, rows), [],
        "align_strips",
    )


def call_scatter(rotor, stator, cells):
    radial = rotor.shape[1]
    shape = lambda *lead: pltpu.VMEM((2, *lead, STRIP, radial), jnp.float32)
    both = [shape(COMPS), shape(COMPS, cells - 1)]
    outs = (*both, *both, shape(), shape(cells - 1), shape(COMPS), shape(COMPS))
    return run(
        lambda refs: scatter_kernel(cells - 1, *refs), [], [rotor, stator], outs, [], "scatter_strips",
        pinned=None,
    )


def shifted(value, steps):
    count = lax.axis_size("theta")
    return lax.ppermute(value, "theta", [(i, (i + steps) % count) for i in range(count)])


def across_chips(value):
    count = lax.axis_size("theta")
    pairs = [(i, (i - 1 if i % 2 == 0 else i + 1) % count) for i in range(count)]
    return lax.ppermute(value, "theta", pairs)


def within_chip(value):
    count = lax.axis_size("theta")
    return lax.ppermute(value, "theta", [(i, i ^ 1) for i in range(count)])


def faced(outer, rotor, stator, sectors):
    count = lax.axis_size("theta")
    if count <= 16:

        def branch(steps):
            def exchange(outer, rotor, stator):
                return [across_chips(x) for x in outer], shifted(rotor, steps), shifted(stator, -steps)

            return exchange

        return lax.switch(sectors, [branch(i) for i in range(count)], outer, rotor, stator)
    amounts = jnp.stack([sectors, count - sectors]) % count
    stacked = jnp.stack([rotor, stator])
    for level in range((count - 1).bit_length()):
        taken = ((amounts >> level) & 1) == 1
        stacked = jnp.where(taken[:, None, None], shifted(stacked, 1 << level), stacked)
    return [across_chips(x) for x in outer], stacked[0], stacked[1]


def per_device(state_now, state_prev, eddy_visc, mean_flow, offset):
    shape = state_now.shape
    cells, radial, axial = shape[2:]
    count = lax.axis_size("theta")
    core = lax.axis_index("theta") % 2
    scalars = scalars_of(mean_flow, jnp.where(core == 1, -1.0, 1.0).astype(jnp.float32), axial)
    shift_cells = offset[0] % (cells * count)
    depth, size = cells - 1, radial // PARTS

    early = call_border(state_now)
    across = [across_chips(early)]
    strips, outer, next_layer, prev_outer, border, late, eddy_outer = call_gather(
        state_now, state_prev, eddy_visc, early
    )
    rotor, stator = call_align(shift_cells % cells, strips, cells)
    sectors = lax.optimization_barrier((shift_cells // cells, across))[0]
    late, rotor, stator = faced(late, rotor, stator, sectors)
    across.append(late)
    partner = [within_chip(x) for x in border]
    now_out, now_in, prev_out, prev_in, eddy_out, eddy_in, edge_across, edge_within = call_scatter(
        rotor, stator, cells
    )

    now_outer, inner, strip_out, strip_in = outer, state_now, now_out, now_in
    f32 = jnp.float32
    square = pltpu.VMEM((radial, axial), f32)
    n = 0
    for _ in range(ITERS):
        base_outer, base_inner, base_out, base_in = outer, inner, strip_out, strip_in
        for _ in SECTION_WEIGHTS:
            n += 1
            plan = Plan(n, shape)

            def outer_call(p, ordered):
                arrays = [eddy_outer, prev_outer[p], next_layer[p] if n == 1 else inner, *outer, now_outer[p]]
                arrays += [] if plan.early else [base_outer[p]]
                arrays += across[p] if n == 1 and p == PARTS - 1 else [across[p]]
                held, arrays = len(arrays), arrays + [strip_out]
                outs = [pltpu.VMEM((2 * COMPS * size, axial), f32)]
                if p == 0 and plan.edges:
                    outs = [pltpu.VMEM((2 * COMPS * (size + plan.edge), axial), f32)]
                if p == 0 and plan.strips:
                    arrays += [edge_across] if n == 1 else []
                    arrays += [strip_in, now_out, prev_out, eddy_out, base_out]
                    outs.append(pltpu.VMEM(strip_out.shape, f32))
                scratch = [square, square]
                if plan.final:
                    scratch += [pltpu.VMEM((2 * COMPS * size, axial), f32), pltpu.SemaphoreType.DMA((2 * COMPS,))]
                elif p > 0:
                    arrays.append(ordered)
                return run(
                    lambda refs: outer_kernel(plan, p, refs), [scalars], arrays, tuple(outs), scratch, "outer",
                    ordered if plan.final else None, shape if plan.final else None, held if n == 1 else 0,
                )

            def inner_call(ordered):
                arrays = [eddy_visc, state_prev, state_now, inner, strip_in, *outer, *partner]
                arrays += [] if plan.early else [base_inner]
                outs = [pltpu.VMEM((COMPS, 2, depth, radial, axial), f32)]
                if plan.strips:
                    arrays += [edge_within] if n == 1 else []
                    arrays += [strip_out, now_in, prev_in, eddy_in, base_in, ordered]
                    outs += [pltpu.VMEM((count * radial, axial), f32) for count in PIECES[:-1]]
                    rows = plan.piece + 2 * COMPS * plan.edge
                    outs += [pltpu.VMEM((rows, axial), f32), pltpu.VMEM(strip_in.shape, f32)]
                scratch = [square, square]
                if plan.final:
                    scratch += [pltpu.VMEM((COMPS, 2, depth, radial, axial), f32), pltpu.SemaphoreType.DMA((depth,))]
                return run(
                    lambda refs: inner_kernel(plan, refs), [scalars], arrays, tuple(outs), scratch, "inner", None,
                    shape if plan.final else None, None if n == 1 else 0,
                )

            if plan.final:
                made = inner_call(None)
                for p in range(PARTS):
                    made = outer_call(p, made)
                return made
            got, new_strip_out = outer_call(0, None)
            new_outer = [got]
            if n > 1:
                made = inner_call(got)
            for p in range(1, PARTS):
                new_outer.append(outer_call(p, made[1] if n > 1 else new_outer[-1])[0])
            if n == 1:
                made = inner_call(new_outer[-1])
            across = [across_chips(x) for x in new_outer]
            partner = [within_chip(x) for x in made[1:-1]]
            inner, strip_in = made[0], made[-1]
            outer, strip_out = new_outer, new_strip_out


def solution(mesh):
    placed = (
        P(None, None, "theta", "groups", None),
        P(None, None, "theta", "groups", None),
        P(None, "theta", "groups", None),
        P(),
        P("groups"),
    )
    return jax.shard_map(
        per_device,
        mesh=mesh,
        in_specs=placed,
        out_specs=P(None, None, "theta", "groups", None),
        check_vma=False,
    )
```
